32 devices in a mesh: dp: 8 (over z, x), spatial: 4 (over y, core).
Axes of the slice: x: 2, y: 2, z: 4, core: 2. Of those that a mesh axis runs over, the one named last changes fastest.
Arguments:
- latents: bfloat16 [16, 32, 32, 640], P('dp', 'spatial'), may hold values from -16 to 16
- plan: bfloat16 [16, 64, 640], P('dp', 'spatial'), may hold values from -45 to 45
- conv_weight: bfloat16 [9, 640, 640], P(None, 'dp'), may hold values from -0.078125 to 0.078125
- gn_gain: float32 [640], replicated, may hold values from 0.5 to 2
- attn_weights: bfloat16 [4, 640, 640], P(None, 'dp'), may hold values from -0.25 to 0.25
- cotangent: bfloat16 [16, 32, 32, 640], P('dp', 'spatial'), may hold values from -6 to 6
Outputs:
- block_out: bfloat16 [16, 32, 32, 640], P('dp', 'spatial')
- weight_grads: float32 [640, 2, 640], P('dp')
The draws below stay inside these ranges and needn't reach their ends.
All inputs are finite; a program needn't handle non-finite values.
Results may differ from the reference program's by a relative error of at most 0.03.
The reference program's roundings to bfloat16 on the way (of `hidden`, `mixed`, `probs_b`, `attended`, `grad_att`, `dscore` and `dquery`) count: a program that leaves them out, or rounds other values in their place, can miss the bound.
Values may be sent and summed in bfloat16 or wider, within the bound.
No kernel may reach another device: no remote copies, remote signals or barrier semaphores. Data moves between devices by JAX's collectives and lax.ppermute only.
A program may use at most 64 MiB of HBM per device.

```python
import math
import jax
import jax.numpy as jnp
from jax import lax

D = 640
GROUPS = 32
HEAD = 64
LAT = 32
IMAGES = 16
PLAN = 64
TOKENS = 16384


def draw_latents(key, part):
    key_base, key_chan = jax.random.split(key, 2)
    base = jnp.clip(jax.random.normal(key_base, (IMAGES, LAT, LAT, D), jnp.float32), -4.0, 4.0)
    level = jnp.arange(LAT, dtype=jnp.float32) / (LAT - 1)
    channel_scale = jax.random.uniform(key_chan, (D,), jnp.float32, 0.5, 1.5)
    row_scale = 0.5 + level
    values = base * row_scale[None, :, None, None] * channel_scale
    return jnp.clip(values, -16.0, 16.0).astype(jnp.bfloat16)


def draw_plan(key, part):
    key_base = jax.random.fold_in(key, 0)
    base = jnp.clip(jax.random.normal(key_base, (IMAGES, PLAN, D), jnp.float32), -6.0, 6.0)
    return jnp.clip(base, -45.0, 45.0).astype(jnp.bfloat16)


def block_scale(stream_key, dims, cuts, smallest, largest):
    factor_of, own = 1.0, jax.random.fold_in(stream_key, 6)
    for axis_at, parts in cuts:
        steps = jnp.exp(jax.random.uniform(jax.random.fold_in(own, axis_at), (parts,), jnp.float32, smallest / len(cuts), largest / len(cuts)))
        factor_of = factor_of * jnp.repeat(steps, dims[axis_at] // parts).reshape([-1 if axis == axis_at else 1 for axis in range(len(dims))])
    return factor_of


def centred(stream_key, dims, deviation, reach, cuts=(), held_as=jnp.bfloat16):
    loudness = block_scale(stream_key, dims, cuts, -0.22, 0.18) if cuts else 1.0
    entries = jax.random.normal(stream_key, dims, jnp.float32) * deviation * loudness
    return jnp.minimum(jnp.maximum(entries, -reach), reach).astype(held_as)


def setup_inputs(seed: int = 0) -> dict:
    splits = jax.random.split(jax.random.key(seed), 7)
    latents = draw_latents(jax.random.fold_in(splits[6], 71), 0)
    plan = draw_plan(jax.random.fold_in(splits[6], 71), 0)
    conv_weight = centred(splits[2], (9, D, D), (9 * D) ** -0.5, 0.078125, ((1, 8),))
    gn_gain = jnp.clip(jnp.exp(jax.random.uniform(splits[3], (D,), jnp.float32, math.log(0.5), math.log(2.0))), 0.5, 2.0)
    attn_weights = centred(splits[4], (4, D, D), D ** -0.5, 0.25, ((1, 8),))
    cotangent = centred(splits[5], (IMAGES, LAT, LAT, D), 1.0, 6.0, ((0, 8), (1, 4)))
    return dict(latents=latents, plan=plan, conv_weight=conv_weight, gn_gain=gn_gain, attn_weights=attn_weights, cotangent=cotangent)


def reference(latents, plan, conv_weight, gn_gain, attn_weights, cotangent):
    heads = D // HEAD
    per_group = D // GROUPS
    scale = 1.0 / math.sqrt(HEAD)
    weight_q = attn_weights[0]
    weight_k = attn_weights[1]
    weight_v = attn_weights[2]
    weight_o = attn_weights[3]

    def one_image(carry, inputs):
        image, plan_image, cot_image = inputs
        flat = image.astype(jnp.float32).reshape(LAT * LAT, GROUPS, per_group)
        counted = float(LAT * LAT * per_group)
        means = lax.optimization_barrier(jnp.sum(flat, axis=(0, 2))) / counted
        variance = lax.optimization_barrier(jnp.sum(flat * flat, axis=(0, 2))) / counted - means * means
        normed = (flat - means[None, :, None]) * lax.rsqrt(variance + 1e-05)[None, :, None]
        normed = normed.reshape(LAT, LAT, D) * gn_gain
        hidden = jax.nn.silu(normed).astype(jnp.bfloat16)
        padded = jnp.pad(hidden, ((1, 1), (1, 1), (0, 0)))
        conv_sum = jnp.zeros((LAT * LAT, D), jnp.float32)
        for offset_y in range(3):
            for offset_x in range(3):
                window = padded[offset_y:offset_y + LAT, offset_x:offset_x + LAT].reshape(LAT * LAT, D)
                conv_sum = conv_sum + jnp.dot(window, conv_weight[3 * offset_y + offset_x], preferred_element_type=jnp.float32)
        mixed = (image.reshape(LAT * LAT, D).astype(jnp.float32) + conv_sum).astype(jnp.bfloat16)
        queries = jnp.dot(mixed, weight_q, preferred_element_type=jnp.float32).astype(jnp.bfloat16)
        keys = jnp.dot(plan_image, weight_k, preferred_element_type=jnp.float32).astype(jnp.bfloat16)
        values = jnp.dot(plan_image, weight_v, preferred_element_type=jnp.float32).astype(jnp.bfloat16)
        query_heads = queries.astype(jnp.float32).reshape(LAT * LAT, heads, HEAD)
        key_heads = keys.astype(jnp.float32).reshape(PLAN, heads, HEAD)
        value_heads = values.astype(jnp.float32).reshape(PLAN, heads, HEAD)
        scores = jnp.einsum('nhe,mhe->hnm', query_heads, key_heads) * scale
        maxima = lax.optimization_barrier(jnp.max(scores, axis=-1, keepdims=True))
        expo = jnp.exp(scores - maxima)
        probs = expo / lax.optimization_barrier(jnp.sum(expo, axis=-1, keepdims=True))
        probs_b = probs.astype(jnp.bfloat16)
        attended = jnp.einsum('hnm,mhe->nhe', probs_b.astype(jnp.float32), value_heads)
        attended = attended.reshape(LAT * LAT, D).astype(jnp.bfloat16)
        output = (mixed.astype(jnp.float32) + jnp.dot(attended, weight_o, preferred_element_type=jnp.float32)).astype(jnp.bfloat16)
        grad_in = cot_image.reshape(LAT * LAT, D)
        grad_att = jnp.dot(grad_in, weight_o.T, preferred_element_type=jnp.float32).astype(jnp.bfloat16)
        grad_heads = grad_att.astype(jnp.float32).reshape(LAT * LAT, heads, HEAD)
        dprob = jnp.einsum('nhe,mhe->hnm', grad_heads, value_heads)
        dscore = (probs * (dprob - lax.optimization_barrier(jnp.sum(probs * dprob, axis=-1, keepdims=True))) * scale).astype(jnp.bfloat16)
        dquery = jnp.einsum('hnm,mhe->nhe', dscore.astype(jnp.float32), key_heads)
        dquery = dquery.reshape(LAT * LAT, D).astype(jnp.bfloat16)
        grad_q = carry[0] + jnp.dot(mixed.T, dquery, preferred_element_type=jnp.float32)
        grad_o = carry[1] + jnp.dot(attended.T, grad_in, preferred_element_type=jnp.float32)
        return ((grad_q, grad_o), output.reshape(LAT, LAT, D))
    start = (jnp.zeros((D, D), jnp.float32), jnp.zeros((D, D), jnp.float32))
    totals, block_out = lax.scan(one_image, start, (latents, plan, cotangent))
    factor = 1.0 / math.sqrt(TOKENS)
    weight_grads = jnp.stack([totals[0], totals[1]], axis=1) * factor
    return (block_out, weight_grads)
```

```python
import math

import jax
import jax.numpy as jnp
from jax import lax
from jax.experimental import pallas as pl
from jax.experimental.pallas import tpu as pltpu
from jax.sharding import PartitionSpec as P

GROUPS = 32
HEAD = 64


eps_norm = 1e-05


def with_halo(cells, sides, width):
    for axis, dim in sides:
        count = lax.axis_size(axis)
        ends = count - 1
        head = lax.slice_in_dim(cells, 0, width, axis=dim)
        tail = lax.slice_in_dim(cells, cells.shape[dim] - width, cells.shape[dim], axis=dim)
        cells = jnp.concatenate(
            [
                lax.ppermute(tail, axis, [(i, (i + 1) % count) for i in range(ends)]),
                cells,
                lax.ppermute(head, axis, [((i + 1) % count, i) for i in range(ends)]),
            ],
            axis=dim,
        )
    return cells


def plain_body(latents, plan, conv_weight, gn_gain, attn_weights, cotangent):
    images, band_rows, columns, channels = latents.shape
    heads = channels // HEAD
    per_group = channels // GROUPS
    tokens_here = images * band_rows * columns
    scale = 1.0 / math.sqrt(HEAD)
    flat_input = latents.astype(jnp.float32).reshape(images, band_rows * columns, GROUPS, per_group)
    first_sums = jnp.sum(flat_input, axis=(1, 3))
    second_sums = jnp.sum(flat_input * flat_input, axis=(1, 3))
    first_sums, second_sums = lax.psum((first_sums, second_sums), "spatial")
    counted = float(band_rows * lax.axis_size("spatial") * columns * per_group)
    means = first_sums / counted
    variance = second_sums / counted - means * means
    inverse = lax.rsqrt(variance + eps_norm)
    normed = (flat_input - means[:, None, :, None]) * inverse[:, None, :, None]
    normed = normed.reshape(images, band_rows, columns, channels) * gn_gain
    hidden = jax.nn.silu(normed).astype(jnp.bfloat16)
    padded = with_halo(hidden, (("spatial", 1),), 1)
    padded = jnp.pad(padded, ((0, 0), (0, 0), (1, 1), (0, 0)))
    tapped = jnp.stack(
        [
            padded[:, offset_y : offset_y + band_rows, offset_x : offset_x + columns].reshape(
                tokens_here, channels
            )
            for offset_y in range(3)
            for offset_x in range(3)
        ],
        1,
    )
    conv_sum = jnp.einsum(
        "ntc,tcd->nd",
        tapped,
        lax.all_gather(conv_weight, "dp", axis=1, tiled=True),
        preferred_element_type=jnp.float32,
    )
    mixed = (latents.reshape(tokens_here, channels).astype(jnp.float32) + conv_sum).astype(
        jnp.bfloat16
    )
    weights = lax.all_gather(attn_weights, "dp", axis=1, tiled=True)
    weight_q = weights[0]
    weight_k = weights[1]
    weight_v = weights[2]
    weight_o = weights[3]
    queries = jnp.dot(mixed, weight_q, preferred_element_type=jnp.float32).astype(jnp.bfloat16)
    plan_all = lax.all_gather(plan, "spatial", axis=1, tiled=True)
    plan_flat = plan_all.reshape(-1, channels)
    keys_all = jnp.dot(plan_flat, weight_k, preferred_element_type=jnp.float32).astype(jnp.bfloat16)
    values_all = jnp.dot(plan_flat, weight_v, preferred_element_type=jnp.float32).astype(
        jnp.bfloat16
    )
    keys_all = keys_all.reshape(images, -1, channels)
    values_all = values_all.reshape(images, -1, channels)
    plan_tokens = keys_all.shape[1]
    query_heads = queries.reshape(images, band_rows * columns, heads, HEAD)
    key_heads = keys_all.reshape(images, plan_tokens, heads, HEAD)
    value_heads = values_all.reshape(images, plan_tokens, heads, HEAD)
    scores = (
        jnp.einsum("bnhe,bmhe->bhnm", query_heads, key_heads, preferred_element_type=jnp.float32)
        * scale
    )
    maxima = jnp.max(scores, axis=-1, keepdims=True)
    expo = jnp.exp(scores - maxima)
    probs = expo / jnp.sum(expo, axis=-1, keepdims=True)
    probs_b = probs.astype(jnp.bfloat16)
    attended = jnp.einsum(
        "bhnm,bmhe->bnhe", probs_b, value_heads, preferred_element_type=jnp.float32
    )
    attended = attended.reshape(tokens_here, channels).astype(jnp.bfloat16)
    result = mixed.astype(jnp.float32) + jnp.dot(
        attended, weight_o, preferred_element_type=jnp.float32
    )
    block_out = result.astype(jnp.bfloat16).reshape(images, band_rows, columns, channels)
    grad_flat = cotangent.reshape(tokens_here, channels)
    grad_att = lax.dot_general(
        grad_flat, weight_o, (((1,), (1,)), ((), ())), preferred_element_type=jnp.float32
    )
    grad_att = grad_att.astype(jnp.bfloat16).reshape(images, band_rows * columns, heads, HEAD)
    dprob = jnp.einsum("bnhe,bmhe->bhnm", grad_att, value_heads, preferred_element_type=jnp.float32)
    dscore = (probs * (dprob - jnp.sum(probs * dprob, axis=-1, keepdims=True)) * scale).astype(
        jnp.bfloat16
    )
    dquery = jnp.einsum("bhnm,bmhe->bnhe", dscore, key_heads, preferred_element_type=jnp.float32)
    dquery = dquery.reshape(tokens_here, channels).astype(jnp.bfloat16)
    total_tokens = images * lax.axis_size("dp") * band_rows * lax.axis_size("spatial") * columns
    factor = 1.0 / math.sqrt(total_tokens)
    contract = (((0,), (0,)), ((), ()))
    grad_query = lax.dot_general(mixed, dquery, contract, preferred_element_type=jnp.float32)
    grad_output = lax.dot_general(attended, grad_flat, contract, preferred_element_type=jnp.float32)
    own_rows = lax.psum_scatter(
        jnp.stack([grad_query, grad_output], 1) * factor, "dp", scatter_dimension=0, tiled=True
    )
    weight_grads = lax.psum(own_rows, "spatial")
    return (block_out, weight_grads)


F32 = jnp.float32
BF16 = jnp.bfloat16
LANES = 128
PIECE = 32
VMEM_LIMIT = 56 * 1024 * 1024
NT = (((1,), (1,)), ((), ()))


def params():
    return pltpu.CompilerParams(vmem_limit_bytes=VMEM_LIMIT)


def whole(shape):
    return pl.BlockSpec(shape, lambda *_: (0,) * len(shape))


def smem():
    return pl.BlockSpec(memory_space=pltpu.SMEM)


def lanes_of(shape):
    return lax.broadcasted_iota(jnp.int32, shape, len(shape) - 1)


def pack_kernel(meta, weight, out):
    s = meta[0]
    out[0:9] = weight[:, :, pl.ds(pl.multiple_of(s * LANES, LANES), LANES)]
    rows = lax.broadcasted_iota(jnp.int32, (LANES, LANES), 0)
    cols = lax.broadcasted_iota(jnp.int32, (LANES, LANES), 1)
    last = 4 * LANES
    for dy in range(3):
        total = None
        for dx in range(3):
            pick = (rows == PIECE * s + cols - PIECE * dx) & (cols >= PIECE * dx) & (cols < PIECE * dx + PIECE)
            part = jnp.dot(
                weight[3 * dy + dx, :, last : last + LANES],
                jnp.where(pick, 1.0, 0.0).astype(BF16),
                preferred_element_type=F32,
            )
            total = part if total is None else total + part
        out[9 + dy] = total.astype(BF16)


def pack(meta, conv_weight):
    taps, rows, channels = conv_weight.shape
    return pl.pallas_call(
        pack_kernel,
        grid=(1,),
        in_specs=[smem(), whole(conv_weight.shape)],
        out_specs=whole((12, rows, LANES)),
        out_shape=jax.ShapeDtypeStruct((12, rows, LANES), BF16),
        compiler_params=params(),
        name="pack_conv",
    )(meta, conv_weight)


def norm_kernel(band, columns, shard, count, meta, x0, x1, x2, x3, gain, hidden, own, same_group):
    s = meta[0]
    pieces = (x0, x1, x2, x3)
    channels = gain.shape[1]
    per_group = channels // GROUPS

    @pl.when(pl.program_id(0) == 0)
    def _():
        shape = (channels, channels)
        row_group = jnp.floor((lax.broadcasted_iota(jnp.int32, shape, 0).astype(F32) + 0.5) * (1.0 / per_group))
        col_group = jnp.floor((lax.broadcasted_iota(jnp.int32, shape, 1).astype(F32) + 0.5) * (1.0 / per_group))
        same_group[...] = jnp.where(row_group == col_group, 1.0, 0.0).astype(BF16)

    first = jnp.zeros((1, channels), F32)
    second = jnp.zeros((1, channels), F32)
    for piece in pieces:
        x = piece[...].astype(F32)
        first += jnp.sum(x, axis=0, keepdims=True)
        second += jnp.sum(x * x, axis=0, keepdims=True)
    sums = jnp.concatenate([first, second], axis=0)
    high = sums.astype(BF16)
    rest = sums - high.astype(F32)
    middle = rest.astype(BF16)
    low = (rest - middle.astype(F32)).astype(BF16)
    grouped = sum(jnp.dot(part, same_group[...], preferred_element_type=F32) for part in (high, middle, low))
    mean = grouped[0:1] / count
    variance = grouped[1:2] / count - mean * mean
    factor = lax.rsqrt(variance + eps_norm) * gain[...]

    hidden[:, 0, 0:columns, :] = jnp.zeros((hidden.shape[0], columns, hidden.shape[3]), BF16)
    end = columns + 4 * band
    hidden[:, 0, end : end + columns, :] = jnp.zeros((hidden.shape[0], columns, hidden.shape[3]), BF16)
    rows = 64
    column = lax.rem(lax.broadcasted_iota(jnp.int32, (rows, channels), 0), columns)
    at_start = column == 0
    at_end = column == columns - 1
    spare = jnp.zeros((rows, hidden.shape[3] - 3 * shard), BF16)
    krow = lax.broadcasted_iota(jnp.int32, (LANES, LANES), 0)
    kcol = lax.broadcasted_iota(jnp.int32, (LANES, LANES), 1)
    repeat = jnp.where(krow == PIECE * s + lax.rem(kcol, PIECE), 1.0, 0.0).astype(BF16)
    for r, piece in enumerate(pieces):
        base = (s ^ r) * band
        own[0, pl.ds(pl.multiple_of(base, band), band), 0:LANES] = piece[
            :, pl.ds(pl.multiple_of(s * LANES, LANES), LANES)
        ]
        own[0, pl.ds(pl.multiple_of(base, band), band), LANES : 2 * LANES] = jnp.dot(
            piece[:, 4 * LANES :], repeat, preferred_element_type=F32
        ).astype(BF16)
        for at in range(0, band, rows):
            x = piece[at : at + rows, :].astype(F32)
            y = (x - mean) * factor
            h = y / (1.0 + jnp.exp(-y))
            left = jnp.where(at_start, 0.0, pltpu.roll(h, 1, 0)).astype(BF16)
            right = jnp.where(at_end, 0.0, pltpu.roll(h, rows - 1, 0)).astype(BF16)
            h = h.astype(BF16)
            target = pl.ds(pl.multiple_of(base + columns + at, columns), rows)
            for j in range(channels // shard):
                cut = slice(shard * j, shard * j + shard)
                hidden[j, 0, target, :] = jnp.concatenate([left[:, cut], h[:, cut], right[:, cut], spare], axis=1)


def normalise(meta, pieces, gain, images, band, columns, shards):
    channels = gain.shape[-1]
    shard = channels // shards
    count = float(4 * band * (channels // GROUPS))
    tokens = 4 * band
    piece_spec = pl.BlockSpec((band, channels), lambda b: (b, 0))
    return pl.pallas_call(
        lambda *refs: norm_kernel(band, columns, shard, count, *refs),
        grid=(images,),
        in_specs=[smem()] + [piece_spec] * 4 + [whole((1, channels))],
        out_specs=[
            pl.BlockSpec((shards, 1, tokens + 2 * columns, 2 * LANES), lambda b: (0, b, 0, 0)),
            pl.BlockSpec((1, tokens, 2 * LANES), lambda b: (b, 0, 0)),
        ],
        out_shape=[
            jax.ShapeDtypeStruct((shards, images, tokens + 2 * columns, 2 * LANES), BF16),
            jax.ShapeDtypeStruct((images, tokens, 2 * LANES), BF16),
        ],
        scratch_shapes=[pltpu.VMEM((channels, channels), BF16)],
        compiler_params=params(),
        name="normalise",
    )(meta, *pieces, gain.reshape(1, channels))


def conv_kernel(band, columns, shards, meta, hidden, own, *refs):
    weights = refs[:shards]
    outs = refs[shards : shards + 4]
    taps = refs[shards + 4]
    s = meta[0]
    shard = weights[0].shape[1]

    @pl.when(pl.program_id(0) == 0)
    def _():
        lane = lanes_of((shard, LANES))
        for i, weight in enumerate(weights):
            for dy in range(3):
                for dx in range(3):
                    at = slice(shard * dx, shard * dx + shard)
                    taps[3 * i + dy, at, 0:LANES] = weight[3 * dy + dx]
                    taps[3 * i + dy, at, LANES : 2 * LANES] = jnp.where(
                        (lane >= PIECE * dx) & (lane < PIECE * dx + PIECE), weight[9 + dy], jnp.zeros((), BF16)
                    )
                taps[3 * i + dy, 3 * shard :, :] = jnp.zeros((2 * LANES - 3 * shard, 2 * LANES), BF16)

    group = band // 4
    lane = lanes_of((group, LANES))
    for r, out in enumerate(outs):
        base = (s ^ r) * band
        total = None
        for i in range(shards):
            j = meta[2 + i]
            for dy in range(3):
                window = hidden[j, 0, pl.ds(pl.multiple_of(base + columns * dy, columns), band), :]
                part = jnp.dot(window, taps[3 * i + dy], preferred_element_type=F32)
                total = part if total is None else total + part
        tail = total[:, LANES:]
        tail = tail + pltpu.roll(tail, 2 * PIECE, 1)
        tail = tail + pltpu.roll(tail, PIECE, 1)
        here = own[0, pl.ds(pl.multiple_of(base, band), band), :].astype(F32)
        out[0, 0:band, :] = (here[:, :LANES] + total[:, :LANES]).astype(BF16)
        tail = here[:, LANES:] + tail
        packed = tail[0:group]
        for g in range(1, 4):
            packed = jnp.where(lane >= PIECE * g, tail[group * g : group * g + group], packed)
        out[0, band : band + group, :] = packed.astype(BF16)


def convolve(meta, hidden, own, weights, band, columns):
    images = own.shape[0]
    shards = len(weights)
    rows = band + band // 4
    return pl.pallas_call(
        lambda *refs: conv_kernel(band, columns, shards, *refs),
        grid=(images,),
        in_specs=[
            smem(),
            pl.BlockSpec((shards, 1) + hidden.shape[2:], lambda b: (0, b, 0, 0)),
            pl.BlockSpec((1,) + own.shape[1:], lambda b: (b, 0, 0)),
        ]
        + [whole(w.shape) for w in weights],
        out_specs=[pl.BlockSpec((1, rows, LANES), lambda b: (b, 0, 0))] * 4,
        out_shape=[jax.ShapeDtypeStruct((images, rows, LANES), BF16)] * 4,
        scratch_shapes=[pltpu.VMEM((3 * shards, 2 * LANES, 2 * LANES), BF16)],
        compiler_params=params(),
        name="convolve",
    )(meta, hidden, own, *weights)


def project_kernel(shards, images, band, meta, p0, p1, p2, p3, *refs):
    weights = refs[:shards]
    out, factor, plan = refs[shards : shards + 3]
    s = meta[0]
    core = meta[1]
    shard, channels = weights[0].shape[1:]
    for i, weight in enumerate(weights):
        at = pl.ds(pl.multiple_of(shard * meta[2 + i], 16), shard)
        out[at, :] = weight[core]
        factor[at, :] = weight[1 - core]
    for r, piece in enumerate((p0, p1, p2, p3)):
        rows = piece.shape[0] // images
        for b in range(images):
            plan[pl.ds(pl.multiple_of(rows * (4 * b + (s ^ r)), 16), rows), :] = piece[rows * b : rows * b + rows, :]
    out[channels:, :] = jnp.dot(plan[...], factor[...], preferred_element_type=F32).astype(BF16)


def project(meta, pieces, weights, images, band):
    shard, channels = weights[0].shape[1:]
    latent_rows = images * band
    rows = pieces[0].shape[0] - latent_rows
    plan_spec = pl.BlockSpec((rows, channels), lambda i: (latent_rows // rows, 0))
    return pl.pallas_call(
        lambda *refs: project_kernel(len(weights), images, band, *refs),
        grid=(1,),
        in_specs=[smem()] + [plan_spec] * 4 + [whole(w.shape) for w in weights],
        out_specs=whole((channels + 4 * rows, channels)),
        out_shape=jax.ShapeDtypeStruct((channels + 4 * rows, channels), BF16),
        scratch_shapes=[pltpu.VMEM((channels, channels), BF16), pltpu.VMEM((4 * rows, channels), BF16)],
        compiler_params=params(),
        name="project_plan",
    )(meta, *pieces, *weights)


def prepare_kernel(images, meta, mine, other, cot, weight_q, weight_o, key, key_t, value_t, dprob, kv):
    core = meta[1]
    channels = cot.shape[1]
    plan_rows = (mine.shape[0] - channels) // images

    @pl.when(core == 0)
    def _():
        weight_q[...] = mine[0:channels]
        weight_o[...] = other[0:channels]
        kv[0] = mine[channels:]
        kv[1] = other[channels:]

    @pl.when(core != 0)
    def _():
        weight_q[...] = other[0:channels]
        weight_o[...] = mine[0:channels]
        kv[0] = other[channels:]
        kv[1] = mine[channels:]

    tokens = cot.shape[0] // images
    lane = lanes_of((plan_rows, LANES))
    for b in range(images):
        back = lax.dot_general(
            cot[tokens * b : tokens * b + tokens, :], weight_o[...], NT, preferred_element_type=F32
        ).astype(BF16)
        for p in range(channels // LANES):
            cut = slice(LANES * p, LANES * p + LANES)
            both = []
            for which in range(2):
                part = kv[which, plan_rows * b : plan_rows * b + plan_rows, cut].astype(F32)
                both.append(
                    jnp.concatenate([jnp.where(lane < HEAD, part, 0.0), jnp.where(lane >= HEAD, part, 0.0)], axis=0)
                )
            key[b, p] = both[0].astype(BF16)
            key_t[b, p] = both[0].T.astype(BF16)
            value_t[b, p] = both[1].T.astype(BF16)
            dprob[b, p] = lax.dot_general(both[1].astype(BF16), back[:, cut], NT, preferred_element_type=F32)


def prepare(meta, mine, other, cot, images):
    channels = cot.shape[1]
    pairs = channels // LANES
    tokens = cot.shape[0] // images
    square = (images, pairs, LANES, LANES)
    shapes = [
        ((channels, channels), BF16),
        ((channels, channels), BF16),
        (square, BF16),
        (square, BF16),
        (square, BF16),
        ((images, pairs, LANES, tokens), F32),
    ]
    return pl.pallas_call(
        lambda *refs: prepare_kernel(images, *refs),
        grid=(1,),
        in_specs=[smem(), whole(mine.shape), whole(other.shape), whole(cot.shape)],
        out_specs=[whole(shape) for shape, _ in shapes],
        out_shape=[jax.ShapeDtypeStruct(shape, kind) for shape, kind in shapes],
        scratch_shapes=[pltpu.VMEM((2, mine.shape[0] - channels, channels), BF16)],
        compiler_params=params(),
        name="prepare_attention",
    )(meta, mine, other, cot)


def attend_kernel(images, factor, meta, c0, c1, c2, c3, weight_q, weight_o, key, key_t, value_t, dprob, cot, result, kept, sent, mixed, att_t, dq_t, grads):
    s = meta[0]
    core = meta[1]
    channels = cot.shape[1]
    tokens = cot.shape[0] // images
    group = tokens // 4
    scale = 1.0 / math.sqrt(HEAD)
    lane = lanes_of((group, LANES))
    krow = lax.broadcasted_iota(jnp.int32, (LANES, LANES), 0)
    kcol = lax.broadcasted_iota(jnp.int32, (LANES, LANES), 1)
    same = lax.rem(krow, PIECE) == lax.rem(kcol, PIECE)
    for b in range(images):
        last = jnp.zeros((tokens, LANES), F32)
        for r, chunk in enumerate((c0, c1, c2, c3)):
            source = s ^ r
            mixed[b, :, pl.ds(pl.multiple_of(source * LANES, LANES), LANES)] = chunk[b, 0:tokens, :]
            packed = chunk[b, tokens : tokens + group, :]
            spread = jnp.concatenate(
                [
                    jnp.where((lane >= PIECE * g) & (lane < PIECE * g + PIECE), packed, jnp.zeros((), BF16))
                    for g in range(4)
                ],
                axis=0,
            )
            place = same & (kcol >= PIECE * source) & (kcol < PIECE * source + PIECE)
            last += jnp.dot(spread, jnp.where(place, 1.0, 0.0).astype(BF16), preferred_element_type=F32)
        mixed[b, :, 4 * LANES :] = last.astype(BF16)
        here = mixed[b]
        queries = jnp.dot(here, weight_q[...], preferred_element_type=F32).astype(BF16)
        for p in range(channels // LANES):
            cut = slice(LANES * p, LANES * p + LANES)
            scores = lax.dot_general(key[b, p], queries[:, cut], NT, preferred_element_type=F32) * scale
            scores = scores.reshape(2, HEAD, tokens)
            expo = jnp.exp(scores - jnp.max(scores, axis=1, keepdims=True))
            probs = expo * (1.0 / jnp.sum(expo, axis=1, keepdims=True))
            att_t[b, cut, :] = jnp.dot(
                value_t[b, p], probs.reshape(LANES, tokens).astype(BF16), preferred_element_type=F32
            ).astype(BF16)
            down = dprob[b, p].reshape(2, HEAD, tokens)
            dscore = probs * (down - jnp.sum(probs * down, axis=1, keepdims=True)) * scale
            dq_t[b, cut, :] = jnp.dot(
                key_t[b, p], dscore.reshape(LANES, tokens).astype(BF16), preferred_element_type=F32
            ).astype(BF16)
        attended_t = att_t[b]
        at = slice(tokens * b, tokens * b + tokens)
        result[at, :] = (
            here.astype(F32) + jnp.dot(attended_t.T, weight_o[...], preferred_element_type=F32)
        ).astype(BF16)
        grad_o = jnp.dot(attended_t, cot[at, :], preferred_element_type=F32)
        grad_q = lax.dot_general(here.T, dq_t[b], NT, preferred_element_type=F32)
        if b:
            grad_o += grads[1]
            grad_q += grads[0]
        if b < images - 1:
            grads[0] = grad_q
            grads[1] = grad_o
        else:
            kept[...] = jnp.where(core == 0, grad_q, grad_o) * factor
            sent[...] = jnp.where(core == 0, grad_o, grad_q) * factor


def attend(meta, chunks, prepared, cot, images, factor):
    channels = cot.shape[1]
    tokens = cot.shape[0] // images
    operands = list(chunks) + list(prepared) + [cot]
    grad = jax.ShapeDtypeStruct((channels, channels), F32)
    return pl.pallas_call(
        lambda *refs: attend_kernel(images, factor, *refs),
        grid=(1,),
        in_specs=[smem()] + [whole(x.shape) for x in operands],
        out_specs=[whole(cot.shape), whole(grad.shape), whole(grad.shape)],
        out_shape=[jax.ShapeDtypeStruct(cot.shape, BF16), grad, grad],
        scratch_shapes=[
            pltpu.VMEM((images, tokens, channels), BF16),
            pltpu.VMEM((images, channels, tokens), BF16),
            pltpu.VMEM((images, channels, tokens), BF16),
            pltpu.VMEM((2, channels, channels), F32),
        ],
        compiler_params=params(),
        name="attend",
    )(meta, *operands)


def flip(x, axis, bits):
    count = lax.axis_size(axis)
    return lax.ppermute(x, axis, [(i, i ^ bits) for i in range(count)])


def ring_place(p):
    return 2 * p if p < 4 else 2 * (7 - p) + 1


def around(x, shards):
    forward = [(ring_place(p), ring_place((p + 1) % shards)) for p in range(shards)]
    backward = [(b, a) for a, b in forward]
    pieces = [x]
    ahead = behind = x
    for step in range(shards // 2):
        ahead = lax.ppermute(ahead, "dp", forward)
        pieces.append(ahead)
        if step < shards // 2 - 1:
            behind = lax.ppermute(behind, "dp", backward)
            pieces.append(behind)
    return pieces


def halve(x, index, axis, bits):
    kept = lax.dynamic_index_in_dim(x, index, 0, keepdims=False)
    sent = lax.dynamic_index_in_dim(x, 1 - index, 0, keepdims=False)
    return kept + flip(sent, axis, bits)


def body(latents, plan, conv_weight, gn_gain, attn_weights, cotangent):
    images, band_rows, columns, channels = latents.shape
    shards = lax.axis_size("dp")
    band = band_rows * columns
    me = lax.axis_index("dp")
    s = lax.axis_index("spatial")
    core = s % 2
    high = s // 2
    along_x = me % 2
    along_z = me // 2
    position = jnp.where(along_x == 0, along_z, 7 - along_z)
    offsets = [0, -1, 1, -2, 2, -3, 3, -4]
    where = [(position + o + 8) % 8 for o in offsets]
    held = [jnp.where(p < 4, 2 * p, 2 * (7 - p) + 1) for p in where]
    meta = jnp.stack([s, core] + held).astype(jnp.int32)

    mine = jnp.concatenate([latents.reshape(images * band, channels), plan.reshape(-1, channels)], axis=0)
    across = flip(mine, "spatial", 2)
    pieces = [mine, flip(mine, "spatial", 1), across, flip(across, "spatial", 1)]
    conv_pieces = around(pack(meta, conv_weight), shards)
    pair = lax.dynamic_slice_in_dim(attn_weights, 2 * core, 2, axis=0)
    attn_pieces = around(pair, shards)

    hidden, own = normalise(meta, pieces, gn_gain, images, band, columns, shards)
    outs = convolve(meta, hidden, own, conv_pieces, band, columns)
    chunks = [outs[0]] + [flip(outs[r], "spatial", r) for r in (1, 2, 3)]

    projected = project(meta, pieces, attn_pieces, images, band)
    cot = cotangent.reshape(images * band, channels)
    prepared = prepare(meta, projected, flip(projected, "spatial", 1), cot, images)
    tokens = images * shards * band * lax.axis_size("spatial")
    result, kept, sent = attend(meta, chunks, prepared, cot, images, 1.0 / math.sqrt(tokens))

    total = kept + flip(sent, "spatial", 1)
    total = total.reshape(4, 2, 2, channels // 16, channels).transpose(2, 0, 1, 3, 4)
    total = halve(total, high, "spatial", 2)
    total = halve(total.transpose(1, 0, 2, 3), along_x, "dp", 1)
    total = total.reshape(2, 2, channels // 16, channels)
    total = halve(total.transpose(1, 0, 2, 3), along_z % 2, "dp", 2)
    total = halve(total, along_z // 2, "dp", 4)
    there = flip(total, "spatial", 2)
    rows = jnp.where(high == 0, jnp.concatenate([total, there]), jnp.concatenate([there, total]))
    partner = flip(rows, "spatial", 1)
    grads = jnp.where(core == 0, jnp.stack([rows, partner], 1), jnp.stack([partner, rows], 1))
    return result.reshape(cotangent.shape), grads


def solution(mesh):
    fits = mesh.shape["dp"] == 8 and mesh.shape["spatial"] == 4
    return jax.shard_map(
        body if fits else plain_body,
        mesh=mesh,
        in_specs=(
            P("dp", "spatial", None, None),
            P("dp", "spatial", None),
            P(None, "dp", None),
            P(),
            P(None, "dp", None),
            P("dp", "spatial", None, None),
        ),
        out_specs=(P("dp", "spatial", None, None), P("dp", None, None)),
        check_vma=False,
    )
```

```python
import math

import jax
import jax.numpy as jnp
from jax import lax
from jax.experimental import pallas as pl
from jax.experimental.pallas import tpu as pltpu
from jax.sharding import PartitionSpec as P

GROUPS = 32
HEAD = 64


eps_norm = 1e-05


def with_halo(cells, sides, width):
    for axis, dim in sides:
        count = lax.axis_size(axis)
        ends = count - 1
        head = lax.slice_in_dim(cells, 0, width, axis=dim)
        tail = lax.slice_in_dim(cells, cells.shape[dim] - width, cells.shape[dim], axis=dim)
        cells = jnp.concatenate(
            [
                lax.ppermute(tail, axis, [(i, (i + 1) % count) for i in range(ends)]),
                cells,
                lax.ppermute(head, axis, [((i + 1) % count, i) for i in range(ends)]),
            ],
            axis=dim,
        )
    return cells


def plain_body(latents, plan, conv_weight, gn_gain, attn_weights, cotangent):
    images, band_rows, columns, channels = latents.shape
    heads = channels // HEAD
    per_group = channels // GROUPS
    tokens_here = images * band_rows * columns
    scale = 1.0 / math.sqrt(HEAD)
    flat_input = latents.astype(jnp.float32).reshape(images, band_rows * columns, GROUPS, per_group)
    first_sums = jnp.sum(flat_input, axis=(1, 3))
    second_sums = jnp.sum(flat_input * flat_input, axis=(1, 3))
    first_sums, second_sums = lax.psum((first_sums, second_sums), "spatial")
    counted = float(band_rows * lax.axis_size("spatial") * columns * per_group)
    means = first_sums / counted
    variance = second_sums / counted - means * means
    inverse = lax.rsqrt(variance + eps_norm)
    normed = (flat_input - means[:, None, :, None]) * inverse[:, None, :, None]
    normed = normed.reshape(images, band_rows, columns, channels) * gn_gain
    hidden = jax.nn.silu(normed).astype(jnp.bfloat16)
    padded = with_halo(hidden, (("spatial", 1),), 1)
    padded = jnp.pad(padded, ((0, 0), (0, 0), (1, 1), (0, 0)))
    tapped = jnp.stack(
        [
            padded[:, offset_y : offset_y + band_rows, offset_x : offset_x + columns].reshape(
                tokens_here, channels
            )
            for offset_y in range(3)
            for offset_x in range(3)
        ],
        1,
    )
    conv_sum = jnp.einsum(
        "ntc,tcd->nd",
        tapped,
        lax.all_gather(conv_weight, "dp", axis=1, tiled=True),
        preferred_element_type=jnp.float32,
    )
    mixed = (latents.reshape(tokens_here, channels).astype(jnp.float32) + conv_sum).astype(
        jnp.bfloat16
    )
    weights = lax.all_gather(attn_weights, "dp", axis=1, tiled=True)
    weight_q = weights[0]
    weight_k = weights[1]
    weight_v = weights[2]
    weight_o = weights[3]
    queries = jnp.dot(mixed, weight_q, preferred_element_type=jnp.float32).astype(jnp.bfloat16)
    plan_all = lax.all_gather(plan, "spatial", axis=1, tiled=True)
    plan_flat = plan_all.reshape(-1, channels)
    keys_all = jnp.dot(plan_flat, weight_k, preferred_element_type=jnp.float32).astype(jnp.bfloat16)
    values_all = jnp.dot(plan_flat, weight_v, preferred_element_type=jnp.float32).astype(
        jnp.bfloat16
    )
    keys_all = keys_all.reshape(images, -1, channels)
    values_all = values_all.reshape(images, -1, channels)
    plan_tokens = keys_all.shape[1]
    query_heads = queries.reshape(images, band_rows * columns, heads, HEAD)
    key_heads = keys_all.reshape(images, plan_tokens, heads, HEAD)
    value_heads = values_all.reshape(images, plan_tokens, heads, HEAD)
    scores = (
        jnp.einsum("bnhe,bmhe->bhnm", query_heads, key_heads, preferred_element_type=jnp.float32)
        * scale
    )
    maxima = jnp.max(scores, axis=-1, keepdims=True)
    expo = jnp.exp(scores - maxima)
    probs = expo / jnp.sum(expo, axis=-1, keepdims=True)
    probs_b = probs.astype(jnp.bfloat16)
    attended = jnp.einsum(
        "bhnm,bmhe->bnhe", probs_b, value_heads, preferred_element_type=jnp.float32
    )
    attended = attended.reshape(tokens_here, channels).astype(jnp.bfloat16)
    result = mixed.astype(jnp.float32) + jnp.dot(
        attended, weight_o, preferred_element_type=jnp.float32
    )
    block_out = result.astype(jnp.bfloat16).reshape(images, band_rows, columns, channels)
    grad_flat = cotangent.reshape(tokens_here, channels)
    grad_att = lax.dot_general(
        grad_flat, weight_o, (((1,), (1,)), ((), ())), preferred_element_type=jnp.float32
    )
    grad_att = grad_att.astype(jnp.bfloat16).reshape(images, band_rows * columns, heads, HEAD)
    dprob = jnp.einsum("bnhe,bmhe->bhnm", grad_att, value_heads, preferred_element_type=jnp.float32)
    dscore = (probs * (dprob - jnp.sum(probs * dprob, axis=-1, keepdims=True)) * scale).astype(
        jnp.bfloat16
    )
    dquery = jnp.einsum("bhnm,bmhe->bnhe", dscore, key_heads, preferred_element_type=jnp.float32)
    dquery = dquery.reshape(tokens_here, channels).astype(jnp.bfloat16)
    total_tokens = images * lax.axis_size("dp") * band_rows * lax.axis_size("spatial") * columns
    factor = 1.0 / math.sqrt(total_tokens)
    contract = (((0,), (0,)), ((), ()))
    grad_query = lax.dot_general(mixed, dquery, contract, preferred_element_type=jnp.float32)
    grad_output = lax.dot_general(attended, grad_flat, contract, preferred_element_type=jnp.float32)
    own_rows = lax.psum_scatter(
        jnp.stack([grad_query, grad_output], 1) * factor, "dp", scatter_dimension=0, tiled=True
    )
    weight_grads = lax.psum(own_rows, "spatial")
    return (block_out, weight_grads)


F32 = jnp.float32
BF16 = jnp.bfloat16
LANES = 128
PIECE = 32
VMEM_LIMIT = 24 * 1024 * 1024
NT = (((1,), (1,)), ((), ()))


def params():
    return pltpu.CompilerParams(vmem_limit_bytes=VMEM_LIMIT)


def whole(shape):
    return pl.BlockSpec(memory_space=pltpu.VMEM)


def smem():
    return pl.BlockSpec(memory_space=pltpu.SMEM)


def lanes_of(shape):
    return lax.broadcasted_iota(jnp.int32, shape, len(shape) - 1)


def pack_kernel(meta, weight, out):
    s = meta[0]
    out[0:9] = weight[:, :, pl.ds(pl.multiple_of(s * LANES, LANES), LANES)]
    rows = lax.broadcasted_iota(jnp.int32, (LANES, LANES), 0)
    cols = lax.broadcasted_iota(jnp.int32, (LANES, LANES), 1)
    last = 4 * LANES
    for dy in range(3):
        total = None
        for dx in range(3):
            pick = (rows == PIECE * s + cols - PIECE * dx) & (cols >= PIECE * dx) & (cols < PIECE * dx + PIECE)
            part = jnp.dot(
                weight[3 * dy + dx, :, last : last + LANES],
                jnp.where(pick, 1.0, 0.0).astype(BF16),
                preferred_element_type=F32,
            )
            total = part if total is None else total + part
        out[9 + dy] = total.astype(BF16)


def pack(meta, conv_weight):
    taps, rows, channels = conv_weight.shape
    return pl.pallas_call(
        pack_kernel,
        in_specs=[smem(), whole(conv_weight.shape)],
        out_specs=whole((12, rows, LANES)),
        out_shape=jax.ShapeDtypeStruct((12, rows, LANES), BF16),
        compiler_params=params(),
        name="pack_conv",
    )(meta, conv_weight)


def norm_kernel(image, band, columns, shard, count, meta, x0, x1, x2, x3, gain, hidden, own, same_group):
    s = meta[0]
    pieces = [x.at[image * band : image * band + band] for x in (x0, x1, x2, x3)]
    channels = gain.shape[1]
    per_group = channels // GROUPS
    shape = (channels, channels)
    row_group = jnp.floor((lax.broadcasted_iota(jnp.int32, shape, 0).astype(F32) + 0.5) * (1.0 / per_group))
    col_group = jnp.floor((lax.broadcasted_iota(jnp.int32, shape, 1).astype(F32) + 0.5) * (1.0 / per_group))
    same_group[...] = jnp.where(row_group == col_group, 1.0, 0.0).astype(BF16)

    first = jnp.zeros((1, channels), F32)
    second = jnp.zeros((1, channels), F32)
    for piece in pieces:
        x = piece[...].astype(F32)
        first += jnp.sum(x, axis=0, keepdims=True)
        second += jnp.sum(x * x, axis=0, keepdims=True)
    sums = jnp.concatenate([first, second], axis=0)
    high = sums.astype(BF16)
    rest = sums - high.astype(F32)
    middle = rest.astype(BF16)
    low = (rest - middle.astype(F32)).astype(BF16)
    grouped = sum(jnp.dot(part, same_group[...], preferred_element_type=F32) for part in (high, middle, low))
    mean = grouped[0:1] / count
    variance = grouped[1:2] / count - mean * mean
    factor = lax.rsqrt(variance + eps_norm) * gain[...]

    hidden[:, 0:columns, :] = jnp.zeros((hidden.shape[0], columns, hidden.shape[2]), BF16)
    end = columns + 4 * band
    hidden[:, end : end + columns, :] = jnp.zeros((hidden.shape[0], columns, hidden.shape[2]), BF16)
    rows = 64
    column = lax.rem(lax.broadcasted_iota(jnp.int32, (rows, channels), 0), columns)
    at_start = column == 0
    at_end = column == columns - 1
    spare = jnp.zeros((rows, hidden.shape[2] - 3 * shard), BF16)
    krow = lax.broadcasted_iota(jnp.int32, (LANES, LANES), 0)
    kcol = lax.broadcasted_iota(jnp.int32, (LANES, LANES), 1)
    repeat = jnp.where(krow == PIECE * s + lax.rem(kcol, PIECE), 1.0, 0.0).astype(BF16)
    for r, piece in enumerate(pieces):
        base = (s ^ r) * band
        own[pl.ds(pl.multiple_of(base, band), band), 0:LANES] = piece[
            :, pl.ds(pl.multiple_of(s * LANES, LANES), LANES)
        ]
        own[pl.ds(pl.multiple_of(base, band), band), LANES : 2 * LANES] = jnp.dot(
            piece[:, 4 * LANES :], repeat, preferred_element_type=F32
        ).astype(BF16)
        for at in range(0, band, rows):
            x = piece[at : at + rows, :].astype(F32)
            y = (x - mean) * factor
            h = y / (1.0 + jnp.exp(-y))
            left = jnp.where(at_start, 0.0, pltpu.roll(h, 1, 0)).astype(BF16)
            right = jnp.where(at_end, 0.0, pltpu.roll(h, rows - 1, 0)).astype(BF16)
            h = h.astype(BF16)
            target = pl.ds(pl.multiple_of(base + columns + at, columns), rows)
            for j in range(channels // shard):
                cut = slice(shard * j, shard * j + shard)
                hidden[meta[2 + channels // shard + j], target, :] = jnp.concatenate(
                    [left[:, cut], h[:, cut], right[:, cut], spare], axis=1
                )


def normalise(meta, pieces, gain, image, band, columns, shards):
    channels = gain.shape[-1]
    shard = channels // shards
    count = float(4 * band * (channels // GROUPS))
    tokens = 4 * band
    hidden = (shards, tokens + 2 * columns, 2 * LANES)
    own = (tokens, 2 * LANES)
    return pl.pallas_call(
        lambda *refs: norm_kernel(image, band, columns, shard, count, *refs),
        in_specs=[smem()] + [whole(None)] * 5,
        out_specs=[whole(hidden), whole(own)],
        out_shape=[jax.ShapeDtypeStruct(hidden, BF16), jax.ShapeDtypeStruct(own, BF16)],
        scratch_shapes=[pltpu.VMEM((channels, channels), BF16)],
        compiler_params=params(),
        name="normalise",
    )(meta, *pieces, gain.reshape(1, channels))


def conv_kernel(band, columns, first, count, last, meta, *refs):
    weights = refs[:count]
    hidden = refs[count]
    refs = refs[count + 1 :]
    taps = refs[-1]
    s = meta[0]
    shard = weights[0].shape[1]
    wide = 2 * LANES
    lane = lanes_of((shard, LANES))
    for i, weight in enumerate(weights):
        for dy in range(3):
            for dx in range(3):
                at = slice(wide * i + shard * dx, wide * i + shard * dx + shard)
                taps[dy, at, 0:LANES] = weight[3 * dy + dx]
                taps[dy, at, LANES:wide] = jnp.where(
                    (lane >= PIECE * dx) & (lane < PIECE * dx + PIECE), weight[9 + dy], jnp.zeros((), BF16)
                )
            taps[dy, wide * i + 3 * shard : wide * i + wide, :] = jnp.zeros((wide - 3 * shard, wide), BF16)

    group = band // 4
    lane = lanes_of((group, LANES))
    for r in range(4):
        base = (s ^ r) * band
        here = pl.ds(pl.multiple_of(base, band), band)
        total = refs[0][here, :] if last else None
        for dy in range(3):
            rows = pl.ds(pl.multiple_of(base + columns * dy, columns), band)
            window = jnp.concatenate([hidden[first + k, rows, :] for k in range(count)], axis=1)
            part = jnp.dot(window, taps[dy], preferred_element_type=F32)
            total = part if total is None else total + part
        if not last:
            refs[0][here, :] = total
            continue
        own, out = refs[1], refs[2 + r]
        tail = total[:, LANES:]
        tail = tail + pltpu.roll(tail, 2 * PIECE, 1)
        tail = tail + pltpu.roll(tail, PIECE, 1)
        cells = own[here, :].astype(F32)
        out[0:band, :] = (cells[:, :LANES] + total[:, :LANES]).astype(BF16)
        tail = cells[:, LANES:] + tail
        packed = tail[0:group]
        for g in range(1, 4):
            packed = jnp.where(lane >= PIECE * g, tail[group * g : group * g + group], packed)
        out[band : band + group, :] = packed.astype(BF16)


def convolve(meta, hidden, weights, first, band, columns, partial=None, own=None):
    count = len(weights)
    tokens = hidden.shape[1] - 2 * columns
    last = partial is not None
    operands = list(weights) + [hidden]
    if last:
        operands += [partial, own]
        shapes = [jax.ShapeDtypeStruct((band + band // 4, LANES), BF16)] * 4
    else:
        shapes = [jax.ShapeDtypeStruct((tokens, 2 * LANES), F32)]
    return pl.pallas_call(
        lambda *refs: conv_kernel(band, columns, first, count, last, *refs),
        in_specs=[smem()] + [whole(x.shape) for x in operands],
        out_specs=[whole(shape.shape) for shape in shapes],
        out_shape=shapes,
        scratch_shapes=[pltpu.VMEM((3, 2 * LANES * count, 2 * LANES), BF16)],
        compiler_params=params(),
        name="convolve_last" if last else "convolve_first",
    )(meta, *operands)


def project_kernel(shards, images, meta, p0, p1, p2, p3, *refs):
    weights = refs[:shards]
    out, factor, plan = refs[shards : shards + 3]
    s = meta[0]
    core = meta[1]
    shard, channels = weights[0].shape[1:]
    for i, weight in enumerate(weights):
        at = pl.ds(pl.multiple_of(shard * meta[2 + i], 16), shard)
        out[at, :] = weight[core]
        factor[at, :] = weight[1 - core]
    for r, piece in enumerate((p0, p1, p2, p3)):
        rows = piece.shape[0] // images
        for b in range(images):
            plan[pl.ds(pl.multiple_of(rows * (4 * b + (s ^ r)), 16), rows), :] = piece[rows * b : rows * b + rows, :]
    out[channels:, :] = jnp.dot(plan[...], factor[...], preferred_element_type=F32).astype(BF16)


def project(meta, pieces, weights, images):
    shard, channels = weights[0].shape[1:]
    rows = pieces[0].shape[0]
    return pl.pallas_call(
        lambda *refs: project_kernel(len(weights), images, *refs),
        in_specs=[smem()] + [whole(x.shape) for x in pieces] + [whole(w.shape) for w in weights],
        out_specs=whole((channels + 4 * rows, channels)),
        out_shape=jax.ShapeDtypeStruct((channels + 4 * rows, channels), BF16),
        scratch_shapes=[pltpu.VMEM((channels, channels), BF16), pltpu.VMEM((4 * rows, channels), BF16)],
        compiler_params=params(),
        name="project_plan",
    )(meta, *pieces, *weights)


def prepare_kernel(images, meta, mine, other, cot, weight_q, weight_o, key, key_t, value_t, dprob, kv):
    core = meta[1]
    channels = cot.shape[1]
    plan_rows = (mine.shape[0] - channels) // images

    @pl.when(core == 0)
    def _():
        weight_q[...] = mine[0:channels]
        weight_o[...] = other[0:channels]
        kv[0] = mine[channels:]
        kv[1] = other[channels:]

    @pl.when(core != 0)
    def _():
        weight_q[...] = other[0:channels]
        weight_o[...] = mine[0:channels]
        kv[0] = other[channels:]
        kv[1] = mine[channels:]

    tokens = cot.shape[0] // images
    lane = lanes_of((plan_rows, LANES))
    for b in range(images):
        back = lax.dot_general(
            cot[tokens * b : tokens * b + tokens, :], weight_o[...], NT, preferred_element_type=F32
        ).astype(BF16)
        for p in range(channels // LANES):
            cut = slice(LANES * p, LANES * p + LANES)
            both = []
            for which in range(2):
                part = kv[which, plan_rows * b : plan_rows * b + plan_rows, cut].astype(F32)
                both.append(
                    jnp.concatenate([jnp.where(lane < HEAD, part, 0.0), jnp.where(lane >= HEAD, part, 0.0)], axis=0)
                )
            key[b, p] = both[0].astype(BF16)
            key_t[b, p] = both[0].T.astype(BF16)
            value_t[b, p] = both[1].T.astype(BF16)
            dprob[b, p] = lax.dot_general(both[1].astype(BF16), back[:, cut], NT, preferred_element_type=F32)


def prepare(meta, mine, other, cot, images):
    channels = cot.shape[1]
    pairs = channels // LANES
    tokens = cot.shape[0] // images
    square = (images, pairs, LANES, LANES)
    shapes = [
        ((channels, channels), BF16),
        ((channels, channels), BF16),
        (square, BF16),
        (square, BF16),
        (square, BF16),
        ((images, pairs, LANES, tokens), F32),
    ]
    return pl.pallas_call(
        lambda *refs: prepare_kernel(images, *refs),
        in_specs=[smem(), whole(mine.shape), whole(other.shape), whole(cot.shape)],
        out_specs=[whole(shape) for shape, _ in shapes],
        out_shape=[jax.ShapeDtypeStruct(shape, kind) for shape, kind in shapes],
        scratch_shapes=[pltpu.VMEM((2, mine.shape[0] - channels, channels), BF16)],
        compiler_params=params(),
        name="prepare_attention",
    )(meta, mine, other, cot)


def attend_kernel(image, factor, meta, c0, c1, c2, c3, weight_q, weight_o, key, key_t, value_t, dprob, cot, *refs):
    key, key_t, value_t, dprob = (x.at[image] for x in (key, key_t, value_t, dprob))
    last = factor is not None
    before = refs[: 3 * image] if last else ()
    refs = refs[len(before) :]
    result, mixed_t, att_t, dq_t = refs[:4]
    mixed = refs[-1]
    s = meta[0]
    core = meta[1]
    channels = cot.shape[1]
    tokens = result.shape[0]
    group = tokens // 4
    scale = 1.0 / math.sqrt(HEAD)
    lane = lanes_of((group, LANES))
    krow = lax.broadcasted_iota(jnp.int32, (LANES, LANES), 0)
    kcol = lax.broadcasted_iota(jnp.int32, (LANES, LANES), 1)
    same = lax.rem(krow, PIECE) == lax.rem(kcol, PIECE)
    tail = jnp.zeros((tokens, LANES), F32)
    for r, chunk in enumerate((c0, c1, c2, c3)):
        source = s ^ r
        mixed[:, pl.ds(pl.multiple_of(source * LANES, LANES), LANES)] = chunk[0:tokens, :]
        packed = chunk[tokens : tokens + group, :]
        spread = jnp.concatenate(
            [
                jnp.where((lane >= PIECE * g) & (lane < PIECE * g + PIECE), packed, jnp.zeros((), BF16))
                for g in range(4)
            ],
            axis=0,
        )
        place = same & (kcol >= PIECE * source) & (kcol < PIECE * source + PIECE)
        tail += jnp.dot(spread, jnp.where(place, 1.0, 0.0).astype(BF16), preferred_element_type=F32)
    mixed[:, 4 * LANES :] = tail.astype(BF16)
    here = mixed[...]
    queries = jnp.dot(here, weight_q[...], preferred_element_type=F32).astype(BF16)
    for p in range(channels // LANES):
        cut = slice(LANES * p, LANES * p + LANES)
        scores = lax.dot_general(key[p], queries[:, cut], NT, preferred_element_type=F32) * scale
        scores = scores.reshape(2, HEAD, tokens)
        expo = jnp.exp(scores - jnp.max(scores, axis=1, keepdims=True))
        probs = expo * (1.0 / jnp.sum(expo, axis=1, keepdims=True))
        att_t[cut, :] = jnp.dot(
            value_t[p], probs.reshape(LANES, tokens).astype(BF16), preferred_element_type=F32
        ).astype(BF16)
        down = dprob[p].reshape(2, HEAD, tokens)
        dscore = probs * (down - jnp.sum(probs * down, axis=1, keepdims=True)) * scale
        dq_t[cut, :] = jnp.dot(
            key_t[p], dscore.reshape(LANES, tokens).astype(BF16), preferred_element_type=F32
        ).astype(BF16)
    result[...] = (here.astype(F32) + jnp.dot(att_t[...].T, weight_o[...], preferred_element_type=F32)).astype(BF16)
    mixed_t[...] = here.T
    if last:
        kept, sent = refs[4:6]
        lefts = [before[3 * i : 3 * i + 3] for i in range(image)] + [(mixed_t, att_t, dq_t)]
        all_mixed, all_att, all_dq = (jnp.concatenate([x[k][...] for x in lefts], axis=1) for k in range(3))
        grad_o = jnp.dot(all_att, cot[...], preferred_element_type=F32) * factor
        grad_q = lax.dot_general(all_mixed, all_dq, NT, preferred_element_type=F32) * factor

        @pl.when(core == 0)
        def _():
            kept[...] = grad_q
            sent[...] = grad_o

        @pl.when(core != 0)
        def _():
            kept[...] = grad_o
            sent[...] = grad_q


def attend(meta, chunks, prepared, cot, image, tokens, factor=None, before=()):
    channels = cot.shape[1]
    weight_q, weight_o, *per_image = prepared
    operands = list(chunks) + [weight_q, weight_o] + per_image + [cot] + list(before)
    shapes = [jax.ShapeDtypeStruct((tokens, channels), BF16)] + [jax.ShapeDtypeStruct((channels, tokens), BF16)] * 3
    if factor is not None:
        shapes += [jax.ShapeDtypeStruct((channels, channels), F32)] * 2
    return pl.pallas_call(
        lambda *refs: attend_kernel(image, factor, *refs),
        in_specs=[smem()] + [whole(x.shape) for x in operands],
        out_specs=[whole(x.shape) for x in shapes],
        out_shape=shapes,
        scratch_shapes=[pltpu.VMEM((tokens, channels), BF16)],
        compiler_params=params(),
        name="attend_last" if factor is not None else "attend_first",
    )(meta, *operands)


def quarter_kernel(meta, kept, there, mine, *sends):
    along_x, along_y = meta[18], meta[0] // 2
    rows = mine.shape[0] // 4
    for r, out in enumerate((mine,) + sends):
        parts = []
        for z in range(4):
            at = pl.multiple_of(rows * (2 * (2 * z + (along_x ^ (r % 2))) + (along_y ^ (r // 2))), 8)
            parts.append(kept[pl.ds(at, rows), :] + there[pl.ds(at, rows), :])
        out[...] = jnp.concatenate(parts, axis=0).astype(out.dtype)


def quarters(meta, kept, there):
    rows, channels = kept.shape
    shapes = [jax.ShapeDtypeStruct((rows // 4, channels), kind) for kind in (F32, BF16, BF16, BF16)]
    return pl.pallas_call(
        quarter_kernel,
        in_specs=[smem(), whole(kept.shape), whole(there.shape)],
        out_specs=[whole(x.shape) for x in shapes],
        out_shape=shapes,
        compiler_params=params(),
        name="sum_cores",
    )(meta, kept, there)


def slab_kernel(meta, a, b, c, d, mine, *sends):
    along_z = meta[19]
    rows = mine.shape[0]
    total = a[...] + b[...].astype(F32) + c[...].astype(F32) + d[...].astype(F32)
    for z in range(4):
        part = total[rows * z : rows * z + rows]
        for r, out in enumerate((mine,) + sends):

            @pl.when((along_z ^ r) == z)
            def _(out=out, part=part):
                out[...] = part.astype(out.dtype)


def slabs(meta, parts, kind):
    rows, channels = parts[0].shape
    shapes = [jax.ShapeDtypeStruct((rows // 4, channels), t) for t in (F32, kind, kind, kind)]
    return pl.pallas_call(
        slab_kernel,
        in_specs=[smem()] + [whole(x.shape) for x in parts],
        out_specs=[whole(x.shape) for x in shapes],
        out_shape=shapes,
        compiler_params=params(),
        name="sum_plane",
    )(meta, *parts)


def flip(x, axis, bits):
    count = lax.axis_size(axis)
    return lax.ppermute(x, axis, [(i, i ^ bits) for i in range(count)])


def flip_plane(x, bits):
    count = lax.axis_size("dp") * lax.axis_size("spatial")
    return lax.ppermute(x, ("dp", "spatial"), [(i, i ^ bits) for i in range(count)])


def ring_place(p):
    return 2 * p if p < 4 else 2 * (7 - p) + 1


def step_ring(x, backward):
    shards = lax.axis_size("dp")
    pairs = [(ring_place(p), ring_place((p + 1) % shards)) for p in range(shards)]
    return lax.ppermute(x, "dp", [(b, a) for a, b in pairs] if backward else pairs)


def after(x, *others):
    return lax.optimization_barrier((x,) + others)[0]


def body(latents, plan, conv_weight, gn_gain, attn_weights, cotangent):
    images, band_rows, columns, channels = latents.shape
    shards = lax.axis_size("dp")
    band = band_rows * columns
    me = lax.axis_index("dp")
    s = lax.axis_index("spatial")
    core = s % 2
    high = s // 2
    along_x = me % 2
    along_z = me // 2
    position = jnp.where(along_x == 0, along_z, 7 - along_z)
    offsets = [0, -1, 1, -2, 2, -3, 3, -4]
    where = [(position + o + 8) % 8 for o in offsets]
    held = [jnp.where(p < 4, 2 * p, 2 * (7 - p) + 1) for p in where]
    slots = [sum(jnp.where(h == j, i, 0) for i, h in enumerate(held)) for j in range(shards)]
    meta = jnp.stack([s, core] + held + slots + [along_x, along_z]).astype(jnp.int32)

    wp = pack(meta, conv_weight)
    mine = latents.reshape(images * band, channels)
    plan_mine = plan.reshape(-1, channels)
    pair = lax.dynamic_slice_in_dim(attn_weights, 2 * core, 2, axis=0)
    conv = [wp]
    attn = [pair]
    across = flip(after(mine, wp), "spatial", 2)
    beside = flip(mine, "spatial", 1)
    conv += [step_ring(wp, False), step_ring(wp, True)]
    attn_in = after(pair, wp)
    attn += [step_ring(attn_in, False), step_ring(attn_in, True)]
    conv += [step_ring(conv[1], False), step_ring(conv[2], True)]
    plan_in = after(plan_mine, conv[2])
    plan_across = flip(plan_in, "spatial", 2)
    plan_pieces = [plan_mine, flip(plan_in, "spatial", 1), plan_across, flip(plan_across, "spatial", 1)]
    conv += [step_ring(conv[3], False), step_ring(conv[4], True)]
    a1, a2 = lax.optimization_barrier((attn[1], attn[2], conv[3], conv[4]))[:2]
    attn += [step_ring(a1, False), step_ring(a2, True)]
    latest = after(across, conv[3])
    pieces = [mine, beside, latest, flip(latest, "spatial", 1)]
    normed = [normalise(meta, pieces, gn_gain, b, band, columns, shards) for b in range(images)]
    conv += [step_ring(conv[5], False)]
    a1, a2 = lax.optimization_barrier((attn[3], attn[4], conv[5], conv[6]))[:2]
    attn += [step_ring(a1, False), step_ring(a2, True)]
    attn += [step_ring(after(attn[5], conv[7]), False)]

    partial = [convolve(meta, hidden, conv[:6], 0, band, columns)[0] for hidden, _ in normed]
    chunks = []
    for b in range(images):
        hidden, own = normed[b]
        outs = convolve(meta, hidden, conv[6:], 6, band, columns, partial[b], own)
        chunks.append([outs[0]] + [flip(outs[r], "spatial", r) for r in (1, 2, 3)])

    projected = project(meta, plan_pieces, attn, images)
    cot = cotangent.reshape(images * band, channels)
    prepared = prepare(meta, projected, flip(projected, "spatial", 1), cot, images)
    tokens = images * shards * band * lax.axis_size("spatial")
    results = []
    before = []
    for b in range(images):
        factor = 1.0 / math.sqrt(tokens) if b == images - 1 else None
        result, *rest = attend(meta, chunks[b], prepared, cot, b, band, factor, before if factor else ())
        results.append(result.reshape(1, band_rows, columns, channels))
        before += rest[:3]
    kept, sent = rest[3:]

    mine, *sends = quarters(meta, kept, flip(sent, "spatial", 1))
    moved = [flip_plane(sends[r - 1], 4 * (r % 2) + 2 * (r // 2)) for r in (1, 2, 3)]
    mine, *sends = slabs(meta, [mine] + moved, BF16)
    moved = [flip(sends[r - 1], "dp", 2 * r) for r in (1, 2, 3)]
    total = mine + moved[0].astype(F32) + moved[1].astype(F32) + moved[2].astype(F32)
    there = flip(total, "spatial", 2)
    rows = jnp.where(high == 0, jnp.concatenate([total, there]), jnp.concatenate([there, total]))
    partner = flip(rows, "spatial", 1)
    grads = jnp.where(core == 0, jnp.stack([rows, partner], 1), jnp.stack([partner, rows], 1))
    return jnp.concatenate(results), grads


def solution(mesh):
    fits = mesh.shape["dp"] == 8 and mesh.shape["spatial"] == 4
    return jax.shard_map(
        body if fits else plain_body,
        mesh=mesh,
        in_specs=(
            P("dp", "spatial", None, None),
            P("dp", "spatial", None),
            P(None, "dp", None),
            P(),
            P(None, "dp", None),
            P("dp", "spatial", None, None),
        ),
        out_specs=(P("dp", "spatial", None, None), P("dp", None, None)),
        check_vma=False,
    )
```

```python
import math

import jax
import jax.numpy as jnp
from jax import lax
from jax.experimental import pallas as pl
from jax.experimental.pallas import tpu as pltpu
from jax.sharding import PartitionSpec as P

GROUPS = 32
HEAD = 64


eps_norm = 1e-05


def with_halo(cells, sides, width):
    for axis, dim in sides:
        count = lax.axis_size(axis)
        ends = count - 1
        head = lax.slice_in_dim(cells, 0, width, axis=dim)
        tail = lax.slice_in_dim(cells, cells.shape[dim] - width, cells.shape[dim], axis=dim)
        cells = jnp.concatenate(
            [
                lax.ppermute(tail, axis, [(i, (i + 1) % count) for i in range(ends)]),
                cells,
                lax.ppermute(head, axis, [((i + 1) % count, i) for i in range(ends)]),
            ],
            axis=dim,
        )
    return cells


def plain_body(latents, plan, conv_weight, gn_gain, attn_weights, cotangent):
    images, band_rows, columns, channels = latents.shape
    heads = channels // HEAD
    per_group = channels // GROUPS
    tokens_here = images * band_rows * columns
    scale = 1.0 / math.sqrt(HEAD)
    flat_input = latents.astype(jnp.float32).reshape(images, band_rows * columns, GROUPS, per_group)
    first_sums = jnp.sum(flat_input, axis=(1, 3))
    second_sums = jnp.sum(flat_input * flat_input, axis=(1, 3))
    first_sums, second_sums = lax.psum((first_sums, second_sums), "spatial")
    counted = float(band_rows * lax.axis_size("spatial") * columns * per_group)
    means = first_sums / counted
    variance = second_sums / counted - means * means
    inverse = lax.rsqrt(variance + eps_norm)
    normed = (flat_input - means[:, None, :, None]) * inverse[:, None, :, None]
    normed = normed.reshape(images, band_rows, columns, channels) * gn_gain
    hidden = jax.nn.silu(normed).astype(jnp.bfloat16)
    padded = with_halo(hidden, (("spatial", 1),), 1)
    padded = jnp.pad(padded, ((0, 0), (0, 0), (1, 1), (0, 0)))
    tapped = jnp.stack(
        [
            padded[:, offset_y : offset_y + band_rows, offset_x : offset_x + columns].reshape(
                tokens_here, channels
            )
            for offset_y in range(3)
            for offset_x in range(3)
        ],
        1,
    )
    conv_sum = jnp.einsum(
        "ntc,tcd->nd",
        tapped,
        lax.all_gather(conv_weight, "dp", axis=1, tiled=True),
        preferred_element_type=jnp.float32,
    )
    mixed = (latents.reshape(tokens_here, channels).astype(jnp.float32) + conv_sum).astype(
        jnp.bfloat16
    )
    weights = lax.all_gather(attn_weights, "dp", axis=1, tiled=True)
    weight_q = weights[0]
    weight_k = weights[1]
    weight_v = weights[2]
    weight_o = weights[3]
    queries = jnp.dot(mixed, weight_q, preferred_element_type=jnp.float32).astype(jnp.bfloat16)
    plan_all = lax.all_gather(plan, "spatial", axis=1, tiled=True)
    plan_flat = plan_all.reshape(-1, channels)
    keys_all = jnp.dot(plan_flat, weight_k, preferred_element_type=jnp.float32).astype(jnp.bfloat16)
    values_all = jnp.dot(plan_flat, weight_v, preferred_element_type=jnp.float32).astype(
        jnp.bfloat16
    )
    keys_all = keys_all.reshape(images, -1, channels)
    values_all = values_all.reshape(images, -1, channels)
    plan_tokens = keys_all.shape[1]
    query_heads = queries.reshape(images, band_rows * columns, heads, HEAD)
    key_heads = keys_all.reshape(images, plan_tokens, heads, HEAD)
    value_heads = values_all.reshape(images, plan_tokens, heads, HEAD)
    scores = (
        jnp.einsum("bnhe,bmhe->bhnm", query_heads, key_heads, preferred_element_type=jnp.float32)
        * scale
    )
    maxima = jnp.max(scores, axis=-1, keepdims=True)
    expo = jnp.exp(scores - maxima)
    probs = expo / jnp.sum(expo, axis=-1, keepdims=True)
    probs_b = probs.astype(jnp.bfloat16)
    attended = jnp.einsum(
        "bhnm,bmhe->bnhe", probs_b, value_heads, preferred_element_type=jnp.float32
    )
    attended = attended.reshape(tokens_here, channels).astype(jnp.bfloat16)
    result = mixed.astype(jnp.float32) + jnp.dot(
        attended, weight_o, preferred_element_type=jnp.float32
    )
    block_out = result.astype(jnp.bfloat16).reshape(images, band_rows, columns, channels)
    grad_flat = cotangent.reshape(tokens_here, channels)
    grad_att = lax.dot_general(
        grad_flat, weight_o, (((1,), (1,)), ((), ())), preferred_element_type=jnp.float32
    )
    grad_att = grad_att.astype(jnp.bfloat16).reshape(images, band_rows * columns, heads, HEAD)
    dprob = jnp.einsum("bnhe,bmhe->bhnm", grad_att, value_heads, preferred_element_type=jnp.float32)
    dscore = (probs * (dprob - jnp.sum(probs * dprob, axis=-1, keepdims=True)) * scale).astype(
        jnp.bfloat16
    )
    dquery = jnp.einsum("bhnm,bmhe->bnhe", dscore, key_heads, preferred_element_type=jnp.float32)
    dquery = dquery.reshape(tokens_here, channels).astype(jnp.bfloat16)
    total_tokens = images * lax.axis_size("dp") * band_rows * lax.axis_size("spatial") * columns
    factor = 1.0 / math.sqrt(total_tokens)
    contract = (((0,), (0,)), ((), ()))
    grad_query = lax.dot_general(mixed, dquery, contract, preferred_element_type=jnp.float32)
    grad_output = lax.dot_general(attended, grad_flat, contract, preferred_element_type=jnp.float32)
    own_rows = lax.psum_scatter(
        jnp.stack([grad_query, grad_output], 1) * factor, "dp", scatter_dimension=0, tiled=True
    )
    weight_grads = lax.psum(own_rows, "spatial")
    return (block_out, weight_grads)


F32 = jnp.float32
BF16 = jnp.bfloat16
LANES = 128
PIECE = 32
VMEM_LIMIT = 24 * 1024 * 1024
NT = (((1,), (1,)), ((), ()))


def cost(microseconds):
    return pl.CostEstimate(flops=0, bytes_accessed=microseconds * 3690000, transcendentals=0)


def params():
    return pltpu.CompilerParams(vmem_limit_bytes=VMEM_LIMIT)


def whole(shape):
    return pl.BlockSpec(memory_space=pltpu.VMEM)


def smem():
    return pl.BlockSpec(memory_space=pltpu.SMEM)


def lanes_of(shape):
    return lax.broadcasted_iota(jnp.int32, shape, len(shape) - 1)


def pack_kernel(meta, weight, out):
    s = meta[0]
    out[0:9] = weight[:, :, pl.ds(pl.multiple_of(s * LANES, LANES), LANES)]
    rows = lax.broadcasted_iota(jnp.int32, (LANES, LANES), 0)
    cols = lax.broadcasted_iota(jnp.int32, (LANES, LANES), 1)
    last = 4 * LANES
    for dy in range(3):
        total = None
        for dx in range(3):
            pick = (rows == PIECE * s + cols - PIECE * dx) & (cols >= PIECE * dx) & (cols < PIECE * dx + PIECE)
            part = jnp.dot(
                weight[3 * dy + dx, :, last : last + LANES],
                jnp.where(pick, 1.0, 0.0).astype(BF16),
                preferred_element_type=F32,
            )
            total = part if total is None else total + part
        out[9 + dy] = total.astype(BF16)


def pack(meta, conv_weight):
    taps, rows, channels = conv_weight.shape
    return pl.pallas_call(
        pack_kernel,
        in_specs=[smem(), whole(conv_weight.shape)],
        out_specs=whole((12, rows, LANES)),
        out_shape=jax.ShapeDtypeStruct((12, rows, LANES), BF16),
        compiler_params=params(),
        cost_estimate=cost(1),
        name="pack_conv",
    )(meta, conv_weight)


def stats_kernel(images, band, per_group, count, meta, x0, x1, x2, x3, gain, out):
    channels = gain.shape[1]
    shape = (channels, channels)
    row_group = jnp.floor((lax.broadcasted_iota(jnp.int32, shape, 0).astype(F32) + 0.5) * (1.0 / per_group))
    col_group = jnp.floor((lax.broadcasted_iota(jnp.int32, shape, 1).astype(F32) + 0.5) * (1.0 / per_group))
    same_group = jnp.where(row_group == col_group, 1.0, 0.0).astype(BF16)
    sums = []
    for b in range(images):
        first = jnp.zeros((1, channels), F32)
        second = jnp.zeros((1, channels), F32)
        for piece in (x0, x1, x2, x3):
            x = piece[band * b : band * b + band, :].astype(F32)
            first += jnp.sum(x, axis=0, keepdims=True)
            second += jnp.sum(x * x, axis=0, keepdims=True)
        sums += [first, second]
    sums = jnp.concatenate(sums, axis=0)
    high = sums.astype(BF16)
    rest = sums - high.astype(F32)
    middle = rest.astype(BF16)
    low = (rest - middle.astype(F32)).astype(BF16)
    grouped = sum(jnp.dot(part, same_group, preferred_element_type=F32) for part in (high, middle, low))
    for b in range(images):
        mean = grouped[2 * b : 2 * b + 1] / count
        variance = grouped[2 * b + 1 : 2 * b + 2] / count - mean * mean
        out[b : b + 1, :] = mean
        out[images + b : images + b + 1, :] = lax.rsqrt(variance + eps_norm) * gain[...] * 0.5


def group_stats(meta, pieces, gain, images, band):
    channels = gain.shape[-1]
    per_group = channels // GROUPS
    return pl.pallas_call(
        lambda *refs: stats_kernel(images, band, per_group, float(4 * band * per_group), *refs),
        in_specs=[smem()] + [whole(None)] * 5,
        out_specs=whole(None),
        out_shape=jax.ShapeDtypeStruct((2 * images, channels), F32),
        compiler_params=params(),
        cost_estimate=cost(2),
        name="group_stats",
    )(meta, *pieces, gain.reshape(1, channels))


def norm_kernel(image, images, band, columns, shard, meta, x0, x1, x2, x3, stats, hidden, own):
    s = meta[0]
    pieces = [x.at[image * band : image * band + band] for x in (x0, x1, x2, x3)]
    channels = stats.shape[1]
    mean = stats[image : image + 1, :]
    factor = stats[images + image : images + image + 1, :]
    hidden[:, 0:columns, :] = jnp.zeros((hidden.shape[0], columns, hidden.shape[2]), BF16)
    end = columns + 4 * band
    hidden[:, end : end + columns, :] = jnp.zeros((hidden.shape[0], columns, hidden.shape[2]), BF16)
    rows = 64
    column = lax.rem(lax.broadcasted_iota(jnp.int32, (rows, channels), 0), columns)
    at_start = column == 0
    at_end = column == columns - 1
    spare = jnp.zeros((rows, hidden.shape[2] - 3 * shard), BF16)
    krow = lax.broadcasted_iota(jnp.int32, (LANES, LANES), 0)
    kcol = lax.broadcasted_iota(jnp.int32, (LANES, LANES), 1)
    repeat = jnp.where(krow == PIECE * s + lax.rem(kcol, PIECE), 1.0, 0.0).astype(BF16)
    for r, piece in enumerate(pieces):
        base = (s ^ r) * band
        own[pl.ds(pl.multiple_of(base, band), band), 0:LANES] = piece[
            :, pl.ds(pl.multiple_of(s * LANES, LANES), LANES)
        ]
        own[pl.ds(pl.multiple_of(base, band), band), LANES : 2 * LANES] = jnp.dot(
            piece[:, 4 * LANES :], repeat, preferred_element_type=F32
        ).astype(BF16)
        for at in range(0, band, rows):
            t = (piece[at : at + rows, :].astype(F32) - mean) * factor
            h = t + t * jnp.tanh(t)
            left = jnp.where(at_start, 0.0, pltpu.roll(h, 1, 0)).astype(BF16)
            right = jnp.where(at_end, 0.0, pltpu.roll(h, rows - 1, 0)).astype(BF16)
            h = h.astype(BF16)
            target = pl.ds(pl.multiple_of(base + columns + at, columns), rows)
            for j in range(channels // shard):
                cut = slice(shard * j, shard * j + shard)
                hidden[meta[2 + channels // shard + j], target, :] = jnp.concatenate(
                    [left[:, cut], h[:, cut], right[:, cut], spare], axis=1
                )


def normalise(meta, pieces, stats, image, images, band, columns, shards):
    channels = stats.shape[-1]
    tokens = 4 * band
    hidden = (shards, tokens + 2 * columns, 2 * LANES)
    own = (tokens, 2 * LANES)
    return pl.pallas_call(
        lambda *refs: norm_kernel(image, images, band, columns, channels // shards, *refs),
        in_specs=[smem()] + [whole(None)] * 5,
        out_specs=[whole(hidden), whole(own)],
        out_shape=[jax.ShapeDtypeStruct(hidden, BF16), jax.ShapeDtypeStruct(own, BF16)],
        compiler_params=params(),
        cost_estimate=cost(3),
        name="normalise",
    )(meta, *pieces, stats)


def conv_kernel(band, columns, first, count, last, resume, meta, *refs):
    given = count + 1 if last else count
    weights = refs[:given]
    hidden = refs[given]
    refs = refs[given + 1 :]
    taps = refs[-1]
    s = meta[0]
    shard = weights[0].shape[1]
    wide = 2 * LANES
    lane = lanes_of((shard, LANES))

    def tap(i, k):
        if not last or i < count - 1:
            return weights[i][k]
        half = weights[-1].shape[0]
        return weights[-2][k] if k < half else weights[-1][k - half]

    for i in range(count):
        for dy in range(3):
            for dx in range(3):
                at = slice(wide * i + shard * dx, wide * i + shard * dx + shard)
                taps[dy, at, 0:LANES] = tap(i, 3 * dy + dx)
                taps[dy, at, LANES:wide] = jnp.where(
                    (lane >= PIECE * dx) & (lane < PIECE * dx + PIECE), tap(i, 9 + dy), jnp.zeros((), BF16)
                )
            taps[dy, wide * i + 3 * shard : wide * i + wide, :] = jnp.zeros((wide - 3 * shard, wide), BF16)

    group = band // 4
    lane = lanes_of((group, LANES))
    for r in range(4):
        base = (s ^ r) * band
        here = pl.ds(pl.multiple_of(base, band), band)
        total = refs[0][here, :] if resume else None
        for dy in range(3):
            rows = pl.ds(pl.multiple_of(base + columns * dy, columns), band)
            window = jnp.concatenate([hidden[first + k, rows, :] for k in range(count)], axis=1)
            part = jnp.dot(window, taps[dy], preferred_element_type=F32)
            total = part if total is None else total + part
        if not last:
            refs[0][here, :] = total
            continue
        own, out = refs[resume], refs[resume + 1 + r]
        tail = total[:, LANES:]
        tail = tail + pltpu.roll(tail, 2 * PIECE, 1)
        tail = tail + pltpu.roll(tail, PIECE, 1)
        cells = own[here, :].astype(F32)
        out[0:band, :] = (cells[:, :LANES] + total[:, :LANES]).astype(BF16)
        tail = cells[:, LANES:] + tail
        packed = tail[0:group]
        for g in range(1, 4):
            packed = jnp.where(lane >= PIECE * g, tail[group * g : group * g + group], packed)
        out[band : band + group, :] = packed.astype(BF16)


def convolve(meta, hidden, weights, band, columns, partial=None, own=None):
    tokens = hidden.shape[1] - 2 * columns
    last = own is not None
    resume = int(partial is not None)
    count = len(weights) - 1 if last else len(weights)
    first = hidden.shape[0] - count if last else 0
    operands = list(weights) + [hidden]
    if last:
        operands += [partial, own] if resume else [own]
        shapes = [jax.ShapeDtypeStruct((band + band // 4, LANES), BF16)] * 4
    else:
        shapes = [jax.ShapeDtypeStruct((tokens, 2 * LANES), F32)]
    return pl.pallas_call(
        lambda *refs: conv_kernel(band, columns, first, count, last, resume, *refs),
        in_specs=[smem()] + [whole(x.shape) for x in operands],
        out_specs=[whole(shape.shape) for shape in shapes],
        out_shape=shapes,
        scratch_shapes=[pltpu.VMEM((3, 2 * LANES * count, 2 * LANES), BF16)],
        compiler_params=params(),
        cost_estimate=cost(3),
        name="convolve_last" if last else "convolve_first",
    )(meta, *operands)


def project_kernel(shards, images, count, meta, p0, p1, p2, p3, *refs):
    weights = refs[:shards]
    out, factor, plan = refs[shards : shards + 3]
    s = meta[0]
    core = meta[1]
    shard, channels = weights[0].shape[1:]
    for i in range(shards):
        at = pl.ds(pl.multiple_of(shard * meta[2 + i], 16), shard)
        out[at, :] = weights[i][core]
        factor[at, :] = weights[i][1 - core]
    for r, piece in enumerate((p0, p1, p2, p3)):
        rows = count // images
        start = piece.shape[0] - count
        for b in range(images):
            plan[pl.ds(pl.multiple_of(rows * (4 * b + (s ^ r)), 16), rows), :] = piece[
                start + rows * b : start + rows * b + rows, :
            ]
    out[channels:, :] = jnp.dot(plan[...], factor[...], preferred_element_type=F32).astype(BF16)


def project(meta, pieces, weights, images, rows):
    shard, channels = weights[0].shape[1:]
    return pl.pallas_call(
        lambda *refs: project_kernel(len(weights), images, rows, *refs),
        in_specs=[smem()] + [whole(x.shape) for x in pieces] + [whole(w.shape) for w in weights],
        out_specs=whole((channels + 4 * rows, channels)),
        out_shape=jax.ShapeDtypeStruct((channels + 4 * rows, channels), BF16),
        scratch_shapes=[pltpu.VMEM((channels, channels), BF16), pltpu.VMEM((4 * rows, channels), BF16)],
        compiler_params=params(),
        cost_estimate=cost(1),
        name="project_plan",
    )(meta, *pieces, *weights)


def prepare_kernel(images, meta, mine, other, cot, weight_q, weight_o, key, key_t, value_t, dprob, cot_t, kv):
    core = meta[1]
    channels = cot.shape[1]
    plan_rows = (mine.shape[0] - channels) // images

    @pl.when(core == 0)
    def _():
        weight_q[...] = mine[0:channels]
        weight_o[...] = other[0:channels]
        kv[0] = mine[channels:]
        kv[1] = other[channels:]

    @pl.when(core != 0)
    def _():
        weight_q[...] = other[0:channels]
        weight_o[...] = mine[0:channels]
        kv[0] = other[channels:]
        kv[1] = mine[channels:]

    tokens = cot.shape[0] // images
    lane = lanes_of((plan_rows, LANES))
    for b in range(images):
        cot_t[b] = cot[tokens * b : tokens * b + tokens, :].T
        back = lax.dot_general(
            cot[tokens * b : tokens * b + tokens, :], weight_o[...], NT, preferred_element_type=F32
        ).astype(BF16)
        for p in range(channels // LANES):
            cut = slice(LANES * p, LANES * p + LANES)
            both = []
            for which in range(2):
                part = kv[which, plan_rows * b : plan_rows * b + plan_rows, cut].astype(F32)
                both.append(
                    jnp.concatenate([jnp.where(lane < HEAD, part, 0.0), jnp.where(lane >= HEAD, part, 0.0)], axis=0)
                )
            key[b, p] = both[0].astype(BF16)
            key_t[b, p] = both[0].T.astype(BF16)
            value_t[b, p] = both[1].T.astype(BF16)
            dprob[b, p] = lax.dot_general(both[1].astype(BF16), back[:, cut], NT, preferred_element_type=F32)


def prepare(meta, mine, other, cot, images):
    channels = cot.shape[1]
    pairs = channels // LANES
    tokens = cot.shape[0] // images
    square = (images, pairs, LANES, LANES)
    shapes = [
        ((channels, channels), BF16),
        ((channels, channels), BF16),
        (square, BF16),
        (square, BF16),
        (square, BF16),
        ((images, pairs, LANES, tokens), F32),
        ((images, channels, tokens), BF16),
    ]
    return pl.pallas_call(
        lambda *refs: prepare_kernel(images, *refs),
        in_specs=[smem(), whole(mine.shape), whole(other.shape), whole(cot.shape)],
        out_specs=[whole(shape) for shape, _ in shapes],
        out_shape=[jax.ShapeDtypeStruct(shape, kind) for shape, kind in shapes],
        scratch_shapes=[pltpu.VMEM((2, mine.shape[0] - channels, channels), BF16)],
        compiler_params=params(),
        cost_estimate=cost(2),
        name="prepare_attention",
    )(meta, mine, other, cot)


def attend_kernel(image, meta, c0, c1, c2, c3, weight_q, weight_o, key, key_t, value_t, dprob, cot_t, result, kept, sent, mixed, att_t, dq_t):
    s = meta[0]
    core = meta[1]
    tokens, channels = result.shape
    group = tokens // 4
    scale = 1.0 / math.sqrt(HEAD)
    lane = lanes_of((group, LANES))
    krow = lax.broadcasted_iota(jnp.int32, (LANES, LANES), 0)
    kcol = lax.broadcasted_iota(jnp.int32, (LANES, LANES), 1)
    same = lax.rem(krow, PIECE) == lax.rem(kcol, PIECE)
    tail = jnp.zeros((tokens, LANES), F32)
    for r, chunk in enumerate((c0, c1, c2, c3)):
        source = s ^ r
        mixed[:, pl.ds(pl.multiple_of(source * LANES, LANES), LANES)] = chunk[0:tokens, :]
        packed = chunk[tokens : tokens + group, :]
        spread = jnp.concatenate(
            [
                jnp.where((lane >= PIECE * g) & (lane < PIECE * g + PIECE), packed, jnp.zeros((), BF16))
                for g in range(4)
            ],
            axis=0,
        )
        place = same & (kcol >= PIECE * source) & (kcol < PIECE * source + PIECE)
        tail += jnp.dot(spread, jnp.where(place, 1.0, 0.0).astype(BF16), preferred_element_type=F32)
    mixed[:, 4 * LANES :] = tail.astype(BF16)
    here = mixed[...]
    queries = jnp.dot(here, weight_q[...], preferred_element_type=F32).astype(BF16)
    for p in range(channels // LANES):
        cut = slice(LANES * p, LANES * p + LANES)
        scores = lax.dot_general(key[image, p], queries[:, cut], NT, preferred_element_type=F32) * scale
        scores = scores.reshape(2, HEAD, tokens)
        expo = jnp.exp(scores - jnp.max(scores, axis=1, keepdims=True))
        probs = expo * (1.0 / jnp.sum(expo, axis=1, keepdims=True))
        att_t[cut, :] = jnp.dot(
            value_t[image, p], probs.reshape(LANES, tokens).astype(BF16), preferred_element_type=F32
        ).astype(BF16)
        down = dprob[image, p].reshape(2, HEAD, tokens)
        dscore = probs * (down - jnp.sum(probs * down, axis=1, keepdims=True)) * scale
        dq_t[cut, :] = jnp.dot(
            key_t[image, p], dscore.reshape(LANES, tokens).astype(BF16), preferred_element_type=F32
        ).astype(BF16)

    @pl.when(core == 0)
    def _():
        kept[0] = here.T
        kept[1] = dq_t[...]
        sent[0] = att_t[...]
        sent[1] = cot_t[image]

    @pl.when(core != 0)
    def _():
        sent[0] = here.T
        sent[1] = dq_t[...]
        kept[0] = att_t[...]
        kept[1] = cot_t[image]

    result[...] = (here.astype(F32) + jnp.dot(att_t[...].T, weight_o[...], preferred_element_type=F32)).astype(BF16)


def attend(meta, chunks, prepared, image, tokens):
    channels = prepared[0].shape[0]
    operands = list(chunks) + list(prepared)
    both = jax.ShapeDtypeStruct((2, channels, tokens), BF16)
    return pl.pallas_call(
        lambda *refs: attend_kernel(image, *refs),
        in_specs=[smem()] + [whole(x.shape) for x in operands],
        out_specs=[whole(None)] * 3,
        out_shape=[jax.ShapeDtypeStruct((tokens, channels), BF16), both, both],
        scratch_shapes=[pltpu.VMEM((tokens, channels), BF16)] + [pltpu.VMEM((channels, tokens), BF16)] * 2,
        compiler_params=params(),
        cost_estimate=cost(3),
        name="attend",
    )(meta, *operands)


def gradient(parts):
    channels = parts[0].shape[1]

    def kernel(*refs):
        left, right = (jnp.concatenate([part[k] for part in refs[:-1]], axis=1) for k in range(2))
        refs[-1][...] = lax.dot_general(left, right, NT, preferred_element_type=F32)

    return pl.pallas_call(
        kernel,
        in_specs=[whole(x.shape) for x in parts],
        out_specs=whole(None),
        out_shape=jax.ShapeDtypeStruct((channels, channels), F32),
        compiler_params=params(),
        cost_estimate=cost(1),
        name="gradient_first",
    )(*parts)


def quarter_kernel(factor, meta, partial, part, mine, *refs):
    sends, total = refs[:-1], refs[-1]
    total[...] = (partial[...] + lax.dot_general(part[0], part[1], NT, preferred_element_type=F32)) * factor
    along_x, along_y = meta[18], meta[0] // 2
    rows = mine.shape[0] // 4
    for r, out in enumerate((mine,) + sends):
        parts = []
        for z in range(4):
            at = pl.multiple_of(rows * (2 * (2 * z + (along_x ^ (r % 2))) + (along_y ^ (r // 2))), 8)
            parts.append(total[pl.ds(at, rows), :])
        out[...] = jnp.concatenate(parts, axis=0).astype(out.dtype)


def quarters(meta, partial, part, factor):
    rows, channels = partial.shape
    shapes = [jax.ShapeDtypeStruct((rows // 4, channels), kind) for kind in (F32, BF16, BF16, BF16)]
    return pl.pallas_call(
        lambda *refs: quarter_kernel(factor, *refs),
        in_specs=[smem(), whole(partial.shape), whole(part.shape)],
        out_specs=[whole(x.shape) for x in shapes],
        out_shape=shapes,
        scratch_shapes=[pltpu.VMEM((rows, channels), F32)],
        compiler_params=params(),
        cost_estimate=cost(1),
        name="gradient_last",
    )(meta, partial, part)


def finish_kernel(meta, mine, beside, across, corner, out):
    core, high = meta[1], meta[0] // 2
    rows = mine.shape[0]

    def ordered(a, b):
        first = jnp.where(high == 0, a[...], b[...])
        second = jnp.where(high == 0, b[...], a[...])
        return jnp.concatenate([first, second], axis=0)

    own, other = ordered(mine, across), ordered(beside, corner)
    out[:, 0, :] = jnp.where(core == 0, own, other)
    out[:, 1, :] = jnp.where(core == 0, other, own)


def finish(meta, parts):
    rows, channels = parts[0].shape
    return pl.pallas_call(
        finish_kernel,
        in_specs=[smem()] + [whole(x.shape) for x in parts],
        out_specs=whole(None),
        out_shape=jax.ShapeDtypeStruct((2 * rows, 2, channels), F32),
        compiler_params=params(),
        cost_estimate=cost(1),
        name="finish",
    )(meta, *parts)


def slab_kernel(meta, a, b, c, d, mine, *sends):
    along_z = meta[19]
    rows = mine.shape[0]
    total = a[...] + b[...].astype(F32) + c[...].astype(F32) + d[...].astype(F32)
    for z in range(4):
        part = total[rows * z : rows * z + rows]
        for r, out in enumerate((mine,) + sends):

            @pl.when((along_z ^ r) == z)
            def _(out=out, part=part):
                out[...] = part.astype(out.dtype)


def slabs(meta, parts, kinds):
    rows, channels = parts[0].shape
    shapes = [jax.ShapeDtypeStruct((rows // 4, channels), t) for t in kinds]
    return pl.pallas_call(
        slab_kernel,
        in_specs=[smem()] + [whole(x.shape) for x in parts],
        out_specs=[whole(x.shape) for x in shapes],
        out_shape=shapes,
        compiler_params=params(),
        cost_estimate=cost(1),
        name="sum_plane",
    )(meta, *parts)


def flip(x, axis, bits):
    count = lax.axis_size(axis)
    return lax.ppermute(x, axis, [(i, i ^ bits) for i in range(count)])


def flip_plane(x, bits):
    count = lax.axis_size("dp") * lax.axis_size("spatial")
    return lax.ppermute(x, ("dp", "spatial"), [(i, i ^ bits) for i in range(count)])


def ring_place(p):
    return 2 * p if p < 4 else 2 * (7 - p) + 1


def step_ring(x, backward):
    shards = lax.axis_size("dp")
    pairs = [(ring_place(p), ring_place((p + 1) % shards)) for p in range(shards)]
    return lax.ppermute(x, "dp", [(b, a) for a, b in pairs] if backward else pairs)


def after(values, *others):
    return lax.optimization_barrier((tuple(values), others))[0]


def body(latents, plan, conv_weight, gn_gain, attn_weights, cotangent):
    images, band_rows, columns, channels = latents.shape
    shards = lax.axis_size("dp")
    band = band_rows * columns
    me = lax.axis_index("dp")
    s = lax.axis_index("spatial")
    core = s % 2
    high = s // 2
    along_x = me % 2
    along_z = me // 2
    position = jnp.where(along_x == 0, along_z, 7 - along_z)
    offsets = [0, -1, 1, -2, 2, -3, 3, -4]
    where = [(position + o + 8) % 8 for o in offsets]
    held = [jnp.where(p < 4, 2 * p, 2 * (7 - p) + 1) for p in where]
    slots = [sum(jnp.where(h == j, i, 0) for i, h in enumerate(held)) for j in range(shards)]
    meta = jnp.stack([s, core] + held + slots + [along_x, along_z]).astype(jnp.int32)

    wp = pack(meta, conv_weight)
    mine = jnp.concatenate([latents.reshape(images * band, channels), plan.reshape(-1, channels)])
    pair = lax.dynamic_slice_in_dim(attn_weights, 2 * core, 2, axis=0)
    mine_in, pair_in = after((mine, pair), wp)
    across = flip(mine_in, "spatial", 2)
    conv = [wp, step_ring(wp, False), step_ring(wp, True)]
    attn = [pair, step_ring(pair_in, False), step_ring(pair_in, True)]
    for _ in range(2):
        conv += [step_ring(conv[-2], False), step_ring(conv[-1], True)]
        attn += [step_ring(attn[-2], False), step_ring(attn[-1], True)]
    (across,) = after([across], *conv[3:5], *attn[3:5])
    pieces = [mine, flip(mine, "spatial", 1), across, flip(across, "spatial", 1)]
    stats = group_stats(meta, pieces, gn_gain, images, band)
    normed = [normalise(meta, pieces, stats, b, images, band, columns, shards) for b in range(images)]

    c5, c6, a5 = after((conv[5], conv[6], attn[5]), *(x[1] for x in normed))
    half = c5.shape[0] // 2
    c7, c8, a7 = step_ring(c5[:half], False), step_ring(c6[half:], True), step_ring(a5, False)
    partial = [convolve(meta, hidden, conv[:6], band, columns)[0] for hidden, _ in normed]
    c6, c7, c8, a7, *partial = after((conv[6], c7, c8, a7, *partial))

    chunks = []
    for b in range(images):
        outs = convolve(meta, normed[b][0], [c6, c7, c8], band, columns, partial[b], normed[b][1])
        chunks.append([outs[0]] + [flip(outs[r], "spatial", r) for r in (1, 2, 3)])

    projected = project(meta, pieces, attn[:7] + [a7], images, plan.shape[0] * plan.shape[1])
    cot = cotangent.reshape(images * band, channels)
    prepared = prepare(meta, projected, flip(projected, "spatial", 1), cot, images)
    tokens = images * shards * band * lax.axis_size("spatial")
    results = []
    kept = []
    given = []
    for b in range(images):
        result, keep, send = attend(meta, chunks[b], prepared, b, band)
        results.append(result.reshape(1, band_rows, columns, channels))
        kept.append(keep)
        given.append(flip(send, "spatial", 1))
    partial = gradient(kept + given[:-1])
    mine, *sends = quarters(meta, partial, given[-1], 1.0 / math.sqrt(tokens))
    moved = [flip_plane(sends[r - 1], 4 * (r % 2) + 2 * (r // 2)) for r in (1, 2, 3)]
    mine, *sends = slabs(meta, [mine] + moved, (F32, F32, F32, BF16))
    moved = [flip(sends[r - 1], "dp", 2 * r).astype(F32) for r in (1, 2, 3)]
    total = mine + moved[0] + moved[1] + moved[2]
    grads = finish(meta, [total] + [flip(total, "spatial", r) for r in (1, 2, 3)])
    return jnp.concatenate(results), grads


def solution(mesh):
    fits = mesh.shape["dp"] == 8 and mesh.shape["spatial"] == 4
    return jax.shard_map(
        body if fits else plain_body,
        mesh=mesh,
        in_specs=(
            P("dp", "spatial", None, None),
            P("dp", "spatial", None),
            P(None, "dp", None),
            P(),
            P(None, "dp", None),
            P("dp", "spatial", None, None),
        ),
        out_specs=(P("dp", "spatial", None, None), P("dp", None, None)),
        check_vma=False,
    )
```

```python
import math

import jax
import jax.numpy as jnp
from jax import lax
from jax.experimental import pallas as pl
from jax.experimental.pallas import tpu as pltpu
from jax.sharding import PartitionSpec as P

GROUPS = 32
HEAD = 64


eps_norm = 1e-05


def with_halo(cells, sides, width):
    for axis, dim in sides:
        count = lax.axis_size(axis)
        ends = count - 1
        head = lax.slice_in_dim(cells, 0, width, axis=dim)
        tail = lax.slice_in_dim(cells, cells.shape[dim] - width, cells.shape[dim], axis=dim)
        cells = jnp.concatenate(
            [
                lax.ppermute(tail, axis, [(i, (i + 1) % count) for i in range(ends)]),
                cells,
                lax.ppermute(head, axis, [((i + 1) % count, i) for i in range(ends)]),
            ],
            axis=dim,
        )
    return cells


def plain_body(latents, plan, conv_weight, gn_gain, attn_weights, cotangent):
    images, band_rows, columns, channels = latents.shape
    heads = channels // HEAD
    per_group = channels // GROUPS
    tokens_here = images * band_rows * columns
    scale = 1.0 / math.sqrt(HEAD)
    flat_input = latents.astype(jnp.float32).reshape(images, band_rows * columns, GROUPS, per_group)
    first_sums = jnp.sum(flat_input, axis=(1, 3))
    second_sums = jnp.sum(flat_input * flat_input, axis=(1, 3))
    first_sums, second_sums = lax.psum((first_sums, second_sums), "spatial")
    counted = float(band_rows * lax.axis_size("spatial") * columns * per_group)
    means = first_sums / counted
    variance = second_sums / counted - means * means
    inverse = lax.rsqrt(variance + eps_norm)
    normed = (flat_input - means[:, None, :, None]) * inverse[:, None, :, None]
    normed = normed.reshape(images, band_rows, columns, channels) * gn_gain
    hidden = jax.nn.silu(normed).astype(jnp.bfloat16)
    padded = with_halo(hidden, (("spatial", 1),), 1)
    padded = jnp.pad(padded, ((0, 0), (0, 0), (1, 1), (0, 0)))
    tapped = jnp.stack(
        [
            padded[:, offset_y : offset_y + band_rows, offset_x : offset_x + columns].reshape(
                tokens_here, channels
            )
            for offset_y in range(3)
            for offset_x in range(3)
        ],
        1,
    )
    conv_sum = jnp.einsum(
        "ntc,tcd->nd",
        tapped,
        lax.all_gather(conv_weight, "dp", axis=1, tiled=True),
        preferred_element_type=jnp.float32,
    )
    mixed = (latents.reshape(tokens_here, channels).astype(jnp.float32) + conv_sum).astype(
        jnp.bfloat16
    )
    weights = lax.all_gather(attn_weights, "dp", axis=1, tiled=True)
    weight_q = weights[0]
    weight_k = weights[1]
    weight_v = weights[2]
    weight_o = weights[3]
    queries = jnp.dot(mixed, weight_q, preferred_element_type=jnp.float32).astype(jnp.bfloat16)
    plan_all = lax.all_gather(plan, "spatial", axis=1, tiled=True)
    plan_flat = plan_all.reshape(-1, channels)
    keys_all = jnp.dot(plan_flat, weight_k, preferred_element_type=jnp.float32).astype(jnp.bfloat16)
    values_all = jnp.dot(plan_flat, weight_v, preferred_element_type=jnp.float32).astype(
        jnp.bfloat16
    )
    keys_all = keys_all.reshape(images, -1, channels)
    values_all = values_all.reshape(images, -1, channels)
    plan_tokens = keys_all.shape[1]
    query_heads = queries.reshape(images, band_rows * columns, heads, HEAD)
    key_heads = keys_all.reshape(images, plan_tokens, heads, HEAD)
    value_heads = values_all.reshape(images, plan_tokens, heads, HEAD)
    scores = (
        jnp.einsum("bnhe,bmhe->bhnm", query_heads, key_heads, preferred_element_type=jnp.float32)
        * scale
    )
    maxima = jnp.max(scores, axis=-1, keepdims=True)
    expo = jnp.exp(scores - maxima)
    probs = expo / jnp.sum(expo, axis=-1, keepdims=True)
    probs_b = probs.astype(jnp.bfloat16)
    attended = jnp.einsum(
        "bhnm,bmhe->bnhe", probs_b, value_heads, preferred_element_type=jnp.float32
    )
    attended = attended.reshape(tokens_here, channels).astype(jnp.bfloat16)
    result = mixed.astype(jnp.float32) + jnp.dot(
        attended, weight_o, preferred_element_type=jnp.float32
    )
    block_out = result.astype(jnp.bfloat16).reshape(images, band_rows, columns, channels)
    grad_flat = cotangent.reshape(tokens_here, channels)
    grad_att = lax.dot_general(
        grad_flat, weight_o, (((1,), (1,)), ((), ())), preferred_element_type=jnp.float32
    )
    grad_att = grad_att.astype(jnp.bfloat16).reshape(images, band_rows * columns, heads, HEAD)
    dprob = jnp.einsum("bnhe,bmhe->bhnm", grad_att, value_heads, preferred_element_type=jnp.float32)
    dscore = (probs * (dprob - jnp.sum(probs * dprob, axis=-1, keepdims=True)) * scale).astype(
        jnp.bfloat16
    )
    dquery = jnp.einsum("bhnm,bmhe->bnhe", dscore, key_heads, preferred_element_type=jnp.float32)
    dquery = dquery.reshape(tokens_here, channels).astype(jnp.bfloat16)
    total_tokens = images * lax.axis_size("dp") * band_rows * lax.axis_size("spatial") * columns
    factor = 1.0 / math.sqrt(total_tokens)
    contract = (((0,), (0,)), ((), ()))
    grad_query = lax.dot_general(mixed, dquery, contract, preferred_element_type=jnp.float32)
    grad_output = lax.dot_general(attended, grad_flat, contract, preferred_element_type=jnp.float32)
    own_rows = lax.psum_scatter(
        jnp.stack([grad_query, grad_output], 1) * factor, "dp", scatter_dimension=0, tiled=True
    )
    weight_grads = lax.psum(own_rows, "spatial")
    return (block_out, weight_grads)


F32 = jnp.float32
BF16 = jnp.bfloat16
LANES = 128
PIECE = 32
VMEM_LIMIT = 24 * 1024 * 1024
NT = (((1,), (1,)), ((), ()))


def cost(microseconds):
    return pl.CostEstimate(flops=0, bytes_accessed=microseconds * 3690000, transcendentals=0)


def params():
    return pltpu.CompilerParams(vmem_limit_bytes=VMEM_LIMIT)


def whole(shape):
    return pl.BlockSpec(memory_space=pltpu.VMEM)


def smem():
    return pl.BlockSpec(memory_space=pltpu.SMEM)


def lanes_of(shape):
    return lax.broadcasted_iota(jnp.int32, shape, len(shape) - 1)


TAPS = 12


def pack_kernel(conv_hbm, attn_hbm, latents_hbm, plan_hbm, out, rows_out, meta, weight, matrix, sems):
    s = lax.axis_index("spatial")
    core, high = s % 2, s // 2
    split = latents_hbm.shape[0]
    copies = [
        pltpu.make_async_copy(conv_hbm, weight, sems.at[0]),
        pltpu.make_async_copy(attn_hbm.at[jnp.where(high == 0, 3 * core, 1 + core)], matrix, sems.at[1]),
        pltpu.make_async_copy(latents_hbm, rows_out.at[pl.ds(0, split)], sems.at[2]),
        pltpu.make_async_copy(plan_hbm, rows_out.at[pl.ds(split, plan_hbm.shape[0])], sems.at[3]),
    ]
    for copy in copies:
        copy.start()
    me = lax.axis_index("dp")
    along_x, along_z = me % 2, me // 2
    position = jnp.where(along_x == 0, along_z, 7 - along_z)
    where = [(position + o + 8) % 8 for o in (0, -1, 1, -2, 2, -3, 3, -4)]
    held = [jnp.where(p < 4, 2 * p, 2 * (7 - p) + 1) for p in where]
    slots = [sum(jnp.where(h == j, i, 0) for i, h in enumerate(held)) for j in range(8)]
    for k, fact in enumerate([s, core] + held + slots + [along_x, along_z]):
        meta[k] = fact.astype(jnp.int32)
    copies[0].wait()
    out[0:9] = weight[:, :, pl.ds(pl.multiple_of(s * LANES, LANES), LANES)]
    rows = lax.broadcasted_iota(jnp.int32, (LANES, LANES), 0)
    cols = lax.broadcasted_iota(jnp.int32, (LANES, LANES), 1)
    last = 4 * LANES
    for dy in range(3):
        total = None
        for dx in range(3):
            pick = (rows == PIECE * s + cols - PIECE * dx) & (cols >= PIECE * dx) & (cols < PIECE * dx + PIECE)
            part = jnp.dot(
                weight[3 * dy + dx, :, last : last + LANES],
                jnp.where(pick, 1.0, 0.0).astype(BF16),
                preferred_element_type=F32,
            )
            total = part if total is None else total + part
        out[9 + dy] = total.astype(BF16)
    copies[1].wait()
    for k in range(matrix.shape[1] // LANES):
        out[TAPS + k] = matrix[:, LANES * k : LANES * k + LANES]
    copies[2].wait()
    copies[3].wait()


def pack(conv_weight, attn_weights, latents, plan):
    taps, rows, channels = conv_weight.shape
    shapes = [(TAPS + channels // LANES, rows, LANES), (latents.shape[0] + plan.shape[0], channels)]
    return pl.pallas_call(
        pack_kernel,
        in_specs=[pl.BlockSpec(memory_space=pltpu.HBM)] * 4,
        out_specs=[whole(shape) for shape in shapes] + [smem()],
        out_shape=[jax.ShapeDtypeStruct(shape, BF16) for shape in shapes] + [jax.ShapeDtypeStruct((20,), jnp.int32)],
        scratch_shapes=[
            pltpu.VMEM(conv_weight.shape, BF16),
            pltpu.VMEM((rows, channels), BF16),
            pltpu.SemaphoreType.DMA((4,)),
        ],
        compiler_params=params(),
        cost_estimate=cost(1),
        name="pack",
    )(*(pltpu.with_memory_space_constraint(x, pltpu.HBM) for x in (conv_weight, attn_weights, latents, plan)))


def collect(parts, first):
    blocks, rows = parts[0].shape[0] - first, parts[0].shape[1]

    def kernel(*refs):
        for k, part in enumerate(refs[:-1]):
            for block in range(blocks):
                refs[-1][k, :, LANES * block : LANES * block + LANES] = part[first + block]

    return pl.pallas_call(
        kernel,
        in_specs=[whole(None)] * len(parts),
        out_specs=whole(None),
        out_shape=jax.ShapeDtypeStruct((len(parts), rows, LANES * blocks), BF16),
        compiler_params=params(),
        cost_estimate=cost(0),
        name="collect",
    )(*parts)


def stats_kernel(images, band, per_group, count, meta, x0, x1, x2, x3, gain, out):
    channels = gain.shape[0]
    shape = (channels, channels)
    row_group = jnp.floor((lax.broadcasted_iota(jnp.int32, shape, 0).astype(F32) + 0.5) * (1.0 / per_group))
    col_group = jnp.floor((lax.broadcasted_iota(jnp.int32, shape, 1).astype(F32) + 0.5) * (1.0 / per_group))
    same_group = jnp.where(row_group == col_group, 1.0, 0.0).astype(BF16)
    sums = []
    for b in range(images):
        first = jnp.zeros((1, channels), F32)
        second = jnp.zeros((1, channels), F32)
        for piece in (x0, x1, x2, x3):
            x = piece[band * b : band * b + band, :].astype(F32)
            first += jnp.sum(x, axis=0, keepdims=True)
            second += jnp.sum(x * x, axis=0, keepdims=True)
        sums += [first, second]
    sums = jnp.concatenate(sums, axis=0)
    high = sums.astype(BF16)
    rest = sums - high.astype(F32)
    middle = rest.astype(BF16)
    low = (rest - middle.astype(F32)).astype(BF16)
    grouped = sum(jnp.dot(part, same_group, preferred_element_type=F32) for part in (high, middle, low))
    for b in range(images):
        mean = grouped[2 * b : 2 * b + 1] / count
        variance = grouped[2 * b + 1 : 2 * b + 2] / count - mean * mean
        out[b : b + 1, :] = mean
        out[images + b : images + b + 1, :] = lax.rsqrt(variance + eps_norm) * gain[...].reshape(1, channels) * 0.5


def group_stats(meta, pieces, gain, images, band):
    channels = gain.shape[-1]
    per_group = channels // GROUPS
    return pl.pallas_call(
        lambda *refs: stats_kernel(images, band, per_group, float(4 * band * per_group), *refs),
        in_specs=[smem()] + [whole(None)] * 5,
        out_specs=whole(None),
        out_shape=jax.ShapeDtypeStruct((2 * images, channels), F32),
        compiler_params=params(),
        cost_estimate=cost(2),
        name="group_stats",
    )(meta, *pieces, gain)


def norm_kernel(image, images, band, columns, shard, meta, x0, x1, x2, x3, stats, hidden, own):
    s = meta[0]
    pieces = [x.at[image * band : image * band + band] for x in (x0, x1, x2, x3)]
    channels = stats.shape[1]
    mean = stats[image : image + 1, :]
    factor = stats[images + image : images + image + 1, :]
    hidden[:, 0:columns, :] = jnp.zeros((hidden.shape[0], columns, hidden.shape[2]), BF16)
    end = columns + 4 * band
    hidden[:, end : end + columns, :] = jnp.zeros((hidden.shape[0], columns, hidden.shape[2]), BF16)
    rows = 64
    column = lax.rem(lax.broadcasted_iota(jnp.int32, (rows, channels), 0), columns)
    at_start = column == 0
    at_end = column == columns - 1
    spare = jnp.zeros((rows, hidden.shape[2] - 3 * shard), BF16)
    krow = lax.broadcasted_iota(jnp.int32, (LANES, LANES), 0)
    kcol = lax.broadcasted_iota(jnp.int32, (LANES, LANES), 1)
    repeat = jnp.where(krow == PIECE * s + lax.rem(kcol, PIECE), 1.0, 0.0).astype(BF16)
    for r, piece in enumerate(pieces):
        base = (s ^ r) * band
        own[pl.ds(pl.multiple_of(base, band), band), 0:LANES] = piece[
            :, pl.ds(pl.multiple_of(s * LANES, LANES), LANES)
        ]
        own[pl.ds(pl.multiple_of(base, band), band), LANES : 2 * LANES] = jnp.dot(
            piece[:, 4 * LANES :], repeat, preferred_element_type=F32
        ).astype(BF16)
        for at in range(0, band, rows):
            t = (piece[at : at + rows, :].astype(F32) - mean) * factor
            h = t + t * jnp.tanh(t)
            left = jnp.where(at_start, 0.0, pltpu.roll(h, 1, 0)).astype(BF16)
            right = jnp.where(at_end, 0.0, pltpu.roll(h, rows - 1, 0)).astype(BF16)
            h = h.astype(BF16)
            target = pl.ds(pl.multiple_of(base + columns + at, columns), rows)
            for j in range(channels // shard):
                cut = slice(shard * j, shard * j + shard)
                hidden[meta[2 + channels // shard + j], target, :] = jnp.concatenate(
                    [left[:, cut], h[:, cut], right[:, cut], spare], axis=1
                )


def normalise(meta, pieces, stats, image, images, band, columns, shards):
    channels = stats.shape[-1]
    tokens = 4 * band
    hidden = (shards, tokens + 2 * columns, 2 * LANES)
    own = (tokens, 2 * LANES)
    return pl.pallas_call(
        lambda *refs: norm_kernel(image, images, band, columns, channels // shards, *refs),
        in_specs=[smem()] + [whole(None)] * 5,
        out_specs=[whole(hidden), whole(own)],
        out_shape=[jax.ShapeDtypeStruct(hidden, BF16), jax.ShapeDtypeStruct(own, BF16)],
        compiler_params=params(),
        cost_estimate=cost(3),
        name="normalise",
    )(meta, *pieces, stats)


def conv_kernel(band, columns, first, count, last, resume, meta, *refs):
    given = count + 1 if last else count
    weights = refs[:given]
    hidden = refs[given]
    refs = refs[given + 1 :]
    taps = refs[-1]
    s = meta[0]
    shard = weights[0].shape[1]
    wide = 2 * LANES
    lane = lanes_of((shard, LANES))

    def tap(i, k):
        if not last or i < count - 1:
            return weights[i][k]
        half = weights[-2].shape[0]
        return weights[-2][k] if k < half else weights[-1][k - half]

    for i in range(count):
        for dy in range(3):
            for dx in range(3):
                at = slice(wide * i + shard * dx, wide * i + shard * dx + shard)
                taps[dy, at, 0:LANES] = tap(i, 3 * dy + dx)
                taps[dy, at, LANES:wide] = jnp.where(
                    (lane >= PIECE * dx) & (lane < PIECE * dx + PIECE), tap(i, 9 + dy), jnp.zeros((), BF16)
                )
            taps[dy, wide * i + 3 * shard : wide * i + wide, :] = jnp.zeros((wide - 3 * shard, wide), BF16)

    group = band // 4
    lane = lanes_of((group, LANES))
    for r in range(4):
        base = (s ^ r) * band
        here = pl.ds(pl.multiple_of(base, band), band)
        total = refs[0][here, :] if resume else None
        for dy in range(3):
            rows = pl.ds(pl.multiple_of(base + columns * dy, columns), band)
            window = jnp.concatenate([hidden[first + k, rows, :] for k in range(count)], axis=1)
            part = jnp.dot(window, taps[dy], preferred_element_type=F32)
            total = part if total is None else total + part
        if not last:
            refs[0][here, :] = total
            continue
        own, out = refs[resume], refs[resume + 1 + r]
        tail = total[:, LANES:]
        tail = tail + pltpu.roll(tail, 2 * PIECE, 1)
        tail = tail + pltpu.roll(tail, PIECE, 1)
        cells = own[here, :].astype(F32)
        out[0:band, :] = (cells[:, :LANES] + total[:, :LANES]).astype(BF16)
        tail = cells[:, LANES:] + tail
        packed = tail[0:group]
        for g in range(1, 4):
            packed = jnp.where(lane >= PIECE * g, tail[group * g : group * g + group], packed)
        out[band : band + group, :] = packed.astype(BF16)


def convolve(meta, hidden, weights, band, columns, partial=None, own=None):
    tokens = hidden.shape[1] - 2 * columns
    last = own is not None
    resume = int(partial is not None)
    count = len(weights) - 1 if last else len(weights)
    first = hidden.shape[0] - count if last else 0
    operands = list(weights) + [hidden]
    if last:
        operands += [partial, own] if resume else [own]
        shapes = [jax.ShapeDtypeStruct((band + band // 4, LANES), BF16)] * 4
    else:
        shapes = [jax.ShapeDtypeStruct((tokens, 2 * LANES), F32)]
    return pl.pallas_call(
        lambda *refs: conv_kernel(band, columns, first, count, last, resume, *refs),
        in_specs=[smem()] + [whole(x.shape) for x in operands],
        out_specs=[whole(shape.shape) for shape in shapes],
        out_shape=shapes,
        scratch_shapes=[pltpu.VMEM((3, 2 * LANES * count, 2 * LANES), BF16)],
        compiler_params=params(),
        cost_estimate=cost(3),
        name="convolve_last" if last else "convolve_first",
    )(meta, *operands)


def project_kernel(shards, images, count, meta, p0, p1, p2, p3, *refs):
    ours, batches = refs[: shards + 1], refs[shards + 1 : -3]
    out, both, plan = refs[-3:]
    s, high = meta[0], meta[0] // 2
    shard, channels = ours[0].shape[1], out.shape[1]
    theirs = [batch.at[k] for batch in batches for k in range(batch.shape[0])]
    for i in range(shards):
        at = pl.ds(pl.multiple_of(shard * meta[2 + i], 16), shard)
        source, first = (ours[i], TAPS) if i < shards - 1 else (ours[-1], TAPS - ours[-2].shape[0])
        for block in range(channels // LANES):
            both[high, at, LANES * block : LANES * block + LANES] = source[first + block]
        both[1 - high, at, :] = theirs[i][...]
    for r, piece in enumerate((p0, p1, p2, p3)):
        rows = count // images
        start = piece.shape[0] - count
        for b in range(images):
            plan[pl.ds(pl.multiple_of(rows * (4 * b + (s ^ r)), 16), rows), :] = piece[
                start + rows * b : start + rows * b + rows, :
            ]
    out[0:channels, :] = both[0]
    out[channels:, :] = jnp.dot(plan[...], both[1], preferred_element_type=F32).astype(BF16)


def project(meta, pieces, ours, theirs, images, rows):
    channels = theirs[0].shape[2]
    operands = list(pieces) + list(ours) + list(theirs)
    return pl.pallas_call(
        lambda *refs: project_kernel(len(ours) - 1, images, rows, *refs),
        in_specs=[smem()] + [whole(x.shape) for x in operands],
        out_specs=whole((channels + 4 * rows, channels)),
        out_shape=jax.ShapeDtypeStruct((channels + 4 * rows, channels), BF16),
        scratch_shapes=[pltpu.VMEM((2, channels, channels), BF16), pltpu.VMEM((4 * rows, channels), BF16)],
        compiler_params=params(),
        cost_estimate=cost(1),
        name="project_plan",
    )(meta, *operands)


def prepare_kernel(images, meta, mine, other, cot, weight_q, weight_o, key, key_t, value_t, dprob, cot_t, kv):
    core = meta[1]
    channels = cot.shape[1]
    plan_rows = (mine.shape[0] - channels) // images

    @pl.when(core == 0)
    def _():
        weight_q[...] = mine[0:channels]
        weight_o[...] = other[0:channels]
        kv[0] = mine[channels:]
        kv[1] = other[channels:]

    @pl.when(core != 0)
    def _():
        weight_q[...] = other[0:channels]
        weight_o[...] = mine[0:channels]
        kv[0] = other[channels:]
        kv[1] = mine[channels:]

    tokens = cot.shape[0] // images
    lane = lanes_of((plan_rows, LANES))
    for b in range(images):
        cot_t[b] = cot[tokens * b : tokens * b + tokens, :].T
        back = lax.dot_general(
            cot[tokens * b : tokens * b + tokens, :], weight_o[...], NT, preferred_element_type=F32
        ).astype(BF16)
        for p in range(channels // LANES):
            cut = slice(LANES * p, LANES * p + LANES)
            both = []
            for which in range(2):
                part = kv[which, plan_rows * b : plan_rows * b + plan_rows, cut].astype(F32)
                both.append(
                    jnp.concatenate([jnp.where(lane < HEAD, part, 0.0), jnp.where(lane >= HEAD, part, 0.0)], axis=0)
                )
            key[b, p] = both[0].astype(BF16)
            key_t[b, p] = both[0].T.astype(BF16)
            value_t[b, p] = both[1].T.astype(BF16)
            dprob[b, p] = lax.dot_general(both[1].astype(BF16), back[:, cut], NT, preferred_element_type=F32)


def prepare(meta, mine, other, cot, images):
    channels = cot.shape[1]
    pairs = channels // LANES
    tokens = cot.shape[0] // images
    square = (images, pairs, LANES, LANES)
    shapes = [
        ((channels, channels), BF16),
        ((channels, channels), BF16),
        (square, BF16),
        (square, BF16),
        (square, BF16),
        ((images, pairs, LANES, tokens), F32),
        ((images, channels, tokens), BF16),
    ]
    return pl.pallas_call(
        lambda *refs: prepare_kernel(images, *refs),
        in_specs=[smem(), whole(mine.shape), whole(other.shape), whole(cot.shape)],
        out_specs=[whole(shape) for shape, _ in shapes],
        out_shape=[jax.ShapeDtypeStruct(shape, kind) for shape, kind in shapes],
        scratch_shapes=[pltpu.VMEM((2, mine.shape[0] - channels, channels), BF16)],
        compiler_params=params(),
        cost_estimate=cost(2),
        name="prepare_attention",
    )(meta, mine, other, cot)


def attend_kernel(image, meta, c0, c1, c2, c3, weight_q, weight_o, key, key_t, value_t, dprob, cot_t, result, kept, sent, mixed, att_t, dq_t):
    s = meta[0]
    core = meta[1]
    tokens, channels = result.shape
    group = tokens // 4
    scale = 1.0 / math.sqrt(HEAD)
    lane = lanes_of((group, LANES))
    krow = lax.broadcasted_iota(jnp.int32, (LANES, LANES), 0)
    kcol = lax.broadcasted_iota(jnp.int32, (LANES, LANES), 1)
    same = lax.rem(krow, PIECE) == lax.rem(kcol, PIECE)
    tail = jnp.zeros((tokens, LANES), F32)
    for r, chunk in enumerate((c0, c1, c2, c3)):
        source = s ^ r
        mixed[:, pl.ds(pl.multiple_of(source * LANES, LANES), LANES)] = chunk[0:tokens, :]
        packed = chunk[tokens : tokens + group, :]
        spread = jnp.concatenate(
            [
                jnp.where((lane >= PIECE * g) & (lane < PIECE * g + PIECE), packed, jnp.zeros((), BF16))
                for g in range(4)
            ],
            axis=0,
        )
        place = same & (kcol >= PIECE * source) & (kcol < PIECE * source + PIECE)
        tail += jnp.dot(spread, jnp.where(place, 1.0, 0.0).astype(BF16), preferred_element_type=F32)
    mixed[:, 4 * LANES :] = tail.astype(BF16)
    here = mixed[...]
    queries = jnp.dot(here, weight_q[...], preferred_element_type=F32).astype(BF16)
    for p in range(channels // LANES):
        cut = slice(LANES * p, LANES * p + LANES)
        scores = lax.dot_general(key[image, p], queries[:, cut], NT, preferred_element_type=F32) * scale
        scores = scores.reshape(2, HEAD, tokens)
        expo = jnp.exp(scores - jnp.max(scores, axis=1, keepdims=True))
        probs = expo * (1.0 / jnp.sum(expo, axis=1, keepdims=True))
        att_t[cut, :] = jnp.dot(
            value_t[image, p], probs.reshape(LANES, tokens).astype(BF16), preferred_element_type=F32
        ).astype(BF16)
        down = dprob[image, p].reshape(2, HEAD, tokens)
        dscore = probs * (down - jnp.sum(probs * down, axis=1, keepdims=True)) * scale
        dq_t[cut, :] = jnp.dot(
            key_t[image, p], dscore.reshape(LANES, tokens).astype(BF16), preferred_element_type=F32
        ).astype(BF16)

    @pl.when(core == 0)
    def _():
        kept[0] = here.T
        kept[1] = dq_t[...]
        sent[0] = att_t[...]
        sent[1] = cot_t[image]

    @pl.when(core != 0)
    def _():
        sent[0] = here.T
        sent[1] = dq_t[...]
        kept[0] = att_t[...]
        kept[1] = cot_t[image]

    result[...] = (here.astype(F32) + jnp.dot(att_t[...].T, weight_o[...], preferred_element_type=F32)).astype(BF16)


def attend(meta, chunks, prepared, image, tokens):
    channels = prepared[0].shape[0]
    operands = list(chunks) + list(prepared)
    both = jax.ShapeDtypeStruct((2, channels, tokens), BF16)
    return pl.pallas_call(
        lambda *refs: attend_kernel(image, *refs),
        in_specs=[smem()] + [whole(x.shape) for x in operands],
        out_specs=[whole(None)] * 3,
        out_shape=[jax.ShapeDtypeStruct((tokens, channels), BF16), both, both],
        scratch_shapes=[pltpu.VMEM((tokens, channels), BF16)] + [pltpu.VMEM((channels, tokens), BF16)] * 2,
        compiler_params=params(),
        cost_estimate=cost(3),
        name="attend",
    )(meta, *operands)


def gradient(parts):
    channels = parts[0].shape[1]

    def kernel(*refs):
        left, right = (jnp.concatenate([part[k] for part in refs[:-1]], axis=1) for k in range(2))
        refs[-1][...] = lax.dot_general(left, right, NT, preferred_element_type=F32)

    return pl.pallas_call(
        kernel,
        in_specs=[whole(x.shape) for x in parts],
        out_specs=whole(None),
        out_shape=jax.ShapeDtypeStruct((channels, channels), F32),
        compiler_params=params(),
        cost_estimate=cost(1),
        name="gradient_first",
    )(*parts)


def quarter_kernel(factor, meta, partial, part, mine, *refs):
    sends, total = refs[:-1], refs[-1]
    total[...] = (partial[...] + lax.dot_general(part[0], part[1], NT, preferred_element_type=F32)) * factor
    along_x, along_y = meta[18], meta[0] // 2
    rows = mine.shape[0] // 4
    for r, out in enumerate((mine,) + sends):
        parts = []
        for z in range(4):
            at = pl.multiple_of(rows * (2 * (2 * z + (along_x ^ (r % 2))) + (along_y ^ (r // 2))), 8)
            parts.append(total[pl.ds(at, rows), :])
        out[...] = jnp.concatenate(parts, axis=0).astype(out.dtype)


def quarters(meta, partial, part, factor):
    rows, channels = partial.shape
    shapes = [jax.ShapeDtypeStruct((rows // 4, channels), kind) for kind in (F32, BF16, BF16, BF16)]
    return pl.pallas_call(
        lambda *refs: quarter_kernel(factor, *refs),
        in_specs=[smem(), whole(partial.shape), whole(part.shape)],
        out_specs=[whole(x.shape) for x in shapes],
        out_shape=shapes,
        scratch_shapes=[pltpu.VMEM((rows, channels), F32)],
        compiler_params=params(),
        cost_estimate=cost(1),
        name="gradient_last",
    )(meta, partial, part)


def line_sum(parts):
    def kernel(a, b, c, d, out):
        out[...] = a[...] + b[...].astype(F32) + c[...].astype(F32) + d[...].astype(F32)

    return pl.pallas_call(
        kernel,
        in_specs=[whole(None)] * 4,
        out_specs=whole(None),
        out_shape=jax.ShapeDtypeStruct(parts[0].shape, F32),
        compiler_params=params(),
        cost_estimate=cost(0),
        name="sum_line",
    )(*parts)


def finish_kernel(meta, mine, beside, across, corner, out):
    core, high = meta[1], meta[0] // 2
    rows = mine.shape[0]

    def ordered(a, b):
        first = jnp.where(high == 0, a[...], b[...])
        second = jnp.where(high == 0, b[...], a[...])
        return jnp.concatenate([first, second], axis=0)

    own, other = ordered(mine, across), ordered(beside, corner)
    out[:, 0, :] = jnp.where(core == 0, own, other)
    out[:, 1, :] = jnp.where(core == 0, other, own)


def finish(meta, parts):
    rows, channels = parts[0].shape
    return pl.pallas_call(
        finish_kernel,
        in_specs=[smem()] + [whole(x.shape) for x in parts],
        out_specs=whole(None),
        out_shape=jax.ShapeDtypeStruct((2 * rows, 2, channels), F32),
        compiler_params=params(),
        cost_estimate=cost(1),
        name="finish",
    )(meta, *parts)


def slab_kernel(meta, a, b, c, d, mine, *sends):
    along_z = meta[19]
    rows = mine.shape[0]
    total = a[...] + b[...].astype(F32) + c[...].astype(F32) + d[...].astype(F32)
    for z in range(4):
        part = total[rows * z : rows * z + rows]
        for r, out in enumerate((mine,) + sends):

            @pl.when((along_z ^ r) == z)
            def _(out=out, part=part):
                out[...] = part.astype(out.dtype)


def slabs(meta, parts, kinds):
    rows, channels = parts[0].shape
    shapes = [jax.ShapeDtypeStruct((rows // 4, channels), t) for t in kinds]
    return pl.pallas_call(
        slab_kernel,
        in_specs=[smem()] + [whole(x.shape) for x in parts],
        out_specs=[whole(x.shape) for x in shapes],
        out_shape=shapes,
        compiler_params=params(),
        cost_estimate=cost(1),
        name="sum_plane",
    )(meta, *parts)


def flip(x, axis, bits):
    count = lax.axis_size(axis)
    return lax.ppermute(x, axis, [(i, i ^ bits) for i in range(count)])


def flip_plane(x, bits):
    count = lax.axis_size("dp") * lax.axis_size("spatial")
    return lax.ppermute(x, ("dp", "spatial"), [(i, i ^ bits) for i in range(count)])


def ring_place(p):
    return 2 * p if p < 4 else 2 * (7 - p) + 1


def step_ring(x, backward):
    shards = lax.axis_size("dp")
    pairs = [(ring_place(p), ring_place((p + 1) % shards)) for p in range(shards)]
    return lax.ppermute(x, "dp", [(b, a) for a, b in pairs] if backward else pairs)


def after(values, *others):
    return lax.optimization_barrier((tuple(values), others))[0]


def body(latents, plan, conv_weight, gn_gain, attn_weights, cotangent):
    images, band_rows, columns, channels = latents.shape
    shards = lax.axis_size("dp")
    band = band_rows * columns
    packed, mine, meta = pack(
        conv_weight, attn_weights, latents.reshape(images * band, channels), plan.reshape(-1, channels)
    )
    ring = [packed, *after((step_ring(packed, False), step_ring(packed, True)))]
    across = flip(mine, "spatial", 2)
    ring += [step_ring(ring[1], False), step_ring(ring[2], True)]
    *ring[3:5], across = after(ring[3:5] + [across])
    ring += [step_ring(ring[3], False), step_ring(ring[4], True)]
    pieces = [mine, flip(mine, "spatial", 1), across, flip(across, "spatial", 1)]
    given = [flip(collect(ring[:5], TAPS), "spatial", 2)]
    stats = group_stats(meta, pieces, gn_gain, images, band)
    normed = [normalise(meta, pieces, stats, b, images, band, columns, shards) for b in range(images)]
    half = packed.shape[0] // 2 + 1
    a, b = after(ring[5:7], *(x[1] for x in normed))
    ring += [step_ring(a[:half], False), step_ring(b[half:], True)]
    given.append(flip(collect(ring[5:7], TAPS), "spatial", 2))
    partial = convolve(meta, normed[0][0], ring[:6], band, columns)[0]
    ring[7], ring[8] = after(ring[7:], partial)
    given.append(flip(collect(ring[8:], TAPS - half), "spatial", 2))

    chunks = []
    for b in range(images):
        if b:
            outs = convolve(meta, normed[b][0], ring, band, columns, None, normed[b][1])
        else:
            outs = convolve(meta, normed[b][0], ring[6:], band, columns, partial, normed[b][1])
            (given[2],) = after([given[2]], outs[0])
        chunks.append([outs[0]] + [flip(outs[r], "spatial", r) for r in (1, 2, 3)])

    projected = project(meta, pieces, ring, given, images, plan.shape[0] * plan.shape[1])
    cot = cotangent.reshape(images * band, channels)
    prepared = prepare(meta, projected, flip(projected, "spatial", 1), cot, images)
    tokens = images * shards * band * lax.axis_size("spatial")
    results = []
    kept = []
    given = []
    for b in range(images):
        result, keep, send = attend(meta, chunks[b], prepared, b, band)
        results.append(result.reshape(1, band_rows, columns, channels))
        kept.append(keep)
        given.append(flip(send, "spatial", 1))
    partial = gradient(kept + given[:-1])
    mine, *sends = quarters(meta, partial, given[-1], 1.0 / math.sqrt(tokens))
    moved = [flip_plane(sends[r - 1], 4 * (r % 2) + 2 * (r // 2)) for r in (1, 2, 3)]
    mine, *sends = slabs(meta, [mine] + moved, (F32, F32, F32, BF16))
    total = line_sum([mine] + [flip(sends[r - 1], "dp", 2 * r) for r in (1, 2, 3)])
    grads = finish(meta, [total] + [flip(total, "spatial", r) for r in (1, 2, 3)])
    return jnp.concatenate(results), grads


def solution(mesh):
    fits = mesh.shape["dp"] == 8 and mesh.shape["spatial"] == 4
    return jax.shard_map(
        body if fits else plain_body,
        mesh=mesh,
        in_specs=(
            P("dp", "spatial", None, None),
            P("dp", "spatial", None),
            P(None, "dp", None),
            P(),
            P(None, "dp", None),
            P("dp", "spatial", None, None),
        ),
        out_specs=(P("dp", "spatial", None, None), P("dp", None, None)),
        check_vma=False,
    )
```

```python
import math

import jax
import jax.numpy as jnp
from jax import lax
from jax.experimental import pallas as pl
from jax.experimental.pallas import tpu as pltpu
from jax.sharding import PartitionSpec as P

GROUPS = 32
HEAD = 64


eps_norm = 1e-05


def with_halo(cells, sides, width):
    for axis, dim in sides:
        count = lax.axis_size(axis)
        ends = count - 1
        head = lax.slice_in_dim(cells, 0, width, axis=dim)
        tail = lax.slice_in_dim(cells, cells.shape[dim] - width, cells.shape[dim], axis=dim)
        cells = jnp.concatenate(
            [
                lax.ppermute(tail, axis, [(i, (i + 1) % count) for i in range(ends)]),
                cells,
                lax.ppermute(head, axis, [((i + 1) % count, i) for i in range(ends)]),
            ],
            axis=dim,
        )
    return cells


def plain_body(latents, plan, conv_weight, gn_gain, attn_weights, cotangent):
    images, band_rows, columns, channels = latents.shape
    heads = channels // HEAD
    per_group = channels // GROUPS
    tokens_here = images * band_rows * columns
    scale = 1.0 / math.sqrt(HEAD)
    flat_input = latents.astype(jnp.float32).reshape(images, band_rows * columns, GROUPS, per_group)
    first_sums = jnp.sum(flat_input, axis=(1, 3))
    second_sums = jnp.sum(flat_input * flat_input, axis=(1, 3))
    first_sums, second_sums = lax.psum((first_sums, second_sums), "spatial")
    counted = float(band_rows * lax.axis_size("spatial") * columns * per_group)
    means = first_sums / counted
    variance = second_sums / counted - means * means
    inverse = lax.rsqrt(variance + eps_norm)
    normed = (flat_input - means[:, None, :, None]) * inverse[:, None, :, None]
    normed = normed.reshape(images, band_rows, columns, channels) * gn_gain
    hidden = jax.nn.silu(normed).astype(jnp.bfloat16)
    padded = with_halo(hidden, (("spatial", 1),), 1)
    padded = jnp.pad(padded, ((0, 0), (0, 0), (1, 1), (0, 0)))
    tapped = jnp.stack(
        [
            padded[:, offset_y : offset_y + band_rows, offset_x : offset_x + columns].reshape(
                tokens_here, channels
            )
            for offset_y in range(3)
            for offset_x in range(3)
        ],
        1,
    )
    conv_sum = jnp.einsum(
        "ntc,tcd->nd",
        tapped,
        lax.all_gather(conv_weight, "dp", axis=1, tiled=True),
        preferred_element_type=jnp.float32,
    )
    mixed = (latents.reshape(tokens_here, channels).astype(jnp.float32) + conv_sum).astype(
        jnp.bfloat16
    )
    weights = lax.all_gather(attn_weights, "dp", axis=1, tiled=True)
    weight_q = weights[0]
    weight_k = weights[1]
    weight_v = weights[2]
    weight_o = weights[3]
    queries = jnp.dot(mixed, weight_q, preferred_element_type=jnp.float32).astype(jnp.bfloat16)
    plan_all = lax.all_gather(plan, "spatial", axis=1, tiled=True)
    plan_flat = plan_all.reshape(-1, channels)
    keys_all = jnp.dot(plan_flat, weight_k, preferred_element_type=jnp.float32).astype(jnp.bfloat16)
    values_all = jnp.dot(plan_flat, weight_v, preferred_element_type=jnp.float32).astype(
        jnp.bfloat16
    )
    keys_all = keys_all.reshape(images, -1, channels)
    values_all = values_all.reshape(images, -1, channels)
    plan_tokens = keys_all.shape[1]
    query_heads = queries.reshape(images, band_rows * columns, heads, HEAD)
    key_heads = keys_all.reshape(images, plan_tokens, heads, HEAD)
    value_heads = values_all.reshape(images, plan_tokens, heads, HEAD)
    scores = (
        jnp.einsum("bnhe,bmhe->bhnm", query_heads, key_heads, preferred_element_type=jnp.float32)
        * scale
    )
    maxima = jnp.max(scores, axis=-1, keepdims=True)
    expo = jnp.exp(scores - maxima)
    probs = expo / jnp.sum(expo, axis=-1, keepdims=True)
    probs_b = probs.astype(jnp.bfloat16)
    attended = jnp.einsum(
        "bhnm,bmhe->bnhe", probs_b, value_heads, preferred_element_type=jnp.float32
    )
    attended = attended.reshape(tokens_here, channels).astype(jnp.bfloat16)
    result = mixed.astype(jnp.float32) + jnp.dot(
        attended, weight_o, preferred_element_type=jnp.float32
    )
    block_out = result.astype(jnp.bfloat16).reshape(images, band_rows, columns, channels)
    grad_flat = cotangent.reshape(tokens_here, channels)
    grad_att = lax.dot_general(
        grad_flat, weight_o, (((1,), (1,)), ((), ())), preferred_element_type=jnp.float32
    )
    grad_att = grad_att.astype(jnp.bfloat16).reshape(images, band_rows * columns, heads, HEAD)
    dprob = jnp.einsum("bnhe,bmhe->bhnm", grad_att, value_heads, preferred_element_type=jnp.float32)
    dscore = (probs * (dprob - jnp.sum(probs * dprob, axis=-1, keepdims=True)) * scale).astype(
        jnp.bfloat16
    )
    dquery = jnp.einsum("bhnm,bmhe->bnhe", dscore, key_heads, preferred_element_type=jnp.float32)
    dquery = dquery.reshape(tokens_here, channels).astype(jnp.bfloat16)
    total_tokens = images * lax.axis_size("dp") * band_rows * lax.axis_size("spatial") * columns
    factor = 1.0 / math.sqrt(total_tokens)
    contract = (((0,), (0,)), ((), ()))
    grad_query = lax.dot_general(mixed, dquery, contract, preferred_element_type=jnp.float32)
    grad_output = lax.dot_general(attended, grad_flat, contract, preferred_element_type=jnp.float32)
    own_rows = lax.psum_scatter(
        jnp.stack([grad_query, grad_output], 1) * factor, "dp", scatter_dimension=0, tiled=True
    )
    weight_grads = lax.psum(own_rows, "spatial")
    return (block_out, weight_grads)


F32 = jnp.float32
BF16 = jnp.bfloat16
LANES = 128
PIECE = 32
VMEM_LIMIT = 24 * 1024 * 1024
NT = (((1,), (1,)), ((), ()))


def cost(microseconds):
    return pl.CostEstimate(flops=0, bytes_accessed=microseconds * 3690000, transcendentals=0)


def params():
    return pltpu.CompilerParams(vmem_limit_bytes=VMEM_LIMIT)


def whole(shape):
    return pl.BlockSpec(memory_space=pltpu.VMEM)


def smem():
    return pl.BlockSpec(memory_space=pltpu.SMEM)


def lanes_of(shape):
    return lax.broadcasted_iota(jnp.int32, shape, len(shape) - 1)


def pack_kernel(conv_hbm, attn_hbm, latents_hbm, plan_hbm, out, more, rows_out, meta, weight, matrix, sems):
    s = lax.axis_index("spatial")
    core, high = s % 2, s // 2
    split = latents_hbm.shape[0]
    copies = [
        pltpu.make_async_copy(conv_hbm, weight, sems.at[0]),
        pltpu.make_async_copy(attn_hbm.at[jnp.where(high == 0, 3 * core, 1 + core)], matrix, sems.at[1]),
        pltpu.make_async_copy(latents_hbm, rows_out.at[pl.ds(0, split)], sems.at[2]),
        pltpu.make_async_copy(plan_hbm, rows_out.at[pl.ds(split, plan_hbm.shape[0])], sems.at[3]),
    ]
    for copy in copies:
        copy.start()
    me = lax.axis_index("dp")
    along_x, along_z = me % 2, me // 2
    position = jnp.where(along_x == 0, along_z, 7 - along_z)
    where = [(position + o + 8) % 8 for o in (0, -1, 1, -2, 2, -3, 3, -4)]
    held = [jnp.where(p < 4, 2 * p, 2 * (7 - p) + 1) for p in where]
    slots = [sum(jnp.where(h == j, i, 0) for i, h in enumerate(held)) for j in range(8)]
    for k, fact in enumerate([s, core] + held + slots + [along_x, along_z]):
        meta[k] = fact.astype(jnp.int32)
    copies[0].wait()
    out[0:9] = weight[:, :, pl.ds(pl.multiple_of(s * LANES, LANES), LANES)]
    rows = lax.broadcasted_iota(jnp.int32, (LANES, LANES), 0)
    cols = lax.broadcasted_iota(jnp.int32, (LANES, LANES), 1)
    last = 4 * LANES
    for dy in range(3):
        total = None
        for dx in range(3):
            pick = (rows == PIECE * s + cols - PIECE * dx) & (cols >= PIECE * dx) & (cols < PIECE * dx + PIECE)
            part = jnp.dot(
                weight[3 * dy + dx, :, last : last + LANES],
                jnp.where(pick, 1.0, 0.0).astype(BF16),
                preferred_element_type=F32,
            )
            total = part if total is None else total + part
        more[dy] = total.astype(BF16)
    copies[1].wait()
    for k in range(matrix.shape[1] // LANES):
        more[3 + k] = matrix[:, LANES * k : LANES * k + LANES]
    copies[2].wait()
    copies[3].wait()


def pack(conv_weight, attn_weights, latents, plan):
    taps, rows, channels = conv_weight.shape
    shapes = [
        (taps, rows, LANES),
        (3 + channels // LANES, rows, LANES),
        (latents.shape[0] + plan.shape[0], channels),
    ]
    return pl.pallas_call(
        pack_kernel,
        in_specs=[pl.BlockSpec(memory_space=pltpu.HBM)] * 4,
        out_specs=[whole(shape) for shape in shapes] + [smem()],
        out_shape=[jax.ShapeDtypeStruct(shape, BF16) for shape in shapes] + [jax.ShapeDtypeStruct((20,), jnp.int32)],
        scratch_shapes=[
            pltpu.VMEM(conv_weight.shape, BF16),
            pltpu.VMEM((rows, channels), BF16),
            pltpu.SemaphoreType.DMA((4,)),
        ],
        compiler_params=params(),
        cost_estimate=cost(1),
        name="pack",
    )(*(pltpu.with_memory_space_constraint(x, pltpu.HBM) for x in (conv_weight, attn_weights, latents, plan)))


def collect(parts, first):
    blocks, rows = parts[0].shape[0] - first, parts[0].shape[1]

    def kernel(*refs):
        for k, part in enumerate(refs[:-1]):
            for block in range(blocks):
                refs[-1][k, :, LANES * block : LANES * block + LANES] = part[first + block]

    return pl.pallas_call(
        kernel,
        in_specs=[whole(None)] * len(parts),
        out_specs=whole(None),
        out_shape=jax.ShapeDtypeStruct((len(parts), rows, LANES * blocks), BF16),
        compiler_params=params(),
        cost_estimate=cost(0),
        name="collect",
    )(*parts)


def stats_kernel(images, band, per_group, count, meta, x0, x1, x2, x3, gain, out):
    channels = gain.shape[0]
    shape = (channels, channels)
    row_group = jnp.floor((lax.broadcasted_iota(jnp.int32, shape, 0).astype(F32) + 0.5) * (1.0 / per_group))
    col_group = jnp.floor((lax.broadcasted_iota(jnp.int32, shape, 1).astype(F32) + 0.5) * (1.0 / per_group))
    same_group = jnp.where(row_group == col_group, 1.0, 0.0).astype(BF16)
    sums = []
    for b in range(images):
        first = jnp.zeros((1, channels), F32)
        second = jnp.zeros((1, channels), F32)
        for piece in (x0, x1, x2, x3):
            x = piece[band * b : band * b + band, :].astype(F32)
            first += jnp.sum(x, axis=0, keepdims=True)
            second += jnp.sum(x * x, axis=0, keepdims=True)
        sums += [first, second]
    sums = jnp.concatenate(sums, axis=0)
    high = sums.astype(BF16)
    rest = sums - high.astype(F32)
    middle = rest.astype(BF16)
    low = (rest - middle.astype(F32)).astype(BF16)
    grouped = sum(jnp.dot(part, same_group, preferred_element_type=F32) for part in (high, middle, low))
    for b in range(images):
        mean = grouped[2 * b : 2 * b + 1] / count
        variance = grouped[2 * b + 1 : 2 * b + 2] / count - mean * mean
        out[b : b + 1, :] = mean
        out[images + b : images + b + 1, :] = lax.rsqrt(variance + eps_norm) * gain[...].reshape(1, channels) * 0.5


def group_stats(meta, pieces, gain, images, band):
    channels = gain.shape[-1]
    per_group = channels // GROUPS
    return pl.pallas_call(
        lambda *refs: stats_kernel(images, band, per_group, float(4 * band * per_group), *refs),
        in_specs=[smem()] + [whole(None)] * 5,
        out_specs=whole(None),
        out_shape=jax.ShapeDtypeStruct((2 * images, channels), F32),
        compiler_params=params(),
        cost_estimate=cost(0),
        name="group_stats",
    )(meta, *pieces, gain)


def norm_kernel(image, images, band, columns, meta, x0, x1, x2, x3, stats, hidden, own):
    s = meta[0]
    pieces = [x.at[image * band : image * band + band] for x in (x0, x1, x2, x3)]
    channels = stats.shape[1]
    mean = stats[image : image + 1, :]
    factor = stats[images + image : images + image + 1, :]
    rows = 64
    hidden[0:columns, :] = jnp.zeros((columns, channels), BF16)
    hidden[columns + 4 * band :, :] = jnp.zeros((columns, channels), BF16)
    krow = lax.broadcasted_iota(jnp.int32, (LANES, LANES), 0)
    kcol = lax.broadcasted_iota(jnp.int32, (LANES, LANES), 1)
    repeat = jnp.where(krow == PIECE * s + lax.rem(kcol, PIECE), 1.0, 0.0).astype(BF16)
    for r, piece in enumerate(pieces):
        base = (s ^ r) * band
        own[pl.ds(pl.multiple_of(base, band), band), 0:LANES] = piece[
            :, pl.ds(pl.multiple_of(s * LANES, LANES), LANES)
        ]
        own[pl.ds(pl.multiple_of(base, band), band), LANES : 2 * LANES] = jnp.dot(
            piece[:, 4 * LANES :], repeat, preferred_element_type=F32
        ).astype(BF16)
        for at in range(0, band, rows):
            t = (piece[at : at + rows, :].astype(F32) - mean) * factor
            hidden[pl.ds(pl.multiple_of(base + columns + at, columns), rows), :] = (t + t * jnp.tanh(t)).astype(BF16)


def normalise(meta, pieces, stats, image, images, band, columns):
    channels = stats.shape[-1]
    tokens = 4 * band
    hidden = (tokens + 2 * columns, channels)
    own = (tokens, 2 * LANES)
    return pl.pallas_call(
        lambda *refs: norm_kernel(image, images, band, columns, *refs),
        in_specs=[smem()] + [whole(None)] * 5,
        out_specs=[whole(hidden), whole(own)],
        out_shape=[jax.ShapeDtypeStruct(hidden, BF16), jax.ShapeDtypeStruct(own, BF16)],
        compiler_params=params(),
        cost_estimate=cost(0),
        name="normalise",
    )(meta, *pieces, stats)


def fill_taps(taps, at, shard, tap):
    lane = lanes_of((shard, LANES))
    wide = 2 * LANES
    rows = taps.shape[0] // 3
    for dy in range(3):
        here = pl.ds(pl.multiple_of(rows * dy + at, 16), shard)
        for dx in range(3):
            taps[here, wide * dx : wide * dx + LANES] = tap(3 * dy + dx)
            taps[here, wide * dx + LANES : wide * dx + wide] = jnp.where(
                (lane >= PIECE * dx) & (lane < PIECE * dx + PIECE), tap(9 + dy), jnp.zeros((), BF16)
            )


def first_taps(meta, weights, more, channels):
    shard, count = weights[0].shape[1], len(weights)

    def kernel(meta, *refs):
        for i in range(count):
            fill_taps(
                refs[-1], shard * meta[2 + i], shard, lambda k, i=i: refs[i][k] if k < 9 else refs[count + i][k - 9]
            )

    return pl.pallas_call(
        kernel,
        in_specs=[smem()] + [whole(None)] * (2 * count),
        out_specs=whole(None),
        out_shape=jax.ShapeDtypeStruct((3 * channels, 6 * LANES), BF16),
        compiler_params=params(),
        cost_estimate=cost(6),
        name="first_taps",
    )(meta, *weights, *more)


def last_taps(meta, taps, halves):
    shard = halves[0].shape[1]

    def kernel(meta, before, one, two, after):
        split = one.shape[0]
        after[...] = before[...]
        fill_taps(after, shard * meta[9], shard, lambda k: one[k] if k < split else two[k - split])

    return pl.pallas_call(
        kernel,
        in_specs=[smem()] + [whole(None)] * 3,
        out_specs=whole(None),
        out_shape=jax.ShapeDtypeStruct(taps.shape, BF16),
        compiler_params=params(),
        cost_estimate=cost(0),
        name="last_taps",
    )(meta, taps, *halves)


def conv_kernel(band, columns, meta, taps, hidden, own, *refs):
    outs = refs
    s = meta[0]
    channels = hidden.shape[1]
    wide = 2 * LANES
    column = lax.rem(lax.broadcasted_iota(jnp.int32, (band, wide), 0), columns)
    group = band // 4
    lane = lanes_of((group, LANES))
    for r, out in enumerate(outs):
        base = (s ^ r) * band
        here = pl.ds(pl.multiple_of(base, band), band)
        window = jnp.concatenate(
            [hidden[pl.ds(pl.multiple_of(base + columns * dy, columns), band), :] for dy in range(3)], axis=1
        )
        parts = jnp.dot(window, taps[...], preferred_element_type=F32)
        total = parts[:, wide : 2 * wide]
        total += jnp.where(column == 0, 0.0, pltpu.roll(parts[:, :wide], 1, 0))
        total += jnp.where(column == columns - 1, 0.0, pltpu.roll(parts[:, 2 * wide :], band - 1, 0))
        tail = total[:, LANES:]
        tail = tail + pltpu.roll(tail, 2 * PIECE, 1)
        tail = tail + pltpu.roll(tail, PIECE, 1)
        cells = own[here, :].astype(F32)
        out[0:band, :] = (cells[:, :LANES] + total[:, :LANES]).astype(BF16)
        tail = cells[:, LANES:] + tail
        packed = tail[0:group]
        for g in range(1, 4):
            packed = jnp.where(lane >= PIECE * g, tail[group * g : group * g + group], packed)
        out[band : band + group, :] = packed.astype(BF16)


def convolve(meta, hidden, taps, own, band, columns):
    operands = [taps, hidden, own]
    channels = hidden.shape[1]
    shapes = [jax.ShapeDtypeStruct((band + band // 4, LANES), BF16)] * 4
    return pl.pallas_call(
        lambda *refs: conv_kernel(band, columns, *refs),
        in_specs=[smem()] + [whole(x.shape) for x in operands],
        out_specs=[whole(shape.shape) for shape in shapes],
        out_shape=shapes,
        compiler_params=params(),
        cost_estimate=cost(4),
        name="convolve",
    )(meta, *operands)


def project_kernel(shards, images, count, meta, p0, p1, p2, p3, *refs):
    ours, batches = refs[:shards], refs[shards:-3]
    out, both, plan = refs[-3:]
    s, high = meta[0], meta[0] // 2
    shard, channels = ours[0].shape[1], out.shape[1]
    theirs = [batch.at[k] for batch in batches for k in range(batch.shape[0])]
    for i in range(shards):
        at = pl.ds(pl.multiple_of(shard * meta[2 + i], 16), shard)
        for block in range(channels // LANES):
            both[high, at, LANES * block : LANES * block + LANES] = ours[i][3 + block]
        both[1 - high, at, :] = theirs[i][...]
    for r, piece in enumerate((p0, p1, p2, p3)):
        rows = count // images
        start = piece.shape[0] - count
        for b in range(images):
            plan[pl.ds(pl.multiple_of(rows * (4 * b + (s ^ r)), 16), rows), :] = piece[
                start + rows * b : start + rows * b + rows, :
            ]
    out[0:channels, :] = both[0]
    out[channels:, :] = jnp.dot(plan[...], both[1], preferred_element_type=F32).astype(BF16)


def project(meta, pieces, ours, theirs, images, rows):
    channels = theirs[0].shape[2]
    operands = list(pieces) + list(ours) + list(theirs)
    return pl.pallas_call(
        lambda *refs: project_kernel(len(ours), images, rows, *refs),
        in_specs=[smem()] + [whole(x.shape) for x in operands],
        out_specs=whole((channels + 4 * rows, channels)),
        out_shape=jax.ShapeDtypeStruct((channels + 4 * rows, channels), BF16),
        scratch_shapes=[pltpu.VMEM((2, channels, channels), BF16), pltpu.VMEM((4 * rows, channels), BF16)],
        compiler_params=params(),
        cost_estimate=cost(1),
        name="project_plan",
    )(meta, *operands)


def prepare_kernel(images, meta, mine, other, cot, key, key_t, value_t, dprob, cot_t, kv, back):
    core = meta[1]
    channels = cot.shape[1]
    plan_rows = (mine.shape[0] - channels) // images

    @pl.when(core == 0)
    def _():
        kv[0] = mine[channels:]
        kv[1] = other[channels:]
        back[...] = lax.dot_general(cot[...], other[0:channels], NT, preferred_element_type=F32).astype(BF16)

    @pl.when(core != 0)
    def _():
        kv[0] = other[channels:]
        kv[1] = mine[channels:]
        back[...] = lax.dot_general(cot[...], mine[0:channels], NT, preferred_element_type=F32).astype(BF16)

    tokens = cot.shape[0] // images
    lane = lanes_of((plan_rows, LANES))
    for b in range(images):
        at = slice(tokens * b, tokens * b + tokens)
        cot_t[b] = cot[at, :].T
        for p in range(channels // LANES):
            cut = slice(LANES * p, LANES * p + LANES)
            both = []
            for which in range(2):
                part = kv[which, plan_rows * b : plan_rows * b + plan_rows, cut].astype(F32)
                both.append(
                    jnp.concatenate([jnp.where(lane < HEAD, part, 0.0), jnp.where(lane >= HEAD, part, 0.0)], axis=0)
                )
            key[b, p] = both[0].astype(BF16)
            key_t[b, p] = both[0].T.astype(BF16)
            value_t[b, p] = both[1].T.astype(BF16)
            dprob[b, p] = lax.dot_general(both[1].astype(BF16), back[at, cut], NT, preferred_element_type=F32)


def prepare(meta, mine, other, cot, images):
    channels = cot.shape[1]
    pairs = channels // LANES
    tokens = cot.shape[0] // images
    square = (images, pairs, LANES, LANES)
    shapes = [
        (square, BF16),
        (square, BF16),
        (square, BF16),
        ((images, pairs, LANES, tokens), F32),
        ((images, channels, tokens), BF16),
    ]
    return pl.pallas_call(
        lambda *refs: prepare_kernel(images, *refs),
        in_specs=[smem(), whole(mine.shape), whole(other.shape), whole(cot.shape)],
        out_specs=[whole(shape) for shape, _ in shapes],
        out_shape=[jax.ShapeDtypeStruct(shape, kind) for shape, kind in shapes],
        scratch_shapes=[pltpu.VMEM((2, mine.shape[0] - channels, channels), BF16), pltpu.VMEM(cot.shape, BF16)],
        compiler_params=params(),
        cost_estimate=cost(2),
        name="prepare_attention",
    )(meta, mine, other, cot)


def attend_kernel(image, meta, c0, c1, c2, c3, mine, other, key, key_t, value_t, dprob, cot_t, result, kept, sent, mixed, queries, att_t, dq_t):
    s = meta[0]
    core = meta[1]
    tokens, channels = result.shape
    group = tokens // 4
    scale = 1.0 / math.sqrt(HEAD)
    lane = lanes_of((group, LANES))
    krow = lax.broadcasted_iota(jnp.int32, (LANES, LANES), 0)
    kcol = lax.broadcasted_iota(jnp.int32, (LANES, LANES), 1)
    same = lax.rem(krow, PIECE) == lax.rem(kcol, PIECE)
    tail = jnp.zeros((tokens, LANES), F32)
    for r, chunk in enumerate((c0, c1, c2, c3)):
        source = s ^ r
        mixed[:, pl.ds(pl.multiple_of(source * LANES, LANES), LANES)] = chunk[0:tokens, :]
        packed = chunk[tokens : tokens + group, :]
        spread = jnp.concatenate(
            [
                jnp.where((lane >= PIECE * g) & (lane < PIECE * g + PIECE), packed, jnp.zeros((), BF16))
                for g in range(4)
            ],
            axis=0,
        )
        place = same & (kcol >= PIECE * source) & (kcol < PIECE * source + PIECE)
        tail += jnp.dot(spread, jnp.where(place, 1.0, 0.0).astype(BF16), preferred_element_type=F32)
    mixed[:, 4 * LANES :] = tail.astype(BF16)
    here = mixed[...]

    @pl.when(core == 0)
    def _():
        queries[...] = jnp.dot(here, mine[0:channels], preferred_element_type=F32).astype(BF16)

    @pl.when(core != 0)
    def _():
        queries[...] = jnp.dot(here, other[0:channels], preferred_element_type=F32).astype(BF16)

    cuts = [slice(LANES * p, LANES * p + LANES) for p in range(channels // LANES)]
    scores = [
        lax.dot_general(key[image, p], queries[:, cut], NT, preferred_element_type=F32) for p, cut in enumerate(cuts)
    ]
    probs = []
    for score in scores:
        score = score.reshape(2, HEAD, tokens) * scale
        expo = jnp.exp(score - jnp.max(score, axis=1, keepdims=True))
        probs.append(expo * (1.0 / jnp.sum(expo, axis=1, keepdims=True)))
    for p, cut in enumerate(cuts):
        att_t[cut, :] = jnp.dot(
            value_t[image, p], probs[p].reshape(LANES, tokens).astype(BF16), preferred_element_type=F32
        ).astype(BF16)
    dscores = []
    for p, prob in enumerate(probs):
        down = dprob[image, p].reshape(2, HEAD, tokens)
        dscore = prob * (down - jnp.sum(prob * down, axis=1, keepdims=True)) * scale
        dscores.append(dscore.reshape(LANES, tokens).astype(BF16))
    for p, cut in enumerate(cuts):
        dq_t[cut, :] = jnp.dot(key_t[image, p], dscores[p], preferred_element_type=F32).astype(BF16)
    attended = att_t[...].T

    @pl.when(core == 0)
    def _():
        kept[0] = here.T
        kept[1] = dq_t[...]
        sent[0] = att_t[...]
        sent[1] = cot_t[image]
        out = jnp.dot(attended, other[0:channels], preferred_element_type=F32)
        result[...] = (here.astype(F32) + out).astype(BF16)

    @pl.when(core != 0)
    def _():
        sent[0] = here.T
        sent[1] = dq_t[...]
        kept[0] = att_t[...]
        kept[1] = cot_t[image]
        out = jnp.dot(attended, mine[0:channels], preferred_element_type=F32)
        result[...] = (here.astype(F32) + out).astype(BF16)


def attend(meta, chunks, prepared, image, tokens):
    channels = prepared[0].shape[1]
    operands = list(chunks) + list(prepared)
    both = jax.ShapeDtypeStruct((2, channels, tokens), BF16)
    return pl.pallas_call(
        lambda *refs: attend_kernel(image, *refs),
        in_specs=[smem()] + [whole(x.shape) for x in operands],
        out_specs=[whole(None)] * 3,
        out_shape=[jax.ShapeDtypeStruct((tokens, channels), BF16), both, both],
        scratch_shapes=[pltpu.VMEM((tokens, channels), BF16)] * 2 + [pltpu.VMEM((channels, tokens), BF16)] * 2,
        compiler_params=params(),
        cost_estimate=cost(3),
        name="attend",
    )(meta, *operands)


def gradient(parts):
    channels = parts[0].shape[1]

    def kernel(*refs):
        left, right = (jnp.concatenate([part[k] for part in refs[:-1]], axis=1) for k in range(2))
        refs[-1][...] = lax.dot_general(left, right, NT, preferred_element_type=F32)

    return pl.pallas_call(
        kernel,
        in_specs=[whole(x.shape) for x in parts],
        out_specs=whole(None),
        out_shape=jax.ShapeDtypeStruct((channels, channels), F32),
        compiler_params=params(),
        cost_estimate=cost(1),
        name="gradient_first",
    )(*parts)


def quarter_kernel(factor, meta, partial, part, mine, *refs):
    sends, total = refs[:-1], refs[-1]
    total[...] = (partial[...] + lax.dot_general(part[0], part[1], NT, preferred_element_type=F32)) * factor
    along_x, along_y = meta[18], meta[0] // 2
    rows = mine.shape[0] // 4
    for r, out in enumerate((mine,) + sends):
        parts = []
        for z in range(4):
            at = pl.multiple_of(rows * (2 * (2 * z + (along_x ^ (r % 2))) + (along_y ^ (r // 2))), 8)
            parts.append(total[pl.ds(at, rows), :])
        out[...] = jnp.concatenate(parts, axis=0).astype(out.dtype)


def quarters(meta, partial, part, factor):
    rows, channels = partial.shape
    shapes = [jax.ShapeDtypeStruct((rows // 4, channels), kind) for kind in (F32, BF16, BF16, BF16)]
    return pl.pallas_call(
        lambda *refs: quarter_kernel(factor, *refs),
        in_specs=[smem(), whole(partial.shape), whole(part.shape)],
        out_specs=[whole(x.shape) for x in shapes],
        out_shape=shapes,
        scratch_shapes=[pltpu.VMEM((rows, channels), F32)],
        compiler_params=params(),
        cost_estimate=cost(1),
        name="gradient_last",
    )(meta, partial, part)


def line_sum(parts):
    def kernel(a, b, c, d, out):
        out[...] = a[...] + b[...].astype(F32) + c[...].astype(F32) + d[...].astype(F32)

    return pl.pallas_call(
        kernel,
        in_specs=[whole(None)] * 4,
        out_specs=whole(None),
        out_shape=jax.ShapeDtypeStruct(parts[0].shape, F32),
        compiler_params=params(),
        cost_estimate=cost(0),
        name="sum_line",
    )(*parts)


def finish_kernel(meta, mine, beside, across, corner, out):
    core, high = meta[1], meta[0] // 2
    rows = mine.shape[0]

    def ordered(a, b):
        first = jnp.where(high == 0, a[...], b[...])
        second = jnp.where(high == 0, b[...], a[...])
        return jnp.concatenate([first, second], axis=0)

    own, other = ordered(mine, across), ordered(beside, corner)
    out[:, 0, :] = jnp.where(core == 0, own, other)
    out[:, 1, :] = jnp.where(core == 0, other, own)


def finish(meta, parts):
    rows, channels = parts[0].shape
    return pl.pallas_call(
        finish_kernel,
        in_specs=[smem()] + [whole(x.shape) for x in parts],
        out_specs=whole(None),
        out_shape=jax.ShapeDtypeStruct((2 * rows, 2, channels), F32),
        compiler_params=params(),
        cost_estimate=cost(1),
        name="finish",
    )(meta, *parts)


def slab_kernel(meta, a, b, c, d, mine, *sends):
    along_z = meta[19]
    rows = mine.shape[0]
    total = a[...] + b[...].astype(F32) + c[...].astype(F32) + d[...].astype(F32)
    for z in range(4):
        part = total[rows * z : rows * z + rows]
        for r, out in enumerate((mine,) + sends):

            @pl.when((along_z ^ r) == z)
            def _(out=out, part=part):
                out[...] = part.astype(out.dtype)


def slabs(meta, parts, kinds):
    rows, channels = parts[0].shape
    shapes = [jax.ShapeDtypeStruct((rows // 4, channels), t) for t in kinds]
    return pl.pallas_call(
        slab_kernel,
        in_specs=[smem()] + [whole(x.shape) for x in parts],
        out_specs=[whole(x.shape) for x in shapes],
        out_shape=shapes,
        compiler_params=params(),
        cost_estimate=cost(1),
        name="sum_plane",
    )(meta, *parts)


def flip(x, axis, bits):
    count = lax.axis_size(axis)
    return lax.ppermute(x, axis, [(i, i ^ bits) for i in range(count)])


def flip_plane(x, bits):
    count = lax.axis_size("dp") * lax.axis_size("spatial")
    return lax.ppermute(x, ("dp", "spatial"), [(i, i ^ bits) for i in range(count)])


def ring_place(p):
    return 2 * p if p < 4 else 2 * (7 - p) + 1


def step_ring(x, backward):
    shards = lax.axis_size("dp")
    pairs = [(ring_place(p), ring_place((p + 1) % shards)) for p in range(shards)]
    return lax.ppermute(x, "dp", [(b, a) for a, b in pairs] if backward else pairs)


def after(values, *others):
    return lax.optimization_barrier((tuple(values), others))[0]


def body(latents, plan, conv_weight, gn_gain, attn_weights, cotangent):
    images, band_rows, columns, channels = latents.shape
    shards = lax.axis_size("dp")
    band = band_rows * columns
    packed, packed_more, mine, meta = pack(
        conv_weight, attn_weights, latents.reshape(images * band, channels), plan.reshape(-1, channels)
    )
    across = flip(mine, "spatial", 2)
    ring = [packed, step_ring(packed, False), step_ring(packed, True)]
    more = [packed_more, step_ring(packed_more, False), step_ring(packed_more, True)]
    for _ in range(2):
        ring += [step_ring(ring[-2], False), step_ring(ring[-1], True)]
        more += [step_ring(more[-2], False), step_ring(more[-1], True)]
    (across,) = after([across], *ring[3:5], *more[3:5])
    pieces = [mine, flip(mine, "spatial", 1), across, flip(across, "spatial", 1)]
    given = [flip(collect(more[:5], 3), "spatial", 2)]
    stats = group_stats(meta, pieces, gn_gain, images, band)
    normed = [normalise(meta, pieces, stats, b, images, band, columns) for b in range(images)]
    a, b = after((ring[5], more[6]), *(x[1] for x in normed))
    ring.append(step_ring(a, False))
    more.append(step_ring(b, True))
    given.append(flip(collect(more[5:7], 3), "spatial", 2))
    taps = first_taps(meta, ring[:7], more[:7], channels)
    ring[7], more[7], taps = after((ring[7], more[7], taps))
    taps = last_taps(meta, taps, (ring[7], more[7]))
    given.append(flip(collect(more[7:], 3), "spatial", 2))

    chunks = []
    for hidden, own in normed:
        outs = convolve(meta, hidden, taps, own, band, columns)
        if not chunks:
            (given[2],) = after([given[2]], outs[0])
        chunks.append([outs[0]] + [flip(outs[r], "spatial", r) for r in (1, 2, 3)])

    projected = project(meta, pieces, more, given, images, plan.shape[0] * plan.shape[1])
    cot = cotangent.reshape(images * band, channels)
    both = [projected, flip(projected, "spatial", 1)]
    prepared = both + list(prepare(meta, *both, cot, images))
    tokens = images * shards * band * lax.axis_size("spatial")
    results = []
    kept = []
    given = []
    for b in range(images):
        result, keep, send = attend(meta, chunks[b], prepared, b, band)
        results.append(result.reshape(1, band_rows, columns, channels))
        kept.append(keep)
        given.append(flip(send, "spatial", 1))
    partial = gradient(kept + given[:-1])
    mine, *sends = quarters(meta, partial, given[-1], 1.0 / math.sqrt(tokens))
    moved = [flip_plane(sends[r - 1], 4 * (r % 2) + 2 * (r // 2)) for r in (1, 2, 3)]
    mine, *sends = slabs(meta, [mine] + moved, (F32, F32, F32, BF16))
    total = line_sum([mine] + [flip(sends[r - 1], "dp", 2 * r) for r in (1, 2, 3)])
    grads = finish(meta, [total] + [flip(total, "spatial", r) for r in (1, 2, 3)])
    return jnp.concatenate(results), grads


def solution(mesh):
    fits = mesh.shape["dp"] == 8 and mesh.shape["spatial"] == 4
    return jax.shard_map(
        body if fits else plain_body,
        mesh=mesh,
        in_specs=(
            P("dp", "spatial", None, None),
            P("dp", "spatial", None),
            P(None, "dp", None),
            P(),
            P(None, "dp", None),
            P("dp", "spatial", None, None),
        ),
        out_specs=(P("dp", "spatial", None, None), P("dp", None, None)),
        check_vma=False,
    )
```

```python
import math

import jax
import jax.numpy as jnp
from jax import lax
from jax.experimental import pallas as pl
from jax.experimental.pallas import tpu as pltpu
from jax.sharding import PartitionSpec as P

GROUPS = 32
HEAD = 64


eps_norm = 1e-05


def with_halo(cells, sides, width):
    for axis, dim in sides:
        count = lax.axis_size(axis)
        ends = count - 1
        head = lax.slice_in_dim(cells, 0, width, axis=dim)
        tail = lax.slice_in_dim(cells, cells.shape[dim] - width, cells.shape[dim], axis=dim)
        cells = jnp.concatenate(
            [
                lax.ppermute(tail, axis, [(i, (i + 1) % count) for i in range(ends)]),
                cells,
                lax.ppermute(head, axis, [((i + 1) % count, i) for i in range(ends)]),
            ],
            axis=dim,
        )
    return cells


def plain_body(latents, plan, conv_weight, gn_gain, attn_weights, cotangent):
    images, band_rows, columns, channels = latents.shape
    heads = channels // HEAD
    per_group = channels // GROUPS
    tokens_here = images * band_rows * columns
    scale = 1.0 / math.sqrt(HEAD)
    flat_input = latents.astype(jnp.float32).reshape(images, band_rows * columns, GROUPS, per_group)
    first_sums = jnp.sum(flat_input, axis=(1, 3))
    second_sums = jnp.sum(flat_input * flat_input, axis=(1, 3))
    first_sums, second_sums = lax.psum((first_sums, second_sums), "spatial")
    counted = float(band_rows * lax.axis_size("spatial") * columns * per_group)
    means = first_sums / counted
    variance = second_sums / counted - means * means
    inverse = lax.rsqrt(variance + eps_norm)
    normed = (flat_input - means[:, None, :, None]) * inverse[:, None, :, None]
    normed = normed.reshape(images, band_rows, columns, channels) * gn_gain
    hidden = jax.nn.silu(normed).astype(jnp.bfloat16)
    padded = with_halo(hidden, (("spatial", 1),), 1)
    padded = jnp.pad(padded, ((0, 0), (0, 0), (1, 1), (0, 0)))
    tapped = jnp.stack(
        [
            padded[:, offset_y : offset_y + band_rows, offset_x : offset_x + columns].reshape(
                tokens_here, channels
            )
            for offset_y in range(3)
            for offset_x in range(3)
        ],
        1,
    )
    conv_sum = jnp.einsum(
        "ntc,tcd->nd",
        tapped,
        lax.all_gather(conv_weight, "dp", axis=1, tiled=True),
        preferred_element_type=jnp.float32,
    )
    mixed = (latents.reshape(tokens_here, channels).astype(jnp.float32) + conv_sum).astype(
        jnp.bfloat16
    )
    weights = lax.all_gather(attn_weights, "dp", axis=1, tiled=True)
    weight_q = weights[0]
    weight_k = weights[1]
    weight_v = weights[2]
    weight_o = weights[3]
    queries = jnp.dot(mixed, weight_q, preferred_element_type=jnp.float32).astype(jnp.bfloat16)
    plan_all = lax.all_gather(plan, "spatial", axis=1, tiled=True)
    plan_flat = plan_all.reshape(-1, channels)
    keys_all = jnp.dot(plan_flat, weight_k, preferred_element_type=jnp.float32).astype(jnp.bfloat16)
    values_all = jnp.dot(plan_flat, weight_v, preferred_element_type=jnp.float32).astype(
        jnp.bfloat16
    )
    keys_all = keys_all.reshape(images, -1, channels)
    values_all = values_all.reshape(images, -1, channels)
    plan_tokens = keys_all.shape[1]
    query_heads = queries.reshape(images, band_rows * columns, heads, HEAD)
    key_heads = keys_all.reshape(images, plan_tokens, heads, HEAD)
    value_heads = values_all.reshape(images, plan_tokens, heads, HEAD)
    scores = (
        jnp.einsum("bnhe,bmhe->bhnm", query_heads, key_heads, preferred_element_type=jnp.float32)
        * scale
    )
    maxima = jnp.max(scores, axis=-1, keepdims=True)
    expo = jnp.exp(scores - maxima)
    probs = expo / jnp.sum(expo, axis=-1, keepdims=True)
    probs_b = probs.astype(jnp.bfloat16)
    attended = jnp.einsum(
        "bhnm,bmhe->bnhe", probs_b, value_heads, preferred_element_type=jnp.float32
    )
    attended = attended.reshape(tokens_here, channels).astype(jnp.bfloat16)
    result = mixed.astype(jnp.float32) + jnp.dot(
        attended, weight_o, preferred_element_type=jnp.float32
    )
    block_out = result.astype(jnp.bfloat16).reshape(images, band_rows, columns, channels)
    grad_flat = cotangent.reshape(tokens_here, channels)
    grad_att = lax.dot_general(
        grad_flat, weight_o, (((1,), (1,)), ((), ())), preferred_element_type=jnp.float32
    )
    grad_att = grad_att.astype(jnp.bfloat16).reshape(images, band_rows * columns, heads, HEAD)
    dprob = jnp.einsum("bnhe,bmhe->bhnm", grad_att, value_heads, preferred_element_type=jnp.float32)
    dscore = (probs * (dprob - jnp.sum(probs * dprob, axis=-1, keepdims=True)) * scale).astype(
        jnp.bfloat16
    )
    dquery = jnp.einsum("bhnm,bmhe->bnhe", dscore, key_heads, preferred_element_type=jnp.float32)
    dquery = dquery.reshape(tokens_here, channels).astype(jnp.bfloat16)
    total_tokens = images * lax.axis_size("dp") * band_rows * lax.axis_size("spatial") * columns
    factor = 1.0 / math.sqrt(total_tokens)
    contract = (((0,), (0,)), ((), ()))
    grad_query = lax.dot_general(mixed, dquery, contract, preferred_element_type=jnp.float32)
    grad_output = lax.dot_general(attended, grad_flat, contract, preferred_element_type=jnp.float32)
    own_rows = lax.psum_scatter(
        jnp.stack([grad_query, grad_output], 1) * factor, "dp", scatter_dimension=0, tiled=True
    )
    weight_grads = lax.psum(own_rows, "spatial")
    return (block_out, weight_grads)


F32 = jnp.float32
BF16 = jnp.bfloat16
LANES = 128
PIECE = 32
VMEM_LIMIT = 24 * 1024 * 1024
NT = (((1,), (1,)), ((), ()))


def cost(microseconds):
    return pl.CostEstimate(flops=0, bytes_accessed=microseconds * 3690000, transcendentals=0)


def params():
    return pltpu.CompilerParams(vmem_limit_bytes=VMEM_LIMIT)


def whole(shape):
    return pl.BlockSpec(memory_space=pltpu.VMEM)


def smem():
    return pl.BlockSpec(memory_space=pltpu.SMEM)


def lanes_of(shape):
    return lax.broadcasted_iota(jnp.int32, shape, len(shape) - 1)


def pack_kernel(conv_hbm, attn_hbm, latents_hbm, plan_hbm, out, more, rows_out, meta, weight, matrix, sems):
    s = lax.axis_index("spatial")
    core, high = s % 2, s // 2
    split = latents_hbm.shape[0]
    copies = [
        pltpu.make_async_copy(conv_hbm, weight, sems.at[0]),
        pltpu.make_async_copy(attn_hbm.at[jnp.where(high == 0, 3 * core, 1 + core)], matrix, sems.at[1]),
        pltpu.make_async_copy(latents_hbm, rows_out.at[pl.ds(0, split)], sems.at[2]),
        pltpu.make_async_copy(plan_hbm, rows_out.at[pl.ds(split, plan_hbm.shape[0])], sems.at[3]),
    ]
    for copy in copies:
        copy.start()
    me = lax.axis_index("dp")
    along_x, along_z = me % 2, me // 2
    position = jnp.where(along_x == 0, along_z, 7 - along_z)
    where = [(position + o + 8) % 8 for o in (0, -1, 1, -2, 2, -3, 3, -4)]
    held = [jnp.where(p < 4, 2 * p, 2 * (7 - p) + 1) for p in where]
    slots = [sum(jnp.where(h == j, i, 0) for i, h in enumerate(held)) for j in range(8)]
    for k, fact in enumerate([s, core] + held + slots + [along_x, along_z]):
        meta[k] = fact.astype(jnp.int32)
    copies[0].wait()
    out[0:9] = weight[:, :, pl.ds(pl.multiple_of(s * LANES, LANES), LANES)]
    rows = lax.broadcasted_iota(jnp.int32, (LANES, LANES), 0)
    cols = lax.broadcasted_iota(jnp.int32, (LANES, LANES), 1)
    last = 4 * LANES
    for dy in range(3):
        total = None
        for dx in range(3):
            pick = (rows == PIECE * s + cols - PIECE * dx) & (cols >= PIECE * dx) & (cols < PIECE * dx + PIECE)
            part = jnp.dot(
                weight[3 * dy + dx, :, last : last + LANES],
                jnp.where(pick, 1.0, 0.0).astype(BF16),
                preferred_element_type=F32,
            )
            total = part if total is None else total + part
        more[dy] = total.astype(BF16)
    copies[1].wait()
    for k in range(matrix.shape[1] // LANES):
        more[3 + k] = matrix[:, LANES * k : LANES * k + LANES]
    copies[2].wait()
    copies[3].wait()


def pack(conv_weight, attn_weights, latents, plan):
    taps, rows, channels = conv_weight.shape
    shapes = [
        (taps, rows, LANES),
        (3 + channels // LANES, rows, LANES),
        (latents.shape[0] + plan.shape[0], channels),
    ]
    return pl.pallas_call(
        pack_kernel,
        in_specs=[pl.BlockSpec(memory_space=pltpu.HBM)] * 4,
        out_specs=[whole(shape) for shape in shapes] + [smem()],
        out_shape=[jax.ShapeDtypeStruct(shape, BF16) for shape in shapes] + [jax.ShapeDtypeStruct((20,), jnp.int32)],
        scratch_shapes=[
            pltpu.VMEM(conv_weight.shape, BF16),
            pltpu.VMEM((rows, channels), BF16),
            pltpu.SemaphoreType.DMA((4,)),
        ],
        compiler_params=params(),
        cost_estimate=cost(1),
        name="pack",
    )(*(pltpu.with_memory_space_constraint(x, pltpu.HBM) for x in (conv_weight, attn_weights, latents, plan)))


def collect(parts, first):
    blocks, rows = parts[0].shape[0] - first, parts[0].shape[1]

    def kernel(*refs):
        for k, part in enumerate(refs[:-1]):
            for block in range(blocks):
                refs[-1][k, :, LANES * block : LANES * block + LANES] = part[first + block]

    return pl.pallas_call(
        kernel,
        in_specs=[whole(None)] * len(parts),
        out_specs=whole(None),
        out_shape=jax.ShapeDtypeStruct((len(parts), rows, LANES * blocks), BF16),
        compiler_params=params(),
        cost_estimate=cost(0),
        name="collect",
    )(*parts)


def stats_kernel(images, band, per_group, count, meta, x0, x1, x2, x3, gain, out):
    channels = gain.shape[0]
    shape = (channels, channels)
    row_group = jnp.floor((lax.broadcasted_iota(jnp.int32, shape, 0).astype(F32) + 0.5) * (1.0 / per_group))
    col_group = jnp.floor((lax.broadcasted_iota(jnp.int32, shape, 1).astype(F32) + 0.5) * (1.0 / per_group))
    same_group = jnp.where(row_group == col_group, 1.0, 0.0).astype(BF16)
    sums = []
    for b in range(images):
        first = jnp.zeros((1, channels), F32)
        second = jnp.zeros((1, channels), F32)
        for piece in (x0, x1, x2, x3):
            x = piece[band * b : band * b + band, :].astype(F32)
            first += jnp.sum(x, axis=0, keepdims=True)
            second += jnp.sum(x * x, axis=0, keepdims=True)
        sums += [first, second]
    sums = jnp.concatenate(sums, axis=0)
    high = sums.astype(BF16)
    rest = sums - high.astype(F32)
    middle = rest.astype(BF16)
    low = (rest - middle.astype(F32)).astype(BF16)
    grouped = sum(jnp.dot(part, same_group, preferred_element_type=F32) for part in (high, middle, low))
    for b in range(images):
        mean = grouped[2 * b : 2 * b + 1] / count
        variance = grouped[2 * b + 1 : 2 * b + 2] / count - mean * mean
        out[b : b + 1, :] = mean
        out[images + b : images + b + 1, :] = lax.rsqrt(variance + eps_norm) * gain[...].reshape(1, channels) * 0.5


def group_stats(meta, pieces, gain, images, band):
    channels = gain.shape[-1]
    per_group = channels // GROUPS
    return pl.pallas_call(
        lambda *refs: stats_kernel(images, band, per_group, float(4 * band * per_group), *refs),
        in_specs=[smem()] + [whole(None)] * 5,
        out_specs=whole(None),
        out_shape=jax.ShapeDtypeStruct((2 * images, channels), F32),
        compiler_params=params(),
        cost_estimate=cost(0),
        name="group_stats",
    )(meta, *pieces, gain)


def norm_kernel(image, images, band, columns, meta, x0, x1, x2, x3, stats, hidden, own):
    s = meta[0]
    pieces = [x.at[image * band : image * band + band] for x in (x0, x1, x2, x3)]
    channels = stats.shape[1]
    mean = stats[image : image + 1, :]
    factor = stats[images + image : images + image + 1, :]
    rows = 64
    hidden[0:columns, :] = jnp.zeros((columns, channels), BF16)
    hidden[columns + 4 * band :, :] = jnp.zeros((columns, channels), BF16)
    krow = lax.broadcasted_iota(jnp.int32, (LANES, LANES), 0)
    kcol = lax.broadcasted_iota(jnp.int32, (LANES, LANES), 1)
    repeat = jnp.where(krow == PIECE * s + lax.rem(kcol, PIECE), 1.0, 0.0).astype(BF16)
    for r, piece in enumerate(pieces):
        base = (s ^ r) * band
        own[pl.ds(pl.multiple_of(base, band), band), 0:LANES] = piece[
            :, pl.ds(pl.multiple_of(s * LANES, LANES), LANES)
        ]
        own[pl.ds(pl.multiple_of(base, band), band), LANES : 2 * LANES] = jnp.dot(
            piece[:, 4 * LANES :], repeat, preferred_element_type=F32
        ).astype(BF16)
        for at in range(0, band, rows):
            t = (piece[at : at + rows, :].astype(F32) - mean) * factor
            hidden[pl.ds(pl.multiple_of(base + columns + at, columns), rows), :] = (t + t * jnp.tanh(t)).astype(BF16)


def normalise(meta, pieces, stats, image, images, band, columns):
    channels = stats.shape[-1]
    tokens = 4 * band
    hidden = (tokens + 2 * columns, channels)
    own = (tokens, 2 * LANES)
    return pl.pallas_call(
        lambda *refs: norm_kernel(image, images, band, columns, *refs),
        in_specs=[smem()] + [whole(None)] * 5,
        out_specs=[whole(hidden), whole(own)],
        out_shape=[jax.ShapeDtypeStruct(hidden, BF16), jax.ShapeDtypeStruct(own, BF16)],
        compiler_params=params(),
        cost_estimate=cost(0),
        name="normalise",
    )(meta, *pieces, stats)


def fill_taps(taps, at, shard, tap):
    lane = lanes_of((shard, LANES))
    wide = 2 * LANES
    rows = taps.shape[0] // 3
    for dy in range(3):
        here = pl.ds(pl.multiple_of(rows * dy + at, 16), shard)
        for dx in range(3):
            taps[here, wide * dx : wide * dx + LANES] = tap(3 * dy + dx)
            taps[here, wide * dx + LANES : wide * dx + wide] = jnp.where(
                (lane >= PIECE * dx) & (lane < PIECE * dx + PIECE), tap(9 + dy), jnp.zeros((), BF16)
            )


def first_taps(meta, weights, more, channels):
    shard, count = weights[0].shape[1], len(weights)

    def kernel(meta, *refs):
        for i in range(count):
            fill_taps(
                refs[-1], shard * meta[2 + i], shard, lambda k, i=i: refs[i][k] if k < 9 else refs[count + i][k - 9]
            )

    return pl.pallas_call(
        kernel,
        in_specs=[smem()] + [whole(None)] * (2 * count),
        out_specs=whole(None),
        out_shape=jax.ShapeDtypeStruct((3 * channels, 6 * LANES), BF16),
        compiler_params=params(),
        cost_estimate=cost(6),
        name="first_taps",
    )(meta, *weights, *more)


def last_taps(meta, taps, halves):
    shard = halves[0].shape[1]

    def kernel(meta, before, one, two, after):
        split = one.shape[0]
        after[...] = before[...]
        fill_taps(after, shard * meta[9], shard, lambda k: one[k] if k < split else two[k - split])

    return pl.pallas_call(
        kernel,
        in_specs=[smem()] + [whole(None)] * 3,
        out_specs=whole(None),
        out_shape=jax.ShapeDtypeStruct(taps.shape, BF16),
        compiler_params=params(),
        cost_estimate=cost(0),
        name="last_taps",
    )(meta, taps, *halves)


def conv_kernel(band, columns, meta, taps, hidden, own, *refs):
    outs = refs
    s = meta[0]
    channels = hidden.shape[1]
    wide = 2 * LANES
    column = lax.rem(lax.broadcasted_iota(jnp.int32, (band, wide), 0), columns)
    group = band // 4
    lane = lanes_of((group, LANES))
    for r, out in enumerate(outs):
        base = (s ^ r) * band
        here = pl.ds(pl.multiple_of(base, band), band)
        window = jnp.concatenate(
            [hidden[pl.ds(pl.multiple_of(base + columns * dy, columns), band), :] for dy in range(3)], axis=1
        )
        parts = jnp.dot(window, taps[...], preferred_element_type=F32)
        total = parts[:, wide : 2 * wide]
        total += jnp.where(column == 0, 0.0, pltpu.roll(parts[:, :wide], 1, 0))
        total += jnp.where(column == columns - 1, 0.0, pltpu.roll(parts[:, 2 * wide :], band - 1, 0))
        tail = total[:, LANES:]
        tail = tail + pltpu.roll(tail, 2 * PIECE, 1)
        tail = tail + pltpu.roll(tail, PIECE, 1)
        cells = own[here, :].astype(F32)
        out[0:band, :] = (cells[:, :LANES] + total[:, :LANES]).astype(BF16)
        tail = cells[:, LANES:] + tail
        packed = tail[0:group]
        for g in range(1, 4):
            packed = jnp.where(lane >= PIECE * g, tail[group * g : group * g + group], packed)
        out[band : band + group, :] = packed.astype(BF16)


def convolve(meta, hidden, taps, own, band, columns):
    operands = [taps, hidden, own]
    channels = hidden.shape[1]
    shapes = [jax.ShapeDtypeStruct((band + band // 4, LANES), BF16)] * 4
    return pl.pallas_call(
        lambda *refs: conv_kernel(band, columns, *refs),
        in_specs=[smem()] + [whole(x.shape) for x in operands],
        out_specs=[whole(shape.shape) for shape in shapes],
        out_shape=shapes,
        compiler_params=params(),
        cost_estimate=cost(4),
        name="convolve",
    )(meta, *operands)


def project_kernel(shards, images, count, meta, p0, p1, p2, p3, *refs):
    ours, batches = refs[:shards], refs[shards:-3]
    out, both, plan = refs[-3:]
    s, high = meta[0], meta[0] // 2
    shard, channels = ours[0].shape[1], out.shape[1]
    theirs = [batch.at[k] for batch in batches for k in range(batch.shape[0])]
    for i in range(shards):
        at = pl.ds(pl.multiple_of(shard * meta[2 + i], 16), shard)
        for block in range(channels // LANES):
            both[high, at, LANES * block : LANES * block + LANES] = ours[i][3 + block]
        both[1 - high, at, :] = theirs[i][...]
    for r, piece in enumerate((p0, p1, p2, p3)):
        rows = count // images
        start = piece.shape[0] - count
        for b in range(images):
            plan[pl.ds(pl.multiple_of(rows * (4 * b + (s ^ r)), 16), rows), :] = piece[
                start + rows * b : start + rows * b + rows, :
            ]
    out[0:channels, :] = both[0]
    out[channels:, :] = jnp.dot(plan[...], both[1], preferred_element_type=F32).astype(BF16)


def project(meta, pieces, ours, theirs, images, rows):
    channels = theirs[0].shape[2]
    operands = list(pieces) + list(ours) + list(theirs)
    return pl.pallas_call(
        lambda *refs: project_kernel(len(ours), images, rows, *refs),
        in_specs=[smem()] + [whole(x.shape) for x in operands],
        out_specs=whole((channels + 4 * rows, channels)),
        out_shape=jax.ShapeDtypeStruct((channels + 4 * rows, channels), BF16),
        scratch_shapes=[pltpu.VMEM((2, channels, channels), BF16), pltpu.VMEM((4 * rows, channels), BF16)],
        compiler_params=params(),
        cost_estimate=cost(1),
        name="project_plan",
    )(meta, *operands)


def prepare_kernel(images, meta, mine, other, cot, key, key_t, value_t, dprob, cot_t, kv, back):
    core = meta[1]
    channels = cot.shape[1]
    plan_rows = (mine.shape[0] - channels) // images

    @pl.when(core == 0)
    def _():
        kv[0] = mine[channels:]
        kv[1] = other[channels:]
        back[...] = lax.dot_general(cot[...], other[0:channels], NT, preferred_element_type=F32).astype(BF16)

    @pl.when(core != 0)
    def _():
        kv[0] = other[channels:]
        kv[1] = mine[channels:]
        back[...] = lax.dot_general(cot[...], mine[0:channels], NT, preferred_element_type=F32).astype(BF16)

    tokens = cot.shape[0] // images
    lane = lanes_of((plan_rows, LANES))
    for b in range(images):
        at = slice(tokens * b, tokens * b + tokens)
        cot_t[b] = cot[at, :].T
        for p in range(channels // LANES):
            cut = slice(LANES * p, LANES * p + LANES)
            both = []
            for which in range(2):
                part = kv[which, plan_rows * b : plan_rows * b + plan_rows, cut].astype(F32)
                both.append(
                    jnp.concatenate([jnp.where(lane < HEAD, part, 0.0), jnp.where(lane >= HEAD, part, 0.0)], axis=0)
                )
            key[b, p] = both[0].astype(BF16)
            key_t[b, p] = both[0].T.astype(BF16)
            value_t[b, p] = both[1].T.astype(BF16)
            dprob[b, p] = lax.dot_general(both[1].astype(BF16), back[at, cut], NT, preferred_element_type=F32)


def prepare(meta, mine, other, cot, images):
    channels = cot.shape[1]
    pairs = channels // LANES
    tokens = cot.shape[0] // images
    square = (images, pairs, LANES, LANES)
    shapes = [
        (square, BF16),
        (square, BF16),
        (square, BF16),
        ((images, pairs, LANES, tokens), F32),
        ((images, channels, tokens), BF16),
    ]
    return pl.pallas_call(
        lambda *refs: prepare_kernel(images, *refs),
        in_specs=[smem(), whole(mine.shape), whole(other.shape), whole(cot.shape)],
        out_specs=[whole(shape) for shape, _ in shapes],
        out_shape=[jax.ShapeDtypeStruct(shape, kind) for shape, kind in shapes],
        scratch_shapes=[pltpu.VMEM((2, mine.shape[0] - channels, channels), BF16), pltpu.VMEM(cot.shape, BF16)],
        compiler_params=params(),
        cost_estimate=cost(2),
        name="prepare_attention",
    )(meta, mine, other, cot)


def attend_kernel(image, meta, c0, c1, c2, c3, mine, other, key, key_t, value_t, dprob, cot_t, result, kept, sent, mixed, queries, att_t, dq_t):
    s = meta[0]
    core = meta[1]
    tokens, channels = result.shape
    group = tokens // 4
    scale = 1.0 / math.sqrt(HEAD)
    lane = lanes_of((group, LANES))
    krow = lax.broadcasted_iota(jnp.int32, (LANES, LANES), 0)
    kcol = lax.broadcasted_iota(jnp.int32, (LANES, LANES), 1)
    same = lax.rem(krow, PIECE) == lax.rem(kcol, PIECE)
    tail = jnp.zeros((tokens, LANES), F32)
    for r, chunk in enumerate((c0, c1, c2, c3)):
        source = s ^ r
        mixed[:, pl.ds(pl.multiple_of(source * LANES, LANES), LANES)] = chunk[0:tokens, :]
        packed = chunk[tokens : tokens + group, :]
        spread = jnp.concatenate(
            [
                jnp.where((lane >= PIECE * g) & (lane < PIECE * g + PIECE), packed, jnp.zeros((), BF16))
                for g in range(4)
            ],
            axis=0,
        )
        place = same & (kcol >= PIECE * source) & (kcol < PIECE * source + PIECE)
        tail += jnp.dot(spread, jnp.where(place, 1.0, 0.0).astype(BF16), preferred_element_type=F32)
    mixed[:, 4 * LANES :] = tail.astype(BF16)
    here = mixed[...]

    @pl.when(core == 0)
    def _():
        queries[...] = jnp.dot(here, mine[0:channels], preferred_element_type=F32).astype(BF16)

    @pl.when(core != 0)
    def _():
        queries[...] = jnp.dot(here, other[0:channels], preferred_element_type=F32).astype(BF16)

    cuts = [slice(LANES * p, LANES * p + LANES) for p in range(channels // LANES)]
    scores = [
        lax.dot_general(key[image, p], queries[:, cut], NT, preferred_element_type=F32) for p, cut in enumerate(cuts)
    ]
    probs = []
    for score in scores:
        score = score.reshape(2, HEAD, tokens) * scale
        expo = jnp.exp(score - jnp.max(score, axis=1, keepdims=True))
        probs.append(expo * (1.0 / jnp.sum(expo, axis=1, keepdims=True)))
    for p, cut in enumerate(cuts):
        att_t[cut, :] = jnp.dot(
            value_t[image, p], probs[p].reshape(LANES, tokens).astype(BF16), preferred_element_type=F32
        ).astype(BF16)
    dscores = []
    for p, prob in enumerate(probs):
        down = dprob[image, p].reshape(2, HEAD, tokens)
        dscore = prob * (down - jnp.sum(prob * down, axis=1, keepdims=True)) * scale
        dscores.append(dscore.reshape(LANES, tokens).astype(BF16))
    for p, cut in enumerate(cuts):
        dq_t[cut, :] = jnp.dot(key_t[image, p], dscores[p], preferred_element_type=F32).astype(BF16)
    attended = att_t[...].T

    @pl.when(core == 0)
    def _():
        kept[0] = here.T
        kept[1] = dq_t[...]
        sent[0] = att_t[...]
        sent[1] = cot_t[image]
        out = jnp.dot(attended, other[0:channels], preferred_element_type=F32)
        result[...] = (here.astype(F32) + out).astype(BF16)

    @pl.when(core != 0)
    def _():
        sent[0] = here.T
        sent[1] = dq_t[...]
        kept[0] = att_t[...]
        kept[1] = cot_t[image]
        out = jnp.dot(attended, mine[0:channels], preferred_element_type=F32)
        result[...] = (here.astype(F32) + out).astype(BF16)


def attend(meta, chunks, prepared, image, tokens):
    channels = prepared[0].shape[1]
    operands = list(chunks) + list(prepared)
    both = jax.ShapeDtypeStruct((2, channels, tokens), BF16)
    return pl.pallas_call(
        lambda *refs: attend_kernel(image, *refs),
        in_specs=[smem()] + [whole(x.shape) for x in operands],
        out_specs=[whole(None)] * 3,
        out_shape=[jax.ShapeDtypeStruct((tokens, channels), BF16), both, both],
        scratch_shapes=[pltpu.VMEM((tokens, channels), BF16)] * 2 + [pltpu.VMEM((channels, tokens), BF16)] * 2,
        compiler_params=params(),
        cost_estimate=cost(3),
        name="attend",
    )(meta, *operands)


def gradient(parts):
    channels = parts[0].shape[1]

    def kernel(*refs):
        left, right = (jnp.concatenate([part[k] for part in refs[:-1]], axis=1) for k in range(2))
        refs[-1][...] = lax.dot_general(left, right, NT, preferred_element_type=F32)

    return pl.pallas_call(
        kernel,
        in_specs=[whole(x.shape) for x in parts],
        out_specs=whole(None),
        out_shape=jax.ShapeDtypeStruct((channels, channels), F32),
        compiler_params=params(),
        cost_estimate=cost(1),
        name="gradient_first",
    )(*parts)


def quarter_kernel(factor, meta, partial, part, mine, *refs):
    sends, total = refs[:-1], refs[-1]
    total[...] = (partial[...] + lax.dot_general(part[0], part[1], NT, preferred_element_type=F32)) * factor
    along_x, along_y = meta[18], meta[0] // 2
    rows = mine.shape[0] // 4
    for r, out in enumerate((mine,) + sends):
        parts = []
        for z in range(4):
            at = pl.multiple_of(rows * (2 * (2 * z + (along_x ^ (r % 2))) + (along_y ^ (r // 2))), 8)
            parts.append(total[pl.ds(at, rows), :])
        out[...] = jnp.concatenate(parts, axis=0).astype(out.dtype)


def quarters(meta, partial, part, factor):
    rows, channels = partial.shape
    shapes = [jax.ShapeDtypeStruct((rows // 4, channels), kind) for kind in (F32, BF16, BF16, BF16)]
    return pl.pallas_call(
        lambda *refs: quarter_kernel(factor, *refs),
        in_specs=[smem(), whole(partial.shape), whole(part.shape)],
        out_specs=[whole(x.shape) for x in shapes],
        out_shape=shapes,
        scratch_shapes=[pltpu.VMEM((rows, channels), F32)],
        compiler_params=params(),
        cost_estimate=cost(1),
        name="gradient_last",
    )(meta, partial, part)


def line_sum(parts):
    def kernel(a, b, c, d, out):
        out[...] = a[...] + b[...].astype(F32) + c[...].astype(F32) + d[...].astype(F32)

    return pl.pallas_call(
        kernel,
        in_specs=[whole(None)] * 4,
        out_specs=whole(None),
        out_shape=jax.ShapeDtypeStruct(parts[0].shape, F32),
        compiler_params=params(),
        cost_estimate=cost(0),
        name="sum_line",
    )(*parts)


def finish_kernel(meta, mine, beside, across, corner, out):
    core, high = meta[1], meta[0] // 2
    rows = mine.shape[0]

    def ordered(a, b):
        first = jnp.where(high == 0, a[...], b[...])
        second = jnp.where(high == 0, b[...], a[...])
        return jnp.concatenate([first, second], axis=0)

    own, other = ordered(mine, across), ordered(beside, corner)
    out[:, 0, :] = jnp.where(core == 0, own, other)
    out[:, 1, :] = jnp.where(core == 0, other, own)


def finish(meta, parts):
    rows, channels = parts[0].shape
    return pl.pallas_call(
        finish_kernel,
        in_specs=[smem()] + [whole(x.shape) for x in parts],
        out_specs=whole(None),
        out_shape=jax.ShapeDtypeStruct((2 * rows, 2, channels), F32),
        compiler_params=params(),
        cost_estimate=cost(1),
        name="finish",
    )(meta, *parts)


def slab_kernel(meta, a, b, c, d, mine, *sends):
    along_z = meta[19]
    rows = mine.shape[0]
    total = a[...] + b[...].astype(F32) + c[...].astype(F32) + d[...].astype(F32)
    for z in range(4):
        part = total[rows * z : rows * z + rows]
        for r, out in enumerate((mine,) + sends):

            @pl.when((along_z ^ r) == z)
            def _(out=out, part=part):
                out[...] = part.astype(out.dtype)


def slabs(meta, parts, kinds):
    rows, channels = parts[0].shape
    shapes = [jax.ShapeDtypeStruct((rows // 4, channels), t) for t in kinds]
    return pl.pallas_call(
        slab_kernel,
        in_specs=[smem()] + [whole(x.shape) for x in parts],
        out_specs=[whole(x.shape) for x in shapes],
        out_shape=shapes,
        compiler_params=params(),
        cost_estimate=cost(1),
        name="sum_plane",
    )(meta, *parts)


def flip(x, axis, bits):
    count = lax.axis_size(axis)
    return lax.ppermute(x, axis, [(i, i ^ bits) for i in range(count)])


def flip_plane(x, bits):
    count = lax.axis_size("dp") * lax.axis_size("spatial")
    return lax.ppermute(x, ("dp", "spatial"), [(i, i ^ bits) for i in range(count)])


def ring_place(p):
    return 2 * p if p < 4 else 2 * (7 - p) + 1


def step_ring(x, backward):
    shards = lax.axis_size("dp")
    pairs = [(ring_place(p), ring_place((p + 1) % shards)) for p in range(shards)]
    return lax.ppermute(x, "dp", [(b, a) for a, b in pairs] if backward else pairs)


def after(values, *others):
    return lax.optimization_barrier((tuple(values), others))[0]


def body(latents, plan, conv_weight, gn_gain, attn_weights, cotangent):
    images, band_rows, columns, channels = latents.shape
    shards = lax.axis_size("dp")
    band = band_rows * columns
    packed, packed_more, mine, meta = pack(
        conv_weight, attn_weights, latents.reshape(images * band, channels), plan.reshape(-1, channels)
    )
    across = flip(mine, "spatial", 2)
    ring = [packed, step_ring(packed, False), step_ring(packed, True)]
    more = [packed_more, step_ring(packed_more, False), step_ring(packed_more, True)]
    for _ in range(2):
        ring += [step_ring(ring[-2], False), step_ring(ring[-1], True)]
        more += [step_ring(more[-2], False), step_ring(more[-1], True)]
    (across,) = after([across], *ring[3:5], *more[3:5])
    pieces = [mine, flip(mine, "spatial", 1), across, flip(across, "spatial", 1)]
    given = [flip(collect(more[:5], 3), "spatial", 2)]
    stats = group_stats(meta, pieces, gn_gain, images, band)
    normed = [normalise(meta, pieces, stats, b, images, band, columns) for b in range(images)]
    a, b = after((ring[5], more[6]), *(x[1] for x in normed))
    ring.append(step_ring(a, False))
    more.append(step_ring(b, True))
    given.append(flip(collect(more[5:7], 3), "spatial", 2))
    taps = first_taps(meta, ring[:7], more[:7], channels)
    ring[7], more[7], taps = after((ring[7], more[7], taps))
    taps = last_taps(meta, taps, (ring[7], more[7]))
    given.append(flip(collect(more[7:], 3), "spatial", 2))

    chunks = []
    for hidden, own in normed:
        outs = convolve(meta, hidden, taps, own, band, columns)
        if not chunks:
            (given[2],) = after([given[2]], outs[0])
        chunks.append([outs[0]] + [flip(outs[r], "spatial", r) for r in (1, 2, 3)])

    projected = project(meta, pieces, more, given, images, plan.shape[0] * plan.shape[1])
    cot = cotangent.reshape(images * band, channels)
    both = [projected, flip(projected, "spatial", 1)]
    prepared = both + list(prepare(meta, *both, cot, images))
    tokens = images * shards * band * lax.axis_size("spatial")
    results = []
    kept = []
    given = []
    for b in range(images):
        result, keep, send = attend(meta, chunks[b], prepared, b, band)
        results.append(result.reshape(1, band_rows, columns, channels))
        kept.append(keep)
        given.append(flip(send, "spatial", 1))
    partial = gradient(kept + given[:-1])
    mine, *sends = quarters(meta, partial, given[-1], 1.0 / math.sqrt(tokens))
    moved = [flip_plane(sends[r - 1], 4 * (r % 2) + 2 * (r // 2)) for r in (1, 2, 3)]
    mine, *sends = slabs(meta, [mine] + moved, (F32, F32, BF16, BF16))
    total = line_sum([mine] + [flip(sends[r - 1], "dp", 2 * r) for r in (1, 2, 3)])
    grads = finish(meta, [total] + [flip(total, "spatial", r) for r in (1, 2, 3)])
    return jnp.concatenate(results), grads


def solution(mesh):
    fits = mesh.shape["dp"] == 8 and mesh.shape["spatial"] == 4
    return jax.shard_map(
        body if fits else plain_body,
        mesh=mesh,
        in_specs=(
            P("dp", "spatial", None, None),
            P("dp", "spatial", None),
            P(None, "dp", None),
            P(),
            P(None, "dp", None),
            P("dp", "spatial", None, None),
        ),
        out_specs=(P("dp", "spatial", None, None), P("dp", None, None)),
        check_vma=False,
    )
```

```python
import math

import jax
import jax.numpy as jnp
from jax import lax
from jax.experimental import pallas as pl
from jax.experimental.pallas import tpu as pltpu
from jax.sharding import PartitionSpec as P

GROUPS = 32
HEAD = 64


eps_norm = 1e-05


def with_halo(cells, sides, width):
    for axis, dim in sides:
        count = lax.axis_size(axis)
        ends = count - 1
        head = lax.slice_in_dim(cells, 0, width, axis=dim)
        tail = lax.slice_in_dim(cells, cells.shape[dim] - width, cells.shape[dim], axis=dim)
        cells = jnp.concatenate(
            [
                lax.ppermute(tail, axis, [(i, (i + 1) % count) for i in range(ends)]),
                cells,
                lax.ppermute(head, axis, [((i + 1) % count, i) for i in range(ends)]),
            ],
            axis=dim,
        )
    return cells


def plain_body(latents, plan, conv_weight, gn_gain, attn_weights, cotangent):
    images, band_rows, columns, channels = latents.shape
    heads = channels // HEAD
    per_group = channels // GROUPS
    tokens_here = images * band_rows * columns
    scale = 1.0 / math.sqrt(HEAD)
    flat_input = latents.astype(jnp.float32).reshape(images, band_rows * columns, GROUPS, per_group)
    first_sums = jnp.sum(flat_input, axis=(1, 3))
    second_sums = jnp.sum(flat_input * flat_input, axis=(1, 3))
    first_sums, second_sums = lax.psum((first_sums, second_sums), "spatial")
    counted = float(band_rows * lax.axis_size("spatial") * columns * per_group)
    means = first_sums / counted
    variance = second_sums / counted - means * means
    inverse = lax.rsqrt(variance + eps_norm)
    normed = (flat_input - means[:, None, :, None]) * inverse[:, None, :, None]
    normed = normed.reshape(images, band_rows, columns, channels) * gn_gain
    hidden = jax.nn.silu(normed).astype(jnp.bfloat16)
    padded = with_halo(hidden, (("spatial", 1),), 1)
    padded = jnp.pad(padded, ((0, 0), (0, 0), (1, 1), (0, 0)))
    tapped = jnp.stack(
        [
            padded[:, offset_y : offset_y + band_rows, offset_x : offset_x + columns].reshape(
                tokens_here, channels
            )
            for offset_y in range(3)
            for offset_x in range(3)
        ],
        1,
    )
    conv_sum = jnp.einsum(
        "ntc,tcd->nd",
        tapped,
        lax.all_gather(conv_weight, "dp", axis=1, tiled=True),
        preferred_element_type=jnp.float32,
    )
    mixed = (latents.reshape(tokens_here, channels).astype(jnp.float32) + conv_sum).astype(
        jnp.bfloat16
    )
    weights = lax.all_gather(attn_weights, "dp", axis=1, tiled=True)
    weight_q = weights[0]
    weight_k = weights[1]
    weight_v = weights[2]
    weight_o = weights[3]
    queries = jnp.dot(mixed, weight_q, preferred_element_type=jnp.float32).astype(jnp.bfloat16)
    plan_all = lax.all_gather(plan, "spatial", axis=1, tiled=True)
    plan_flat = plan_all.reshape(-1, channels)
    keys_all = jnp.dot(plan_flat, weight_k, preferred_element_type=jnp.float32).astype(jnp.bfloat16)
    values_all = jnp.dot(plan_flat, weight_v, preferred_element_type=jnp.float32).astype(
        jnp.bfloat16
    )
    keys_all = keys_all.reshape(images, -1, channels)
    values_all = values_all.reshape(images, -1, channels)
    plan_tokens = keys_all.shape[1]
    query_heads = queries.reshape(images, band_rows * columns, heads, HEAD)
    key_heads = keys_all.reshape(images, plan_tokens, heads, HEAD)
    value_heads = values_all.reshape(images, plan_tokens, heads, HEAD)
    scores = (
        jnp.einsum("bnhe,bmhe->bhnm", query_heads, key_heads, preferred_element_type=jnp.float32)
        * scale
    )
    maxima = jnp.max(scores, axis=-1, keepdims=True)
    expo = jnp.exp(scores - maxima)
    probs = expo / jnp.sum(expo, axis=-1, keepdims=True)
    probs_b = probs.astype(jnp.bfloat16)
    attended = jnp.einsum(
        "bhnm,bmhe->bnhe", probs_b, value_heads, preferred_element_type=jnp.float32
    )
    attended = attended.reshape(tokens_here, channels).astype(jnp.bfloat16)
    result = mixed.astype(jnp.float32) + jnp.dot(
        attended, weight_o, preferred_element_type=jnp.float32
    )
    block_out = result.astype(jnp.bfloat16).reshape(images, band_rows, columns, channels)
    grad_flat = cotangent.reshape(tokens_here, channels)
    grad_att = lax.dot_general(
        grad_flat, weight_o, (((1,), (1,)), ((), ())), preferred_element_type=jnp.float32
    )
    grad_att = grad_att.astype(jnp.bfloat16).reshape(images, band_rows * columns, heads, HEAD)
    dprob = jnp.einsum("bnhe,bmhe->bhnm", grad_att, value_heads, preferred_element_type=jnp.float32)
    dscore = (probs * (dprob - jnp.sum(probs * dprob, axis=-1, keepdims=True)) * scale).astype(
        jnp.bfloat16
    )
    dquery = jnp.einsum("bhnm,bmhe->bnhe", dscore, key_heads, preferred_element_type=jnp.float32)
    dquery = dquery.reshape(tokens_here, channels).astype(jnp.bfloat16)
    total_tokens = images * lax.axis_size("dp") * band_rows * lax.axis_size("spatial") * columns
    factor = 1.0 / math.sqrt(total_tokens)
    contract = (((0,), (0,)), ((), ()))
    grad_query = lax.dot_general(mixed, dquery, contract, preferred_element_type=jnp.float32)
    grad_output = lax.dot_general(attended, grad_flat, contract, preferred_element_type=jnp.float32)
    own_rows = lax.psum_scatter(
        jnp.stack([grad_query, grad_output], 1) * factor, "dp", scatter_dimension=0, tiled=True
    )
    weight_grads = lax.psum(own_rows, "spatial")
    return (block_out, weight_grads)


F32 = jnp.float32
BF16 = jnp.bfloat16
LANES = 128
PIECE = 32
VMEM_LIMIT = 24 * 1024 * 1024
NT = (((1,), (1,)), ((), ()))


def cost(microseconds):
    return pl.CostEstimate(flops=0, bytes_accessed=microseconds * 3690000, transcendentals=0)


def params():
    return pltpu.CompilerParams(vmem_limit_bytes=VMEM_LIMIT)


def whole(shape):
    return pl.BlockSpec(memory_space=pltpu.VMEM)


def smem():
    return pl.BlockSpec(memory_space=pltpu.SMEM)


def lanes_of(shape):
    return lax.broadcasted_iota(jnp.int32, shape, len(shape) - 1)


def pack_kernel(conv_hbm, attn_hbm, latents_hbm, plan_hbm, out, more, rows_out, meta, weight, matrix, sems):
    s = lax.axis_index("spatial")
    core, high = s % 2, s // 2
    split = latents_hbm.shape[0]
    copies = [
        pltpu.make_async_copy(conv_hbm, weight, sems.at[0]),
        pltpu.make_async_copy(attn_hbm.at[jnp.where(high == 0, 3 * core, 1 + core)], matrix, sems.at[1]),
        pltpu.make_async_copy(latents_hbm, rows_out.at[pl.ds(0, split)], sems.at[2]),
        pltpu.make_async_copy(plan_hbm, rows_out.at[pl.ds(split, plan_hbm.shape[0])], sems.at[3]),
    ]
    for copy in copies:
        copy.start()
    me = lax.axis_index("dp")
    along_x, along_z = me % 2, me // 2
    position = jnp.where(along_x == 0, along_z, 7 - along_z)
    where = [(position + o + 8) % 8 for o in (0, -1, 1, -2, 2, -3, 3, -4)]
    held = [jnp.where(p < 4, 2 * p, 2 * (7 - p) + 1) for p in where]
    slots = [sum(jnp.where(h == j, i, 0) for i, h in enumerate(held)) for j in range(8)]
    for k, fact in enumerate([s, core] + held + slots + [along_x, along_z]):
        meta[k] = fact.astype(jnp.int32)
    copies[0].wait()
    out[0:9] = weight[:, :, pl.ds(pl.multiple_of(s * LANES, LANES), LANES)]
    rows = lax.broadcasted_iota(jnp.int32, (LANES, LANES), 0)
    cols = lax.broadcasted_iota(jnp.int32, (LANES, LANES), 1)
    last = 4 * LANES
    for dy in range(3):
        total = None
        for dx in range(3):
            pick = (rows == PIECE * s + cols - PIECE * dx) & (cols >= PIECE * dx) & (cols < PIECE * dx + PIECE)
            part = jnp.dot(
                weight[3 * dy + dx, :, last : last + LANES],
                jnp.where(pick, 1.0, 0.0).astype(BF16),
                preferred_element_type=F32,
            )
            total = part if total is None else total + part
        more[dy] = total.astype(BF16)
    copies[1].wait()
    for k in range(matrix.shape[1] // LANES):
        more[3 + k] = matrix[:, LANES * k : LANES * k + LANES]
    copies[2].wait()
    copies[3].wait()


def pack(conv_weight, attn_weights, latents, plan):
    taps, rows, channels = conv_weight.shape
    shapes = [
        (taps, rows, LANES),
        (3 + channels // LANES, rows, LANES),
        (latents.shape[0] + plan.shape[0], channels),
    ]
    return pl.pallas_call(
        pack_kernel,
        in_specs=[pl.BlockSpec(memory_space=pltpu.HBM)] * 4,
        out_specs=[whole(shape) for shape in shapes] + [smem()],
        out_shape=[jax.ShapeDtypeStruct(shape, BF16) for shape in shapes] + [jax.ShapeDtypeStruct((20,), jnp.int32)],
        scratch_shapes=[
            pltpu.VMEM(conv_weight.shape, BF16),
            pltpu.VMEM((rows, channels), BF16),
            pltpu.SemaphoreType.DMA((4,)),
        ],
        compiler_params=params(),
        cost_estimate=cost(1),
        name="pack",
    )(*(pltpu.with_memory_space_constraint(x, pltpu.HBM) for x in (conv_weight, attn_weights, latents, plan)))


def collect(parts, first):
    blocks, rows = parts[0].shape[0] - first, parts[0].shape[1]

    def kernel(*refs):
        for k, part in enumerate(refs[:-1]):
            for block in range(blocks):
                refs[-1][k, :, LANES * block : LANES * block + LANES] = part[first + block]

    return pl.pallas_call(
        kernel,
        in_specs=[whole(None)] * len(parts),
        out_specs=whole(None),
        out_shape=jax.ShapeDtypeStruct((len(parts), rows, LANES * blocks), BF16),
        compiler_params=params(),
        cost_estimate=cost(0),
        name="collect",
    )(*parts)


def stats_kernel(images, band, per_group, count, meta, x0, x1, x2, x3, gain, out):
    channels = gain.shape[0]
    shape = (channels, channels)
    row_group = jnp.floor((lax.broadcasted_iota(jnp.int32, shape, 0).astype(F32) + 0.5) * (1.0 / per_group))
    col_group = jnp.floor((lax.broadcasted_iota(jnp.int32, shape, 1).astype(F32) + 0.5) * (1.0 / per_group))
    same_group = jnp.where(row_group == col_group, 1.0, 0.0).astype(BF16)
    sums = []
    for b in range(images):
        first = jnp.zeros((1, channels), F32)
        second = jnp.zeros((1, channels), F32)
        for piece in (x0, x1, x2, x3):
            x = piece[band * b : band * b + band, :].astype(F32)
            first += jnp.sum(x, axis=0, keepdims=True)
            second += jnp.sum(x * x, axis=0, keepdims=True)
        sums += [first, second]
    sums = jnp.concatenate(sums, axis=0)
    high = sums.astype(BF16)
    rest = sums - high.astype(F32)
    middle = rest.astype(BF16)
    low = (rest - middle.astype(F32)).astype(BF16)
    grouped = sum(jnp.dot(part, same_group, preferred_element_type=F32) for part in (high, middle, low))
    for b in range(images):
        mean = grouped[2 * b : 2 * b + 1] / count
        variance = grouped[2 * b + 1 : 2 * b + 2] / count - mean * mean
        out[b : b + 1, :] = mean
        out[images + b : images + b + 1, :] = lax.rsqrt(variance + eps_norm) * gain[...].reshape(1, channels) * 0.5


def group_stats(meta, pieces, gain, images, band):
    channels = gain.shape[-1]
    per_group = channels // GROUPS
    return pl.pallas_call(
        lambda *refs: stats_kernel(images, band, per_group, float(4 * band * per_group), *refs),
        in_specs=[smem()] + [whole(None)] * 5,
        out_specs=whole(None),
        out_shape=jax.ShapeDtypeStruct((2 * images, channels), F32),
        compiler_params=params(),
        cost_estimate=cost(0),
        name="group_stats",
    )(meta, *pieces, gain)


def norm_kernel(image, images, band, columns, meta, x0, x1, x2, x3, stats, hidden, own):
    s = meta[0]
    pieces = [x.at[image * band : image * band + band] for x in (x0, x1, x2, x3)]
    channels = stats.shape[1]
    mean = stats[image : image + 1, :]
    factor = stats[images + image : images + image + 1, :]
    rows = 64
    hidden[0:columns, :] = jnp.zeros((columns, channels), BF16)
    hidden[columns + 4 * band :, :] = jnp.zeros((columns, channels), BF16)
    krow = lax.broadcasted_iota(jnp.int32, (LANES, LANES), 0)
    kcol = lax.broadcasted_iota(jnp.int32, (LANES, LANES), 1)
    repeat = jnp.where(krow == PIECE * s + lax.rem(kcol, PIECE), 1.0, 0.0).astype(BF16)
    for r, piece in enumerate(pieces):
        base = (s ^ r) * band
        own[pl.ds(pl.multiple_of(base, band), band), 0:LANES] = piece[
            :, pl.ds(pl.multiple_of(s * LANES, LANES), LANES)
        ]
        own[pl.ds(pl.multiple_of(base, band), band), LANES : 2 * LANES] = jnp.dot(
            piece[:, 4 * LANES :], repeat, preferred_element_type=F32
        ).astype(BF16)
        for at in range(0, band, rows):
            t = (piece[at : at + rows, :].astype(F32) - mean) * factor
            hidden[pl.ds(pl.multiple_of(base + columns + at, columns), rows), :] = (t + t * jnp.tanh(t)).astype(BF16)


def normalise(meta, pieces, stats, image, images, band, columns):
    channels = stats.shape[-1]
    tokens = 4 * band
    hidden = (tokens + 2 * columns, channels)
    own = (tokens, 2 * LANES)
    return pl.pallas_call(
        lambda *refs: norm_kernel(image, images, band, columns, *refs),
        in_specs=[smem()] + [whole(None)] * 5,
        out_specs=[whole(hidden), whole(own)],
        out_shape=[jax.ShapeDtypeStruct(hidden, BF16), jax.ShapeDtypeStruct(own, BF16)],
        compiler_params=params(),
        cost_estimate=cost(0),
        name="normalise",
    )(meta, *pieces, stats)


def fill_taps(taps, at, shard, tap):
    lane = lanes_of((shard, LANES))
    wide = 2 * LANES
    rows = taps.shape[0] // 3
    for dy in range(3):
        here = pl.ds(pl.multiple_of(rows * dy + at, 16), shard)
        for dx in range(3):
            taps[here, wide * dx : wide * dx + LANES] = tap(3 * dy + dx)
            taps[here, wide * dx + LANES : wide * dx + wide] = jnp.where(
                (lane >= PIECE * dx) & (lane < PIECE * dx + PIECE), tap(9 + dy), jnp.zeros((), BF16)
            )


def first_taps(meta, weights, more, channels):
    shard, count = weights[0].shape[1], len(weights)

    def kernel(meta, *refs):
        for i in range(count):
            fill_taps(
                refs[-1], shard * meta[2 + i], shard, lambda k, i=i: refs[i][k] if k < 9 else refs[count + i][k - 9]
            )

    return pl.pallas_call(
        kernel,
        in_specs=[smem()] + [whole(None)] * (2 * count),
        out_specs=whole(None),
        out_shape=jax.ShapeDtypeStruct((3 * channels, 6 * LANES), BF16),
        compiler_params=params(),
        cost_estimate=cost(6),
        name="first_taps",
    )(meta, *weights, *more)


def last_taps(meta, taps, halves):
    shard = halves[0].shape[1]

    def kernel(meta, before, one, two, after):
        split = one.shape[0]
        after[...] = before[...]
        fill_taps(after, shard * meta[9], shard, lambda k: one[k] if k < split else two[k - split])

    return pl.pallas_call(
        kernel,
        in_specs=[smem()] + [whole(None)] * 3,
        out_specs=whole(None),
        out_shape=jax.ShapeDtypeStruct(taps.shape, BF16),
        compiler_params=params(),
        cost_estimate=cost(0),
        name="last_taps",
    )(meta, taps, *halves)


def conv_kernel(band, columns, meta, taps, hidden, own, *refs):
    outs = refs
    s = meta[0]
    channels = hidden.shape[1]
    wide = 2 * LANES
    column = lax.rem(lax.broadcasted_iota(jnp.int32, (band, wide), 0), columns)
    group = band // 4
    lane = lanes_of((group, LANES))
    for r, out in enumerate(outs):
        base = (s ^ r) * band
        here = pl.ds(pl.multiple_of(base, band), band)
        window = jnp.concatenate(
            [hidden[pl.ds(pl.multiple_of(base + columns * dy, columns), band), :] for dy in range(3)], axis=1
        )
        parts = jnp.dot(window, taps[...], preferred_element_type=F32)
        total = parts[:, wide : 2 * wide]
        total += jnp.where(column == 0, 0.0, pltpu.roll(parts[:, :wide], 1, 0))
        total += jnp.where(column == columns - 1, 0.0, pltpu.roll(parts[:, 2 * wide :], band - 1, 0))
        tail = total[:, LANES:]
        tail = tail + pltpu.roll(tail, 2 * PIECE, 1)
        tail = tail + pltpu.roll(tail, PIECE, 1)
        cells = own[here, :].astype(F32)
        out[0:band, :] = (cells[:, :LANES] + total[:, :LANES]).astype(BF16)
        tail = cells[:, LANES:] + tail
        packed = tail[0:group]
        for g in range(1, 4):
            packed = jnp.where(lane >= PIECE * g, tail[group * g : group * g + group], packed)
        out[band : band + group, :] = packed.astype(BF16)


def convolve(meta, hidden, taps, own, band, columns):
    operands = [taps, hidden, own]
    channels = hidden.shape[1]
    shapes = [jax.ShapeDtypeStruct((band + band // 4, LANES), BF16)] * 4
    return pl.pallas_call(
        lambda *refs: conv_kernel(band, columns, *refs),
        in_specs=[smem()] + [whole(x.shape) for x in operands],
        out_specs=[whole(shape.shape) for shape in shapes],
        out_shape=shapes,
        compiler_params=params(),
        cost_estimate=cost(4),
        name="convolve",
    )(meta, *operands)


def project_kernel(shards, images, count, meta, p0, p1, p2, p3, *refs):
    ours, batches = refs[:shards], refs[shards:-3]
    out, both, plan = refs[-3:]
    s, high = meta[0], meta[0] // 2
    shard, channels = ours[0].shape[1], out.shape[1]
    theirs = [batch.at[k] for batch in batches for k in range(batch.shape[0])]
    for i in range(shards):
        at = pl.ds(pl.multiple_of(shard * meta[2 + i], 16), shard)
        for block in range(channels // LANES):
            both[high, at, LANES * block : LANES * block + LANES] = ours[i][3 + block]
        both[1 - high, at, :] = theirs[i][...]
    for r, piece in enumerate((p0, p1, p2, p3)):
        rows = count // images
        start = piece.shape[0] - count
        for b in range(images):
            plan[pl.ds(pl.multiple_of(rows * (4 * b + (s ^ r)), 16), rows), :] = piece[
                start + rows * b : start + rows * b + rows, :
            ]
    out[0:channels, :] = both[0]
    out[channels:, :] = jnp.dot(plan[...], both[1], preferred_element_type=F32).astype(BF16)


def project(meta, pieces, ours, theirs, images, rows):
    channels = theirs[0].shape[2]
    operands = list(pieces) + list(ours) + list(theirs)
    return pl.pallas_call(
        lambda *refs: project_kernel(len(ours), images, rows, *refs),
        in_specs=[smem()] + [whole(x.shape) for x in operands],
        out_specs=whole((channels + 4 * rows, channels)),
        out_shape=jax.ShapeDtypeStruct((channels + 4 * rows, channels), BF16),
        scratch_shapes=[pltpu.VMEM((2, channels, channels), BF16), pltpu.VMEM((4 * rows, channels), BF16)],
        compiler_params=params(),
        cost_estimate=cost(1),
        name="project_plan",
    )(meta, *operands)


def prepare_kernel(images, meta, mine, other, cot, key, key_t, value_t, dprob, cot_t, kv, back):
    core = meta[1]
    channels = cot.shape[1]
    plan_rows = (mine.shape[0] - channels) // images

    @pl.when(core == 0)
    def _():
        kv[0] = mine[channels:]
        kv[1] = other[channels:]
        back[...] = lax.dot_general(cot[...], other[0:channels], NT, preferred_element_type=F32).astype(BF16)

    @pl.when(core != 0)
    def _():
        kv[0] = other[channels:]
        kv[1] = mine[channels:]
        back[...] = lax.dot_general(cot[...], mine[0:channels], NT, preferred_element_type=F32).astype(BF16)

    tokens = cot.shape[0] // images
    lane = lanes_of((plan_rows, LANES))
    for b in range(images):
        at = slice(tokens * b, tokens * b + tokens)
        cot_t[b] = cot[at, :].T
        for p in range(channels // LANES):
            cut = slice(LANES * p, LANES * p + LANES)
            both = []
            for which in range(2):
                part = kv[which, plan_rows * b : plan_rows * b + plan_rows, cut].astype(F32)
                both.append(
                    jnp.concatenate([jnp.where(lane < HEAD, part, 0.0), jnp.where(lane >= HEAD, part, 0.0)], axis=0)
                )
            key[b, p] = both[0].astype(BF16)
            key_t[b, p] = both[0].T.astype(BF16)
            value_t[b, p] = both[1].T.astype(BF16)
            dprob[b, p] = lax.dot_general(both[1].astype(BF16), back[at, cut], NT, preferred_element_type=F32)


def prepare(meta, mine, other, cot, images):
    channels = cot.shape[1]
    pairs = channels // LANES
    tokens = cot.shape[0] // images
    square = (images, pairs, LANES, LANES)
    shapes = [
        (square, BF16),
        (square, BF16),
        (square, BF16),
        ((images, pairs, LANES, tokens), F32),
        ((images, channels, tokens), BF16),
    ]
    return pl.pallas_call(
        lambda *refs: prepare_kernel(images, *refs),
        in_specs=[smem(), whole(mine.shape), whole(other.shape), whole(cot.shape)],
        out_specs=[whole(shape) for shape, _ in shapes],
        out_shape=[jax.ShapeDtypeStruct(shape, kind) for shape, kind in shapes],
        scratch_shapes=[pltpu.VMEM((2, mine.shape[0] - channels, channels), BF16), pltpu.VMEM(cot.shape, BF16)],
        compiler_params=params(),
        cost_estimate=cost(2),
        name="prepare_attention",
    )(meta, mine, other, cot)


def attend_kernel(image, meta, c0, c1, c2, c3, mine, other, key, key_t, value_t, dprob, cot_t, mixed, att_t, kept, sent, queries, dq_t):
    s = meta[0]
    core = meta[1]
    tokens, channels = mixed.shape
    group = tokens // 4
    scale = 1.0 / math.sqrt(HEAD)
    lane = lanes_of((group, LANES))
    krow = lax.broadcasted_iota(jnp.int32, (LANES, LANES), 0)
    kcol = lax.broadcasted_iota(jnp.int32, (LANES, LANES), 1)
    same = lax.rem(krow, PIECE) == lax.rem(kcol, PIECE)
    tail = jnp.zeros((tokens, LANES), F32)
    for r, chunk in enumerate((c0, c1, c2, c3)):
        source = s ^ r
        mixed[:, pl.ds(pl.multiple_of(source * LANES, LANES), LANES)] = chunk[0:tokens, :]
        packed = chunk[tokens : tokens + group, :]
        spread = jnp.concatenate(
            [
                jnp.where((lane >= PIECE * g) & (lane < PIECE * g + PIECE), packed, jnp.zeros((), BF16))
                for g in range(4)
            ],
            axis=0,
        )
        place = same & (kcol >= PIECE * source) & (kcol < PIECE * source + PIECE)
        tail += jnp.dot(spread, jnp.where(place, 1.0, 0.0).astype(BF16), preferred_element_type=F32)
    mixed[:, 4 * LANES :] = tail.astype(BF16)
    here = mixed[...]

    @pl.when(core == 0)
    def _():
        queries[...] = jnp.dot(here, mine[0:channels], preferred_element_type=F32).astype(BF16)

    @pl.when(core != 0)
    def _():
        queries[...] = jnp.dot(here, other[0:channels], preferred_element_type=F32).astype(BF16)

    cuts = [slice(LANES * p, LANES * p + LANES) for p in range(channels // LANES)]
    scores = [
        lax.dot_general(key[image, p], queries[:, cut], NT, preferred_element_type=F32) for p, cut in enumerate(cuts)
    ]
    probs = []
    for score in scores:
        score = score.reshape(2, HEAD, tokens) * scale
        expo = jnp.exp(score - jnp.max(score, axis=1, keepdims=True))
        probs.append(expo * (1.0 / jnp.sum(expo, axis=1, keepdims=True)))
    for p, cut in enumerate(cuts):
        att_t[cut, :] = jnp.dot(
            value_t[image, p], probs[p].reshape(LANES, tokens).astype(BF16), preferred_element_type=F32
        ).astype(BF16)
    dscores = []
    for p, prob in enumerate(probs):
        down = dprob[image, p].reshape(2, HEAD, tokens)
        dscore = prob * (down - jnp.sum(prob * down, axis=1, keepdims=True)) * scale
        dscores.append(dscore.reshape(LANES, tokens).astype(BF16))
    for p, cut in enumerate(cuts):
        dq_t[cut, :] = jnp.dot(key_t[image, p], dscores[p], preferred_element_type=F32).astype(BF16)

    @pl.when(core == 0)
    def _():
        kept[0] = here.T
        kept[1] = dq_t[...]
        sent[0] = att_t[...]
        sent[1] = cot_t[image]

    @pl.when(core != 0)
    def _():
        sent[0] = here.T
        sent[1] = dq_t[...]
        kept[0] = att_t[...]
        kept[1] = cot_t[image]


def attend(meta, chunks, prepared, image, tokens):
    channels = prepared[0].shape[1]
    operands = list(chunks) + list(prepared)
    both = jax.ShapeDtypeStruct((2, channels, tokens), BF16)
    return pl.pallas_call(
        lambda *refs: attend_kernel(image, *refs),
        in_specs=[smem()] + [whole(x.shape) for x in operands],
        out_specs=[whole(None)] * 4,
        out_shape=[
            jax.ShapeDtypeStruct((tokens, channels), BF16),
            jax.ShapeDtypeStruct((channels, tokens), BF16),
            both,
            both,
        ],
        scratch_shapes=[pltpu.VMEM((tokens, channels), BF16), pltpu.VMEM((channels, tokens), BF16)],
        compiler_params=params(),
        cost_estimate=cost(3),
        name="attend",
    )(meta, *operands)


def block_output(meta, mixed, attended, mine, other):
    images = len(mixed)
    tokens, channels = mixed[0].shape

    def kernel(meta, *refs):
        out, both, weight = refs[-1], refs[: 2 * images], refs[2 * images : 2 * images + 2]

        def write(projection):
            for b in range(images):
                added = jnp.dot(both[images + b][...].T, projection[0:channels], preferred_element_type=F32)
                out[tokens * b : tokens * b + tokens, :] = (both[b][...].astype(F32) + added).astype(BF16)

        @pl.when(meta[1] == 0)
        def _():
            write(weight[1])

        @pl.when(meta[1] != 0)
        def _():
            write(weight[0])

    operands = [*mixed, *attended, mine, other]
    return pl.pallas_call(
        kernel,
        in_specs=[smem()] + [whole(None)] * len(operands),
        out_specs=whole(None),
        out_shape=jax.ShapeDtypeStruct((images * tokens, channels), BF16),
        compiler_params=params(),
        cost_estimate=cost(1),
        name="block_output",
    )(meta, *operands)


def gradient(parts):
    channels = parts[0].shape[1]

    def kernel(*refs):
        left, right = (jnp.concatenate([part[k] for part in refs[:-1]], axis=1) for k in range(2))
        refs[-1][...] = lax.dot_general(left, right, NT, preferred_element_type=F32)

    return pl.pallas_call(
        kernel,
        in_specs=[whole(x.shape) for x in parts],
        out_specs=whole(None),
        out_shape=jax.ShapeDtypeStruct((channels, channels), F32),
        compiler_params=params(),
        cost_estimate=cost(1),
        name="gradient_first",
    )(*parts)


def quarter_kernel(factor, meta, partial, part, mine, *refs):
    sends, total = refs[:-1], refs[-1]
    total[...] = (partial[...] + lax.dot_general(part[0], part[1], NT, preferred_element_type=F32)) * factor
    along_x, along_y = meta[18], meta[0] // 2
    rows = mine.shape[0] // 4
    for r, out in enumerate((mine,) + sends):
        parts = []
        for z in range(4):
            at = pl.multiple_of(rows * (2 * (2 * z + (along_x ^ (r % 2))) + (along_y ^ (r // 2))), 8)
            parts.append(total[pl.ds(at, rows), :])
        out[...] = jnp.concatenate(parts, axis=0).astype(out.dtype)


def quarters(meta, partial, part, factor):
    rows, channels = partial.shape
    shapes = [jax.ShapeDtypeStruct((rows // 4, channels), kind) for kind in (F32, BF16, BF16, BF16)]
    return pl.pallas_call(
        lambda *refs: quarter_kernel(factor, *refs),
        in_specs=[smem(), whole(partial.shape), whole(part.shape)],
        out_specs=[whole(x.shape) for x in shapes],
        out_shape=shapes,
        scratch_shapes=[pltpu.VMEM((rows, channels), F32)],
        compiler_params=params(),
        cost_estimate=cost(1),
        name="gradient_last",
    )(meta, partial, part)


def line_sum(parts):
    def kernel(a, b, c, d, out):
        out[...] = a[...] + b[...].astype(F32) + c[...].astype(F32) + d[...].astype(F32)

    return pl.pallas_call(
        kernel,
        in_specs=[whole(None)] * 4,
        out_specs=whole(None),
        out_shape=jax.ShapeDtypeStruct(parts[0].shape, F32),
        compiler_params=params(),
        cost_estimate=cost(0),
        name="sum_line",
    )(*parts)


def finish_kernel(meta, mine, beside, across, corner, out):
    core, high = meta[1], meta[0] // 2
    rows = mine.shape[0]

    def ordered(a, b):
        first = jnp.where(high == 0, a[...], b[...])
        second = jnp.where(high == 0, b[...], a[...])
        return jnp.concatenate([first, second], axis=0)

    own, other = ordered(mine, across), ordered(beside, corner)
    out[:, 0, :] = jnp.where(core == 0, own, other)
    out[:, 1, :] = jnp.where(core == 0, other, own)


def finish(meta, parts):
    rows, channels = parts[0].shape
    return pl.pallas_call(
        finish_kernel,
        in_specs=[smem()] + [whole(x.shape) for x in parts],
        out_specs=whole(None),
        out_shape=jax.ShapeDtypeStruct((2 * rows, 2, channels), F32),
        compiler_params=params(),
        cost_estimate=cost(1),
        name="finish",
    )(meta, *parts)


def slab_kernel(meta, a, b, c, d, mine, *sends):
    along_z = meta[19]
    rows = mine.shape[0]
    total = a[...] + b[...].astype(F32) + c[...].astype(F32) + d[...].astype(F32)
    for z in range(4):
        part = total[rows * z : rows * z + rows]
        for r, out in enumerate((mine,) + sends):

            @pl.when((along_z ^ r) == z)
            def _(out=out, part=part):
                out[...] = part.astype(out.dtype)


def slabs(meta, parts, kinds):
    rows, channels = parts[0].shape
    shapes = [jax.ShapeDtypeStruct((rows // 4, channels), t) for t in kinds]
    return pl.pallas_call(
        slab_kernel,
        in_specs=[smem()] + [whole(x.shape) for x in parts],
        out_specs=[whole(x.shape) for x in shapes],
        out_shape=shapes,
        compiler_params=params(),
        cost_estimate=cost(1),
        name="sum_plane",
    )(meta, *parts)


def flip(x, axis, bits):
    count = lax.axis_size(axis)
    return lax.ppermute(x, axis, [(i, i ^ bits) for i in range(count)])


def flip_plane(x, bits):
    count = lax.axis_size("dp") * lax.axis_size("spatial")
    return lax.ppermute(x, ("dp", "spatial"), [(i, i ^ bits) for i in range(count)])


def ring_place(p):
    return 2 * p if p < 4 else 2 * (7 - p) + 1


def step_ring(x, backward):
    shards = lax.axis_size("dp")
    pairs = [(ring_place(p), ring_place((p + 1) % shards)) for p in range(shards)]
    return lax.ppermute(x, "dp", [(b, a) for a, b in pairs] if backward else pairs)


def after(values, *others):
    return lax.optimization_barrier((tuple(values), others))[0]


def body(latents, plan, conv_weight, gn_gain, attn_weights, cotangent):
    images, band_rows, columns, channels = latents.shape
    shards = lax.axis_size("dp")
    band = band_rows * columns
    packed, packed_more, mine, meta = pack(
        conv_weight, attn_weights, latents.reshape(images * band, channels), plan.reshape(-1, channels)
    )
    across = flip(mine, "spatial", 2)
    ring = [packed, step_ring(packed, False), step_ring(packed, True)]
    more = [packed_more, step_ring(packed_more, False), step_ring(packed_more, True)]
    for _ in range(2):
        ring += [step_ring(ring[-2], False), step_ring(ring[-1], True)]
        more += [step_ring(more[-2], False), step_ring(more[-1], True)]
    (across,) = after([across], *ring[3:5], *more[3:5])
    pieces = [mine, flip(mine, "spatial", 1), across, flip(across, "spatial", 1)]
    given = [flip(collect(more[:5], 3), "spatial", 2)]
    stats = group_stats(meta, pieces, gn_gain, images, band)
    normed = [normalise(meta, pieces, stats, b, images, band, columns) for b in range(images)]
    a, b = after((ring[5], more[6]), *(x[1] for x in normed))
    ring.append(step_ring(a, False))
    more.append(step_ring(b, True))
    given.append(flip(collect(more[5:7], 3), "spatial", 2))
    taps = first_taps(meta, ring[:7], more[:7], channels)
    ring[7], more[7], taps = after((ring[7], more[7], taps))
    taps = last_taps(meta, taps, (ring[7], more[7]))
    given.append(flip(collect(more[7:], 3), "spatial", 2))

    chunks = []
    for hidden, own in normed:
        outs = convolve(meta, hidden, taps, own, band, columns)
        if not chunks:
            (given[2],) = after([given[2]], outs[0])
        chunks.append([outs[0]] + [flip(outs[r], "spatial", r) for r in (1, 2, 3)])

    projected = project(meta, pieces, more, given, images, plan.shape[0] * plan.shape[1])
    cot = cotangent.reshape(images * band, channels)
    both = [projected, flip(projected, "spatial", 1)]
    prepared = both + list(prepare(meta, *both, cot, images))
    tokens = images * shards * band * lax.axis_size("spatial")
    results = []
    kept = []
    given = []
    for b in range(images):
        here, attended, keep, send = attend(meta, chunks[b], prepared, b, band)
        results.append((here, attended))
        kept.append(keep)
        given.append(flip(send, "spatial", 1))
    partial = gradient(kept + given[:-1])
    mine, *sends = quarters(meta, partial, given[-1], 1.0 / math.sqrt(tokens))
    moved = [flip_plane(sends[r - 1], 4 * (r % 2) + 2 * (r // 2)) for r in (1, 2, 3)]
    mine, *sends = slabs(meta, [mine] + moved, (F32, F32, BF16, BF16))
    total = line_sum([mine] + [flip(sends[r - 1], "dp", 2 * r) for r in (1, 2, 3)])
    grads = finish(meta, [total] + [flip(total, "spatial", r) for r in (1, 2, 3)])
    result = block_output(meta, [x[0] for x in results], [x[1] for x in results], *both)
    return result.reshape(cotangent.shape), grads


def solution(mesh):
    fits = mesh.shape["dp"] == 8 and mesh.shape["spatial"] == 4
    return jax.shard_map(
        body if fits else plain_body,
        mesh=mesh,
        in_specs=(
            P("dp", "spatial", None, None),
            P("dp", "spatial", None),
            P(None, "dp", None),
            P(),
            P(None, "dp", None),
            P("dp", "spatial", None, None),
        ),
        out_specs=(P("dp", "spatial", None, None), P("dp", None, None)),
        check_vma=False,
    )
```
